32 devices in a mesh: groups: 2 (over y), ep: 8 (over z, x), tp: 2 (over core).
Axes of the slice: x: 2, y: 2, z: 4, core: 2. Of those that a mesh axis runs over, the one named last changes fastest.
Arguments:
- tokens: bfloat16 [1024, 2880], P(('groups', 'ep'), 'tp'), parts along dimension 0, may hold values from -6 to 6
- expert_ids: int32 [1024, 4], P(('groups', 'ep')), parts along dimension 0, may hold values from 0 to 7, all different within a row; in each aligned block of 64 rows (0 to 63, 64 to 127, ...) at most 48 rows name the same one
- gate_probs: float32 [1024, 4], P(('groups', 'ep')), parts along dimension 0, may hold values from 0.05 to 1
- w_gate: bfloat16 [8, 2880, 1440], P('ep', None, 'tp'), may hold values from -0.109375 to 0.109375
- w_up: bfloat16 [8, 2880, 1440], P('ep', None, 'tp'), may hold values from -0.109375 to 0.109375
- w_down: bfloat16 [8, 1440, 2880], P('ep', 'tp'), may hold values from -0.15625 to 0.15625
Outputs:
- mixed: bfloat16 [1024, 2880], P(('groups', 'ep'), 'tp'), parts along dimension 0
The draws below stay inside these ranges and needn't reach their ends.
There are 2 independent parts, one for each index of `groups`. The reference program is written for one: setup_inputs(seed, part) draws one part's arguments, and reference() takes and returns one part's arrays. A program takes and returns all parts, laid end to end along the dimension named above; an argument that names none is the same for every part. Nothing has to cross between parts.
Inputs may be any that keep to these rules, and one draw needn't show every extreme that they name: `expert_ids`: within each block of 64 rows that one index of ep holds, no expert is named by more than 48 rows, and in every draw some expert is named by exactly 48 rows of some block; the numbers of one row differ.
All inputs are finite; a program needn't handle non-finite values.
Results may differ from the reference program's by a relative error of at most 0.0058.
Values may be sent and summed in bfloat16 or wider, within the bound.
No kernel may reach another device: no remote copies, remote signals or barrier semaphores. Data moves between devices by JAX's collectives and lax.ppermute only.
A program may use at most 128 MiB of HBM per device.

```python
import math
import jax
import jax.numpy as jnp
import numpy as np
from jax import lax

D = 2880
FF = 1440
TOP = 4
TOK_EP = 64
EXPERTS = 8
TOKENS = 512
CAP_SRC = 48
N_EP = 8


def level_of(own_key, dims, split, smallest, largest):
    level = 1.0
    for position, parts in split:
        steps = jax.random.uniform(jax.random.fold_in(jax.random.fold_in(own_key, 6), position), (parts,), jnp.float32, smallest / len(split), largest / len(split))
        level = level * jnp.repeat(jnp.exp(steps), dims[position] // parts).reshape((-1,) + (1,) * (len(dims) - 1 - position))
    return level


def deal_out(own_key, own, number, rows, amount, top, limit, skew):
    sequence = jax.random.permutation(own_key, amount)
    crowded, common = load_shares(amount, rows * top, limit, skew, True), load_shares(amount, rows * top, limit, skew, False)
    places = jnp.arange(amount)

    def named(tallies, rotation):
        used = int((tallies > 0).sum())
        fixed = max(1, used // 4)
        moved = fixed + (places - fixed + rotation * (used - fixed)) % max(1, amount - fixed)
        return jnp.zeros((amount,), jnp.int32).at[sequence[jnp.where(places < fixed, places, moved)]].set(jnp.asarray(tallies, jnp.int32))

    tallies = jnp.where(number % 4 == 0, named(crowded, number // 4), named(common, number - number // 4 - 1))
    mixed = jax.random.permutation(jax.random.fold_in(own, 3), amount)
    donor, taker = mixed[0:amount // 2 * 2:2], mixed[1:amount // 2 * 2:2]
    slack = jnp.minimum(tallies[donor] - 1, limit - tallies[taker]) // 2
    slack = jnp.where((donor == sequence[0]) | (taker == sequence[0]) | (tallies[taker] == 0), 0, jnp.maximum(slack, 0))
    moved = jax.random.randint(jax.random.fold_in(own, 4), (amount // 2,), 0, 1 << 20) % (slack + 1)
    tallies = tallies.at[donor].add(-moved).at[taker].add(moved)
    labels = jnp.searchsorted(jnp.cumsum(tallies), jnp.arange(rows * top), side="right").astype(jnp.int32)
    listing = labels.reshape(top, rows).T
    listing = listing[jax.random.permutation(jax.random.fold_in(own, 1), rows)]
    rotation = jax.random.randint(jax.random.fold_in(own, 2), (rows, 1), 0, top)
    return jnp.take_along_axis(listing, (jnp.arange(top)[None, :] + rotation) % top, axis=1)


def load_shares(amount, total, bound, slope, full):
    portions = [(1 << 20) // math.isqrt(grade ** slope) + 1 for grade in range(1, amount + 1)]
    largest = bound if full else min(bound, max(-(-total // amount), total * portions[0] // sum(portions)))
    least = 1 if total - largest >= amount - 1 else 0
    holding, surplus = [largest] + [least] * (amount - 1), total - largest - least * (amount - 1)
    while surplus > 0:
        candidates = [i for i in range(1, amount) if holding[i] < largest] or [i for i in range(1, amount) if holding[i] < bound]
        whole, left = sum([portions[i] for i in candidates]), surplus
        for i in candidates:
            addition = min(bound - holding[i], max(1, left * portions[i] // whole), surplus)
            holding[i] = holding[i] + addition
            surplus = surplus - addition
    return np.array(holding)


def noise(rng, extent, scale, most, pieces=(), kind=jnp.bfloat16):
    drawn = scale * jax.random.normal(rng, extent, jnp.float32)
    if pieces:
        drawn = drawn * level_of(rng, extent, pieces, -0.22, 0.18)
    return jnp.clip(drawn, -most, most).astype(kind)


def setup_inputs(seed: int = 0, part: int = 0) -> dict:
    streams_of = jax.random.split(jax.random.key(seed), 7)
    part_splits = jax.random.split(jax.random.fold_in(streams_of[6], part), 7)
    tokens = noise(part_splits[0], (TOKENS, D), 1.0, 6.0, ((0, 8), (1, 2)))
    expert_ids_keys = jax.random.split(jax.random.fold_in(part_splits[1], 1), TOKENS // TOK_EP)
    expert_ids_turns = jax.random.permutation(jax.random.fold_in(part_splits[1], 3), TOKENS // TOK_EP)
    expert_ids = jax.vmap(lambda own, number: deal_out(jax.random.fold_in(part_splits[1], 2), own, number, TOK_EP, EXPERTS, TOP, CAP_SRC, 2))(expert_ids_keys, expert_ids_turns).reshape((TOKENS, TOP))
    gate_probs = jnp.clip(jnp.exp(math.log(1.0) - 2.9957323 * jax.random.uniform(part_splits[2], (TOKENS, TOP), jnp.float32) ** level_of(part_splits[2], (TOKENS, TOP), ((0, 8),), -0.2, 0.2)), 0.05, 1.0)
    w_gate = noise(streams_of[3], (EXPERTS, D, FF), D ** -0.5, 0.109375, ((0, 8), (2, 2)))
    w_up = noise(streams_of[4], (EXPERTS, D, FF), D ** -0.5, 0.109375, ((0, 8), (2, 2)))
    w_down = noise(streams_of[5], (EXPERTS, FF, D), FF ** -0.5, 0.15625, ((0, 8), (1, 2)))
    return {"tokens": tokens, "expert_ids": expert_ids, "gate_probs": gate_probs, "w_gate": w_gate, "w_up": w_up, "w_down": w_down}


def reference(tokens, expert_ids, gate_probs, w_gate, w_up, w_down):
    n_experts = w_gate.shape[0]
    routed = expert_ids.reshape(N_EP, TOK_EP * TOP)
    onehot = (routed[:, :, None] == jnp.arange(n_experts, dtype=jnp.int32)[None, None, :]).astype(jnp.int32)
    before = jnp.cumsum(onehot, axis=1) - onehot
    slots = jnp.sum(before * onehot, axis=2).astype(jnp.int32)
    source = jnp.arange(N_EP, dtype=jnp.int32)[:, None]
    positions = ((routed * N_EP + source) * CAP_SRC + slots).astype(jnp.int32).reshape(TOKENS * TOP)
    pair_token = jnp.repeat(jnp.arange(TOKENS, dtype=jnp.int32), TOP)
    owners = jnp.full((n_experts * N_EP * CAP_SRC,), TOKENS, jnp.int32).at[positions].set(pair_token)
    padded = jnp.concatenate([tokens, jnp.zeros((1, D), tokens.dtype)], 0)

    def expert_output(packed):
        row_index, gate_part, up_part, down_part = packed
        rows = padded[row_index]
        gated = jnp.dot(rows, gate_part, preferred_element_type=jnp.float32)
        lifted = jnp.dot(rows, up_part, preferred_element_type=jnp.float32)
        hidden = (jax.nn.silu(gated) * lifted).astype(jnp.bfloat16)
        return jnp.dot(hidden, down_part, preferred_element_type=jnp.float32).astype(jnp.bfloat16)

    outputs = lax.map(expert_output, (owners.reshape(n_experts, N_EP * CAP_SRC), w_gate, w_up, w_down))
    outputs = outputs.reshape(n_experts * N_EP * CAP_SRC, D)
    chosen = positions.reshape(TOKENS, TOP)
    mixed = jnp.zeros((TOKENS, D), jnp.float32)
    for choice_index in range(TOP):
        picked = outputs[chosen[:, choice_index]].astype(jnp.float32)
        mixed = mixed + gate_probs[:, choice_index][:, None] * picked
    return mixed.astype(jnp.bfloat16)
```

```python
import functools

import jax
import jax.numpy as jnp
from jax import lax
from jax.experimental import pallas as pl
from jax.experimental.pallas import tpu as pltpu
from jax.sharding import PartitionSpec as P

ROWS_BY_ROWS = (((1,), (1,)), ((), ()))
SPLITS = 3


def split_gates(expert_ids, gate_probs, n_experts):
    chosen = expert_ids[:, :, None] == jnp.arange(n_experts, dtype=jnp.int32)[None, None, :]
    rest = jnp.sum(jnp.where(chosen, gate_probs[:, :, None], 0.0), axis=1)
    terms = []
    for _ in range(SPLITS):
        term = lax.reduce_precision(rest, 8, 7)
        terms.append(term.astype(jnp.bfloat16))
        rest = rest - term
    return jnp.concatenate(terms, axis=1)


def expert_kernel(n_blocks, n_experts, place, *refs):
    own, across = refs[:n_blocks], refs[n_blocks : 2 * n_blocks]
    w_gate, w_up, w_down, mine, theirs, x = refs[2 * n_blocks :]
    lane, expert = place[0], place[1]
    half = mine.shape[1]
    start = 0
    for a, b in zip(own, across):
        span = slice(start, start + a.shape[0])
        start += a.shape[0]

        @pl.when(lane == 0)
        def _():
            x[span, :half] = a[:, :half]
            x[span, half:] = b[:, :half]

        @pl.when(lane != 0)
        def _():
            x[span, :half] = b[:, :half]
            x[span, half:] = a[:, :half]

    gated = lax.dot_general(x[...], w_gate[...], ROWS_BY_ROWS, preferred_element_type=jnp.float32)
    lifted = lax.dot_general(x[...], w_up[...], ROWS_BY_ROWS, preferred_element_type=jnp.float32)
    hidden = (gated / (1.0 + jnp.exp(-gated)) * lifted).astype(jnp.bfloat16)
    out = jnp.dot(hidden, w_down[...], preferred_element_type=jnp.float32)
    start = 0
    for a in own:
        span = slice(start, start + a.shape[0])
        start += a.shape[0]
        terms = a[:, half:].astype(jnp.float32)
        column = lax.broadcasted_iota(jnp.int32, terms.shape, 1)
        weight = jnp.sum(jnp.where(lax.rem(column, n_experts) == expert, terms, 0.0), axis=1, keepdims=True)
        low = (out[span, :half] * weight).astype(jnp.bfloat16)
        high = (out[span, half:] * weight).astype(jnp.bfloat16)

        @pl.when(lane == 0)
        def _():
            mine[span] = low
            theirs[span] = high

        @pl.when(lane != 0)
        def _():
            mine[span] = high
            theirs[span] = low


def run_expert(place, own, across, weights, n_experts):
    hidden, width = weights[0].shape
    rows = sum(a.shape[0] for a in own)
    vmem = pl.BlockSpec(memory_space=pltpu.VMEM)
    held = [pltpu.with_memory_space_constraint(w, pltpu.VMEM) for w in weights]
    return pl.pallas_call(
        functools.partial(expert_kernel, len(own), n_experts),
        out_shape=[jax.ShapeDtypeStruct((rows, width // 2), jnp.bfloat16)] * 2,
        in_specs=[pl.BlockSpec(memory_space=pltpu.SMEM)] + [vmem] * (2 * len(own) + 3),
        out_specs=[vmem] * 2,
        scratch_shapes=[pltpu.VMEM((rows, width), jnp.bfloat16)],
        compiler_params=pltpu.CompilerParams(vmem_limit_bytes=24 << 20),
        cost_estimate=pl.CostEstimate(flops=6 * rows * hidden * width, bytes_accessed=6 * hidden * width, transcendentals=0),
    )(place, *own, *across, *held)


def ring_body(tokens, expert_ids, gate_probs, w_gate, w_up, w_down):
    n = lax.axis_size("ep")
    rows, half = tokens.shape
    order = list(range(0, n, 2)) + list(range(n - 1, 0, -2))
    ahead = [(order[i], order[(i + 1) % n]) for i in range(n)]
    back = [(b, a) for a, b in ahead]
    swap = functools.partial(lax.ppermute, axis_name="tp", perm=[(0, 1), (1, 0)])
    far = n // 2
    place = jnp.stack([lax.axis_index("tp"), lax.axis_index("ep")]).astype(jnp.int32)
    weights = (w_gate[0].T, w_up[0].T, w_down[0])
    packed = jnp.concatenate([tokens, split_gates(expert_ids, gate_probs, n)], axis=1)

    came = {0: packed}
    for k in range(1, far):
        came[k] = lax.ppermute(came[k - 1], "ep", ahead)
        came[-k] = lax.ppermute(came[1 - k], "ep", back)
    far_low = lax.ppermute(came[far - 1][: rows // 2], "ep", ahead)
    far_high = lax.ppermute(came[1 - far][rows // 2 :], "ep", back)

    def expert(blocks):
        mine, theirs = run_expert(place, blocks, [swap(b) for b in blocks], weights, n)
        return mine.astype(jnp.float32) + swap(theirs).astype(jnp.float32)

    near = [0] + [s * k for k in range(1, far - 1) for s in (1, -1)]
    value = {}
    for group in (near[:3], near[3:]):
        out = expert([came[k] for k in group])
        for i, k in enumerate(group):
            value[k] = out[i * rows : (i + 1) * rows]
    out = expert([came[far - 1], came[1 - far], far_low, far_high])
    value[far - 1], value[1 - far] = out[:rows], out[rows : 2 * rows]
    far_value = out[2 * rows :]

    to_ahead = far_value[: rows // 2].astype(jnp.bfloat16)
    to_back = far_value[rows // 2 :].astype(jnp.bfloat16)
    pad_low, pad_high = ((0, rows - rows // 2), (0, 0)), ((rows // 2, 0), (0, 0))
    for k in range(far - 1, -1, -1):
        from_behind = lax.ppermute(to_ahead, "ep", ahead).astype(jnp.float32)
        from_front = lax.ppermute(to_back, "ep", back).astype(jnp.float32)
        if k == far - 1:
            from_behind, from_front = jnp.pad(from_behind, pad_low), jnp.pad(from_front, pad_high)
        if k:
            to_ahead = (value[-k] + from_behind).astype(jnp.bfloat16)
            to_back = (value[k] + from_front).astype(jnp.bfloat16)
    return (value[0] + from_behind + from_front).astype(jnp.bfloat16)


def swiglu_expert(rows, gate_part, up_part, down_part):
    gated = jnp.dot(rows, gate_part, preferred_element_type=jnp.float32)
    lifted = jnp.dot(rows, up_part, preferred_element_type=jnp.float32)
    hidden = (jax.nn.silu(gated) * lifted).astype(jnp.bfloat16)
    return jnp.dot(hidden, down_part, preferred_element_type=jnp.float32)


def slot_table(expert_ids, n_experts):
    routed = expert_ids.reshape(-1)
    pair_count = routed.shape[0]
    onehot = (routed[:, None] == jnp.arange(n_experts, dtype=jnp.int32)[None, :]).astype(
        jnp.bfloat16
    )
    row_index = lax.broadcasted_iota(jnp.int32, (pair_count, pair_count), 0)
    col_index = lax.broadcasted_iota(jnp.int32, (pair_count, pair_count), 1)
    earlier = (row_index > col_index).astype(jnp.bfloat16)
    before = jnp.dot(earlier, onehot, preferred_element_type=jnp.float32)
    slots = jnp.sum(before * onehot.astype(jnp.float32), axis=1).astype(jnp.int32)
    return (routed, slots)


def slot_body(tokens, expert_ids, gate_probs, w_gate, w_up, w_down):
    n_experts = lax.axis_size("ep")
    tok_rows, top_count = expert_ids.shape
    capacity = 3 * tok_rows * top_count // (2 * n_experts)
    routed, slots = slot_table(expert_ids, n_experts)
    positions = routed * capacity + slots
    pair_token = jnp.repeat(jnp.arange(tok_rows, dtype=jnp.int32), top_count)
    buffer_rows = n_experts * capacity
    owners = jnp.full((buffer_rows,), tok_rows, jnp.int32).at[positions].set(pair_token)
    half_slots = capacity // 2
    whole_tokens = lax.all_gather(tokens, "tp", axis=1, tiled=True)
    width = whole_tokens.shape[1]
    gate_full, up_full = (
        lax.all_gather(w_gate, "tp", axis=2, tiled=True),
        lax.all_gather(w_up, "tp", axis=2, tiled=True),
    )
    down_full = lax.all_gather(w_down, "tp", axis=1, tiled=True)
    padded = jnp.concatenate([whole_tokens, jnp.zeros((1, width), whole_tokens.dtype)], 0)
    outgoing = padded[owners].reshape(n_experts, capacity, width)
    lane = lax.axis_index("tp")
    mine = lax.dynamic_slice_in_dim(outgoing, lane * half_slots, half_slots, 1)
    block = lax.all_to_all(mine, "ep", split_axis=0, concat_axis=0, tiled=True)
    sources, items, columns = block.shape
    result = swiglu_expert(
        block.reshape(sources * items, columns), gate_full[0], up_full[0], down_full[0]
    )
    result = result.astype(jnp.bfloat16).reshape(sources, items, columns)
    returned = lax.all_to_all(result, "ep", split_axis=0, concat_axis=0, tiled=True)
    received = returned.reshape(n_experts * half_slots, width)
    in_half = slots // half_slots == lane
    local_pos = routed * half_slots + slots % half_slots
    picked = received[local_pos].astype(jnp.float32).reshape(tok_rows, top_count, width)
    weighted = jnp.where(in_half.reshape(tok_rows, top_count), gate_probs, 0.0)
    partial_value = jnp.sum(weighted[:, :, None] * picked, axis=1)
    return lax.psum_scatter(partial_value, "tp", scatter_dimension=1, tiled=True).astype(
        jnp.bfloat16
    )


def solution(mesh):
    in_specs = (
        P(("groups", "ep"), "tp"),
        P(("groups", "ep"), None),
        P(("groups", "ep"), None),
        P("ep", None, "tp"),
        P("ep", None, "tp"),
        P("ep", "tp", None),
    )
    out_specs = P(("groups", "ep"), "tp")

    def body(tokens, expert_ids, *rest):
        n, top = lax.axis_size("ep"), expert_ids.shape[1]
        small = n <= 4 * top and n % 2 == 0 and n >= 6 and lax.axis_size("tp") == 2
        return (ring_body if small else slot_body)(tokens, expert_ids, *rest)

    return jax.shard_map(body, mesh=mesh, in_specs=in_specs, out_specs=out_specs, check_vma=False)
```

```python
import functools

import jax
import jax.numpy as jnp
from jax import lax
from jax.experimental import pallas as pl
from jax.experimental.pallas import tpu as pltpu
from jax.sharding import PartitionSpec as P

SPLITS = 3


def in_vmem(shape, dtype=jnp.bfloat16):
    return pltpu.MemorySpace.VMEM(shape, dtype)


def hold(x):
    return pltpu.with_memory_space_constraint(x, pltpu.VMEM)


def after(x, done):
    return lax.optimization_barrier((x, done))[0]


def pack_kernel(n_experts, tokens, ids, probs, packed):
    top, rows = ids.shape
    half = tokens.shape[1]
    packed[:, :half] = tokens[...]
    expert = lax.broadcasted_iota(jnp.int32, (n_experts, rows), 0)
    rest = jnp.zeros((n_experts, rows), jnp.float32)
    for k in range(top):
        rest += jnp.where(ids[k : k + 1, :] == expert, probs[k : k + 1, :], 0.0)
    terms = []
    for _ in range(SPLITS):
        term = rest.astype(jnp.bfloat16).astype(jnp.float32)
        terms.append(term)
        rest = rest - term
    packed[:, half:] = jnp.concatenate(terms, axis=0).T.astype(jnp.bfloat16)


def pack(tokens, expert_ids, gate_probs, n_experts):
    rows, half = tokens.shape
    return pl.pallas_call(
        functools.partial(pack_kernel, n_experts),
        out_shape=in_vmem((rows, half + SPLITS * n_experts)),
        compiler_params=pltpu.CompilerParams(vmem_limit_bytes=8 << 20),
    )(tokens, expert_ids.T, gate_probs.T)


def load_kernel(place, gate_in, up_in, down_in, gate, up, down_mine, down_theirs, done, gate_buf, up_buf, down_buf, sems):
    lane = place[0]
    half = down_mine.shape[1]
    copies = [
        pltpu.make_async_copy(src, dst, sems.at[i])
        for i, (src, dst) in enumerate(((gate_in, gate_buf), (up_in, up_buf), (down_in, down_buf)))
    ]
    for copy in copies:
        copy.start()
    copies[0].wait()
    gate[...] = gate_buf[...].T
    copies[1].wait()
    up[...] = up_buf[...].T
    copies[2].wait()

    @pl.when(lane == 0)
    def _():
        down_mine[...] = down_buf[:, :half]
        down_theirs[...] = down_buf[:, half:]

    @pl.when(lane != 0)
    def _():
        down_mine[...] = down_buf[:, half:]
        down_theirs[...] = down_buf[:, :half]

    done[...] = jnp.zeros_like(done)


def load_weights(place, w_gate, w_up, w_down):
    hidden, width = w_down.shape
    return pl.pallas_call(
        load_kernel,
        out_shape=[in_vmem((width, hidden))] * 2 + [in_vmem((hidden, width // 2))] * 2 + [in_vmem((8, 128), jnp.float32)],
        in_specs=[pl.BlockSpec(memory_space=pltpu.SMEM)] + [pl.BlockSpec(memory_space=pltpu.HBM)] * 3,
        out_specs=[pl.BlockSpec(memory_space=pltpu.VMEM)] * 5,
        scratch_shapes=[pltpu.VMEM((hidden, width), jnp.bfloat16)] * 3 + [pltpu.SemaphoreType.DMA((3,))],
        compiler_params=pltpu.CompilerParams(vmem_limit_bytes=32 << 20),
        cost_estimate=pl.CostEstimate(flops=0, bytes_accessed=12 * hidden * width, transcendentals=0),
    )(place, *[pltpu.with_memory_space_constraint(w, pltpu.HBM) for w in (w_gate.T, w_up.T, w_down)])


def expert_kernel(n_blocks, n_experts, place, *refs):
    own, across = refs[:n_blocks], refs[n_blocks : 2 * n_blocks]
    w_gate, w_up, down_mine, down_theirs, mine, theirs, x_own, x_across = refs[2 * n_blocks :]
    lane, expert = place[0], place[1]
    half = mine.shape[1]
    spans, start = [], 0
    for a, b in zip(own, across):
        spans.append(slice(start, start + a.shape[0]))
        x_own[spans[-1], :] = a[:, :half]
        x_across[spans[-1], :] = b[:, :half]
        start += a.shape[0]
    here = pl.ds(pl.multiple_of(lane * half, 16), half)
    there = pl.ds(pl.multiple_of((1 - lane) * half, 16), half)

    def project(w):
        near = jnp.dot(x_own[...], w[here, :], preferred_element_type=jnp.float32)
        return near + jnp.dot(x_across[...], w[there, :], preferred_element_type=jnp.float32)

    gated = project(w_gate)
    lifted = project(w_up)
    hidden = (gated / (1.0 + jnp.exp(-gated)) * lifted).astype(jnp.bfloat16)
    weights = []
    for a in own:
        terms = a[:, half:].astype(jnp.float32)
        column = lax.broadcasted_iota(jnp.int32, terms.shape, 1)
        weights.append(jnp.sum(jnp.where(lax.rem(column, n_experts) == expert, terms, 0.0), axis=1, keepdims=True))
    for w, out in ((down_theirs, theirs), (down_mine, mine)):
        value = jnp.dot(hidden, w[...], preferred_element_type=jnp.float32)
        for span, weight in zip(spans, weights):
            out[span] = (value[span] * weight).astype(jnp.bfloat16)


def run_expert(place, own, across, weights, n_experts):
    width, hidden = weights[0].shape
    rows = sum(a.shape[0] for a in own)
    vmem = pl.BlockSpec(memory_space=pltpu.VMEM)
    return pl.pallas_call(
        functools.partial(expert_kernel, len(own), n_experts),
        out_shape=[in_vmem((rows, width // 2))] * 2,
        in_specs=[pl.BlockSpec(memory_space=pltpu.SMEM)] + [vmem] * (2 * len(own) + 4),
        out_specs=[vmem] * 2,
        scratch_shapes=[pltpu.VMEM((rows, width // 2), jnp.bfloat16)] * 2,
        compiler_params=pltpu.CompilerParams(vmem_limit_bytes=16 << 20),
        cost_estimate=pl.CostEstimate(flops=6 * rows * hidden * width, bytes_accessed=6 * hidden * width, transcendentals=0),
    )(place, *[hold(a) for a in own], *[hold(a) for a in across], *[hold(w) for w in weights])


def ring_body(tokens, expert_ids, gate_probs, w_gate, w_up, w_down):
    n = lax.axis_size("ep")
    rows = tokens.shape[0]
    order = list(range(0, n, 2)) + list(range(n - 1, 0, -2))
    ahead = [(order[i], order[(i + 1) % n]) for i in range(n)]
    back = [(b, a) for a, b in ahead]
    swap = functools.partial(lax.ppermute, axis_name="tp", perm=[(0, 1), (1, 0)])
    far = n // 2
    place = jnp.stack([lax.axis_index("tp"), lax.axis_index("ep")]).astype(jnp.int32)
    packed = pack(tokens, expert_ids, gate_probs, n)
    *weights, loaded = load_weights(after(place, packed), w_gate[0], w_up[0], w_down[0])

    came, across, value = {0: packed}, {}, {}

    def run(keys, wait_for=None):
        at = place if wait_for is None else after(place, wait_for)
        mine, theirs = run_expert(at, [came[k] for k in keys], [across[k] for k in keys], weights, n)
        theirs = swap(theirs)
        start = 0
        for k in keys:
            span = slice(start, start + came[k].shape[0])
            start = span.stop
            value[k] = mine[span].astype(jnp.float32) + theirs[span].astype(jnp.float32)
        return mine

    hidden_work = loaded
    for k in range(1, far):
        came[k] = lax.ppermute(after(came[k - 1], hidden_work) if k > 1 else packed, "ep", ahead)
        came[-k] = lax.ppermute(after(came[1 - k], hidden_work) if k > 1 else packed, "ep", back)
        across[k - 1] = swap(came[k - 1])
        if k > 1:
            across[1 - k] = swap(came[1 - k])
            hidden_work = run([0] if k == 2 else [k - 2, 2 - k])
    far_keys = ("low", "high")
    came["low"] = lax.ppermute(after(came[far - 1], hidden_work)[: rows // 2], "ep", ahead)
    came["high"] = lax.ppermute(after(came[1 - far], hidden_work)[rows // 2 :], "ep", back)
    for k in (far - 1, 1 - far, *far_keys):
        across[k] = swap(came[k])
    run(far_keys)

    to_ahead = value["low"].astype(jnp.bfloat16)
    to_back = value["high"].astype(jnp.bfloat16)
    run([far - 1, 1 - far], (to_ahead, to_back))
    pad_low, pad_high = ((0, rows - rows // 2), (0, 0)), ((rows // 2, 0), (0, 0))
    for k in range(far - 1, -1, -1):
        behind = lax.ppermute(to_ahead, "ep", ahead)
        front = lax.ppermute(to_back, "ep", back)
        if k == far - 1:
            run([far - 2, 2 - far], (behind, front))
        behind, front = behind.astype(jnp.float32), front.astype(jnp.float32)
        if k == far - 1:
            behind, front = jnp.pad(behind, pad_low), jnp.pad(front, pad_high)
        if k:
            to_ahead = (value[-k] + behind).astype(jnp.bfloat16)
            to_back = (value[k] + front).astype(jnp.bfloat16)
    return (value[0] + behind + front).astype(jnp.bfloat16)


def swiglu_expert(rows, gate_part, up_part, down_part):
    gated = jnp.dot(rows, gate_part, preferred_element_type=jnp.float32)
    lifted = jnp.dot(rows, up_part, preferred_element_type=jnp.float32)
    hidden = (jax.nn.silu(gated) * lifted).astype(jnp.bfloat16)
    return jnp.dot(hidden, down_part, preferred_element_type=jnp.float32)


def slot_table(expert_ids, n_experts):
    routed = expert_ids.reshape(-1)
    pair_count = routed.shape[0]
    onehot = (routed[:, None] == jnp.arange(n_experts, dtype=jnp.int32)[None, :]).astype(
        jnp.bfloat16
    )
    row_index = lax.broadcasted_iota(jnp.int32, (pair_count, pair_count), 0)
    col_index = lax.broadcasted_iota(jnp.int32, (pair_count, pair_count), 1)
    earlier = (row_index > col_index).astype(jnp.bfloat16)
    before = jnp.dot(earlier, onehot, preferred_element_type=jnp.float32)
    slots = jnp.sum(before * onehot.astype(jnp.float32), axis=1).astype(jnp.int32)
    return (routed, slots)


def slot_body(tokens, expert_ids, gate_probs, w_gate, w_up, w_down):
    n_experts = lax.axis_size("ep")
    tok_rows, top_count = expert_ids.shape
    capacity = 3 * tok_rows * top_count // (2 * n_experts)
    routed, slots = slot_table(expert_ids, n_experts)
    positions = routed * capacity + slots
    pair_token = jnp.repeat(jnp.arange(tok_rows, dtype=jnp.int32), top_count)
    buffer_rows = n_experts * capacity
    owners = jnp.full((buffer_rows,), tok_rows, jnp.int32).at[positions].set(pair_token)
    half_slots = capacity // 2
    whole_tokens = lax.all_gather(tokens, "tp", axis=1, tiled=True)
    width = whole_tokens.shape[1]
    gate_full, up_full = (
        lax.all_gather(w_gate, "tp", axis=2, tiled=True),
        lax.all_gather(w_up, "tp", axis=2, tiled=True),
    )
    down_full = lax.all_gather(w_down, "tp", axis=1, tiled=True)
    padded = jnp.concatenate([whole_tokens, jnp.zeros((1, width), whole_tokens.dtype)], 0)
    outgoing = padded[owners].reshape(n_experts, capacity, width)
    lane = lax.axis_index("tp")
    mine = lax.dynamic_slice_in_dim(outgoing, lane * half_slots, half_slots, 1)
    block = lax.all_to_all(mine, "ep", split_axis=0, concat_axis=0, tiled=True)
    sources, items, columns = block.shape
    result = swiglu_expert(
        block.reshape(sources * items, columns), gate_full[0], up_full[0], down_full[0]
    )
    result = result.astype(jnp.bfloat16).reshape(sources, items, columns)
    returned = lax.all_to_all(result, "ep", split_axis=0, concat_axis=0, tiled=True)
    received = returned.reshape(n_experts * half_slots, width)
    in_half = slots // half_slots == lane
    local_pos = routed * half_slots + slots % half_slots
    picked = received[local_pos].astype(jnp.float32).reshape(tok_rows, top_count, width)
    weighted = jnp.where(in_half.reshape(tok_rows, top_count), gate_probs, 0.0)
    partial_value = jnp.sum(weighted[:, :, None] * picked, axis=1)
    return lax.psum_scatter(partial_value, "tp", scatter_dimension=1, tiled=True).astype(
        jnp.bfloat16
    )


def solution(mesh):
    in_specs = (
        P(("groups", "ep"), "tp"),
        P(("groups", "ep"), None),
        P(("groups", "ep"), None),
        P("ep", None, "tp"),
        P("ep", None, "tp"),
        P("ep", "tp", None),
    )
    out_specs = P(("groups", "ep"), "tp")

    def body(tokens, expert_ids, *rest):
        n, top = lax.axis_size("ep"), expert_ids.shape[1]
        small = n <= 4 * top and n % 2 == 0 and n >= 6 and lax.axis_size("tp") == 2
        return (ring_body if small else slot_body)(tokens, expert_ids, *rest)

    return jax.shard_map(body, mesh=mesh, in_specs=in_specs, out_specs=out_specs, check_vma=False)
```

```python
import functools

import jax
import jax.numpy as jnp
from jax import lax
from jax.experimental import pallas as pl
from jax.experimental.pallas import tpu as pltpu
from jax.sharding import PartitionSpec as P

SPLITS = 3


def in_vmem(shape, dtype=jnp.bfloat16):
    return pltpu.MemorySpace.VMEM(shape, dtype)


def hold(x):
    return pltpu.with_memory_space_constraint(x, pltpu.VMEM)


def after(x, done):
    return lax.optimization_barrier((x, done))[0]


def pack_kernel(n_experts, tokens_in, ids_in, probs_in, packed, tokens, ids, probs, sems):
    copies = [
        pltpu.make_async_copy(src, dst, sems.at[i])
        for i, (src, dst) in enumerate(((ids_in, ids), (probs_in, probs), (tokens_in, tokens)))
    ]
    for copy in copies:
        copy.start()
    top, rows = ids.shape
    half = tokens.shape[1]
    copies[0].wait()
    copies[1].wait()
    expert = lax.broadcasted_iota(jnp.int32, (n_experts, rows), 0)
    rest = jnp.zeros((n_experts, rows), jnp.float32)
    for k in range(top):
        rest += jnp.where(ids[k : k + 1, :] == expert, probs[k : k + 1, :], 0.0)
    terms = []
    for _ in range(SPLITS):
        term = rest.astype(jnp.bfloat16).astype(jnp.float32)
        terms.append(term)
        rest = rest - term
    packed[:, half:] = jnp.concatenate(terms, axis=0).T.astype(jnp.bfloat16)
    copies[2].wait()
    packed[:, :half] = tokens[...]


def pack(tokens, expert_ids, gate_probs, n_experts):
    rows, half = tokens.shape
    args = (tokens, expert_ids.T, gate_probs.T)
    return pl.pallas_call(
        functools.partial(pack_kernel, n_experts),
        out_shape=in_vmem((rows, half + SPLITS * n_experts)),
        in_specs=[pl.BlockSpec(memory_space=pltpu.HBM)] * 3,
        out_specs=pl.BlockSpec(memory_space=pltpu.VMEM),
        scratch_shapes=[pltpu.VMEM(a.shape, a.dtype) for a in args] + [pltpu.SemaphoreType.DMA((3,))],
        compiler_params=pltpu.CompilerParams(vmem_limit_bytes=8 << 20),
    )(*[pltpu.with_memory_space_constraint(a, pltpu.HBM) for a in args])


def turn_kernel(after_this, gate_in, up_in, gate, up, gate_buf, up_buf, sems):
    copies = [
        pltpu.make_async_copy(src, dst, sems.at[i])
        for i, (src, dst) in enumerate(((gate_in, gate_buf), (up_in, up_buf)))
    ]
    for copy in copies:
        copy.start()
    for copy, buf, out in zip(copies, (gate_buf, up_buf), (gate, up)):
        copy.wait()
        out[...] = buf[...].T


def turn_weights(after_this, *weights):
    hidden, width = weights[0].shape
    return pl.pallas_call(
        turn_kernel,
        out_shape=[in_vmem((width, hidden))] * 2,
        in_specs=[pl.BlockSpec(memory_space=pltpu.SMEM)] + [pl.BlockSpec(memory_space=pltpu.HBM)] * 2,
        out_specs=[pl.BlockSpec(memory_space=pltpu.VMEM)] * 2,
        scratch_shapes=[pltpu.VMEM((hidden, width), jnp.bfloat16)] * 2 + [pltpu.SemaphoreType.DMA((2,))],
        compiler_params=pltpu.CompilerParams(vmem_limit_bytes=32 << 20),
        cost_estimate=pl.CostEstimate(flops=0, bytes_accessed=8 * hidden * width, transcendentals=0),
    )(after_this, *[pltpu.with_memory_space_constraint(w, pltpu.HBM) for w in weights])


def halve_kernel(place, down_in, down_mine, down_theirs, down_buf, sem):
    lane = place[0]
    half = down_mine.shape[1]
    copy = pltpu.make_async_copy(down_in, down_buf, sem)
    copy.start()
    copy.wait()

    @pl.when(lane == 0)
    def _():
        down_mine[...] = down_buf[:, :half]
        down_theirs[...] = down_buf[:, half:]

    @pl.when(lane != 0)
    def _():
        down_mine[...] = down_buf[:, half:]
        down_theirs[...] = down_buf[:, :half]


def halve_weights(place, w_down):
    hidden, width = w_down.shape
    return pl.pallas_call(
        halve_kernel,
        out_shape=[in_vmem((hidden, width // 2))] * 2,
        in_specs=[pl.BlockSpec(memory_space=pltpu.SMEM), pl.BlockSpec(memory_space=pltpu.HBM)],
        out_specs=[pl.BlockSpec(memory_space=pltpu.VMEM)] * 2,
        scratch_shapes=[pltpu.VMEM((hidden, width), jnp.bfloat16), pltpu.SemaphoreType.DMA],
        compiler_params=pltpu.CompilerParams(vmem_limit_bytes=32 << 20),
        cost_estimate=pl.CostEstimate(flops=0, bytes_accessed=8 * hidden * width, transcendentals=0),
    )(place, pltpu.with_memory_space_constraint(w_down, pltpu.HBM))


def expert_kernel(n_blocks, n_experts, place, *refs):
    own, across = refs[:n_blocks], refs[n_blocks : 2 * n_blocks]
    w_gate, w_up, down_mine, down_theirs, mine, theirs, x_own, x_across = refs[2 * n_blocks :]
    lane, expert = place[0], place[1]
    half = mine.shape[1]
    spans, start = [], 0
    for a, b in zip(own, across):
        spans.append(slice(start, start + a.shape[0]))
        x_own[spans[-1], :] = a[:, :half]
        x_across[spans[-1], :] = b[:, :half]
        start += a.shape[0]
    here = pl.ds(pl.multiple_of(lane * half, 16), half)
    there = pl.ds(pl.multiple_of((1 - lane) * half, 16), half)

    def project(w):
        near = jnp.dot(x_own[...], w[here, :], preferred_element_type=jnp.float32)
        return near + jnp.dot(x_across[...], w[there, :], preferred_element_type=jnp.float32)

    gated = project(w_gate)
    lifted = project(w_up)
    hidden = (gated / (1.0 + jnp.exp(-gated)) * lifted).astype(jnp.bfloat16)
    weights = []
    for a in own:
        terms = a[:, half:].astype(jnp.float32)
        column = lax.broadcasted_iota(jnp.int32, terms.shape, 1)
        weights.append(jnp.sum(jnp.where(lax.rem(column, n_experts) == expert, terms, 0.0), axis=1, keepdims=True))
    for w, out in ((down_theirs, theirs), (down_mine, mine)):
        value = jnp.dot(hidden, w[...], preferred_element_type=jnp.float32)
        for span, weight in zip(spans, weights):
            out[span] = (value[span] * weight).astype(jnp.bfloat16)


def run_expert(place, own, across, weights, n_experts):
    width, hidden = weights[0].shape
    rows = sum(a.shape[0] for a in own)
    vmem = pl.BlockSpec(memory_space=pltpu.VMEM)
    return pl.pallas_call(
        functools.partial(expert_kernel, len(own), n_experts),
        out_shape=[in_vmem((rows, width // 2))] * 2,
        in_specs=[pl.BlockSpec(memory_space=pltpu.SMEM)] + [vmem] * (2 * len(own) + 4),
        out_specs=[vmem] * 2,
        scratch_shapes=[pltpu.VMEM((rows, width // 2), jnp.bfloat16)] * 2,
        compiler_params=pltpu.CompilerParams(vmem_limit_bytes=16 << 20),
        cost_estimate=pl.CostEstimate(flops=6 * rows * hidden * width, bytes_accessed=6 * hidden * width, transcendentals=0),
    )(place, *[hold(a) for a in own], *[hold(a) for a in across], *[hold(w) for w in weights])


def ring_body(tokens, expert_ids, gate_probs, w_gate, w_up, w_down):
    n = lax.axis_size("ep")
    rows = tokens.shape[0]
    order = list(range(0, n, 2)) + list(range(n - 1, 0, -2))
    ahead = [(order[i], order[(i + 1) % n]) for i in range(n)]
    back = [(b, a) for a, b in ahead]
    swap = functools.partial(lax.ppermute, axis_name="tp", perm=[(0, 1), (1, 0)])
    far = n // 2
    place = jnp.stack([lax.axis_index("tp"), lax.axis_index("ep")]).astype(jnp.int32)
    packed = pack(tokens, expert_ids, gate_probs, n)
    gate, up = turn_weights(after(place, packed), w_gate[0].T, w_up[0].T)

    came, across, value = {0: packed}, {}, {}

    def run(keys, wait_for=None):
        at = place if wait_for is None else after(place, wait_for)
        mine, theirs = run_expert(at, [came[k] for k in keys], [across[k] for k in keys], weights, n)
        done, theirs = theirs, swap(theirs)
        start = 0
        for k in keys:
            span = slice(start, start + came[k].shape[0])
            start = span.stop
            value[k] = mine[span].astype(jnp.float32) + theirs[span].astype(jnp.float32)
        return done

    came[1] = lax.ppermute(packed, "ep", ahead)
    came[-1] = lax.ppermute(packed, "ep", back)
    across[0] = swap(packed)
    weights, done = [gate, up], up
    for k in range(2, far):
        came[k - 1], came[1 - k] = after((came[k - 1], came[1 - k]), done)
        came[k] = lax.ppermute(came[k - 1], "ep", ahead)
        came[-k] = lax.ppermute(came[1 - k], "ep", back)
        across[k - 1], across[1 - k] = swap(came[k - 1]), swap(came[1 - k])
        if k == 2:
            weights += halve_weights(after(place, came[1]), w_down[0])
            done = weights[-1]
        else:
            done = run([k - 2, 2 - k])
    came[far - 1], came[1 - far] = after((came[far - 1], came[1 - far]), done)
    came["low"] = lax.ppermute(came[far - 1][: rows // 2], "ep", ahead)
    came["high"] = lax.ppermute(came[1 - far][rows // 2 :], "ep", back)
    across[far - 1], across[1 - far] = swap(came[far - 1]), swap(came[1 - far])
    done = run([far - 1, 1 - far])
    came["low"], came["high"] = after((came["low"], came["high"]), done)
    across["low"], across["high"] = swap(came["low"]), swap(came["high"])
    done = run(["low", "high"])
    run([far - 2, 2 - far], done)
    run([0], done)

    to_ahead = value["low"].astype(jnp.bfloat16)
    to_back = value["high"].astype(jnp.bfloat16)
    pad_low, pad_high = ((0, rows - rows // 2), (0, 0)), ((rows // 2, 0), (0, 0))
    for k in range(far - 1, -1, -1):
        behind = lax.ppermute(to_ahead, "ep", ahead)
        front = lax.ppermute(to_back, "ep", back)
        behind, front = behind.astype(jnp.float32), front.astype(jnp.float32)
        if k == far - 1:
            behind, front = jnp.pad(behind, pad_low), jnp.pad(front, pad_high)
        if k:
            to_ahead = (value[-k] + behind).astype(jnp.bfloat16)
            to_back = (value[k] + front).astype(jnp.bfloat16)
    return (value[0] + behind + front).astype(jnp.bfloat16)


def swiglu_expert(rows, gate_part, up_part, down_part):
    gated = jnp.dot(rows, gate_part, preferred_element_type=jnp.float32)
    lifted = jnp.dot(rows, up_part, preferred_element_type=jnp.float32)
    hidden = (jax.nn.silu(gated) * lifted).astype(jnp.bfloat16)
    return jnp.dot(hidden, down_part, preferred_element_type=jnp.float32)


def slot_table(expert_ids, n_experts):
    routed = expert_ids.reshape(-1)
    pair_count = routed.shape[0]
    onehot = (routed[:, None] == jnp.arange(n_experts, dtype=jnp.int32)[None, :]).astype(
        jnp.bfloat16
    )
    row_index = lax.broadcasted_iota(jnp.int32, (pair_count, pair_count), 0)
    col_index = lax.broadcasted_iota(jnp.int32, (pair_count, pair_count), 1)
    earlier = (row_index > col_index).astype(jnp.bfloat16)
    before = jnp.dot(earlier, onehot, preferred_element_type=jnp.float32)
    slots = jnp.sum(before * onehot.astype(jnp.float32), axis=1).astype(jnp.int32)
    return (routed, slots)


def slot_body(tokens, expert_ids, gate_probs, w_gate, w_up, w_down):
    n_experts = lax.axis_size("ep")
    tok_rows, top_count = expert_ids.shape
    capacity = 3 * tok_rows * top_count // (2 * n_experts)
    routed, slots = slot_table(expert_ids, n_experts)
    positions = routed * capacity + slots
    pair_token = jnp.repeat(jnp.arange(tok_rows, dtype=jnp.int32), top_count)
    buffer_rows = n_experts * capacity
    owners = jnp.full((buffer_rows,), tok_rows, jnp.int32).at[positions].set(pair_token)
    half_slots = capacity // 2
    whole_tokens = lax.all_gather(tokens, "tp", axis=1, tiled=True)
    width = whole_tokens.shape[1]
    gate_full, up_full = (
        lax.all_gather(w_gate, "tp", axis=2, tiled=True),
        lax.all_gather(w_up, "tp", axis=2, tiled=True),
    )
    down_full = lax.all_gather(w_down, "tp", axis=1, tiled=True)
    padded = jnp.concatenate([whole_tokens, jnp.zeros((1, width), whole_tokens.dtype)], 0)
    outgoing = padded[owners].reshape(n_experts, capacity, width)
    lane = lax.axis_index("tp")
    mine = lax.dynamic_slice_in_dim(outgoing, lane * half_slots, half_slots, 1)
    block = lax.all_to_all(mine, "ep", split_axis=0, concat_axis=0, tiled=True)
    sources, items, columns = block.shape
    result = swiglu_expert(
        block.reshape(sources * items, columns), gate_full[0], up_full[0], down_full[0]
    )
    result = result.astype(jnp.bfloat16).reshape(sources, items, columns)
    returned = lax.all_to_all(result, "ep", split_axis=0, concat_axis=0, tiled=True)
    received = returned.reshape(n_experts * half_slots, width)
    in_half = slots // half_slots == lane
    local_pos = routed * half_slots + slots % half_slots
    picked = received[local_pos].astype(jnp.float32).reshape(tok_rows, top_count, width)
    weighted = jnp.where(in_half.reshape(tok_rows, top_count), gate_probs, 0.0)
    partial_value = jnp.sum(weighted[:, :, None] * picked, axis=1)
    return lax.psum_scatter(partial_value, "tp", scatter_dimension=1, tiled=True).astype(
        jnp.bfloat16
    )


def solution(mesh):
    in_specs = (
        P(("groups", "ep"), "tp"),
        P(("groups", "ep"), None),
        P(("groups", "ep"), None),
        P("ep", None, "tp"),
        P("ep", None, "tp"),
        P("ep", "tp", None),
    )
    out_specs = P(("groups", "ep"), "tp")

    def body(tokens, expert_ids, *rest):
        n, top = lax.axis_size("ep"), expert_ids.shape[1]
        small = n <= 4 * top and n % 2 == 0 and n >= 6 and lax.axis_size("tp") == 2
        return (ring_body if small else slot_body)(tokens, expert_ids, *rest)

    return jax.shard_map(body, mesh=mesh, in_specs=in_specs, out_specs=out_specs, check_vma=False)
```

```python
import functools

import jax
import jax.numpy as jnp
from jax import lax
from jax.experimental import pallas as pl
from jax.experimental.pallas import tpu as pltpu
from jax.sharding import PartitionSpec as P

SPLITS = 3


def in_vmem(shape, dtype=jnp.bfloat16):
    return pltpu.MemorySpace.VMEM(shape, dtype)


def hold(x):
    return pltpu.with_memory_space_constraint(x, pltpu.VMEM)


def after(x, done):
    return lax.optimization_barrier((x, done))[0]


def pack_kernel(n_experts, tokens_in, ids_in, probs_in, packed, tokens, ids, probs, sems):
    copies = [
        pltpu.make_async_copy(src, dst, sems.at[i])
        for i, (src, dst) in enumerate(((ids_in, ids), (probs_in, probs), (tokens_in, tokens)))
    ]
    for copy in copies:
        copy.start()
    top, rows = ids.shape
    half = tokens.shape[1]
    copies[0].wait()
    copies[1].wait()
    expert = lax.broadcasted_iota(jnp.int32, (n_experts, rows), 0)
    rest = jnp.zeros((n_experts, rows), jnp.float32)
    for k in range(top):
        rest += jnp.where(ids[k : k + 1, :] == expert, probs[k : k + 1, :], 0.0)
    terms = []
    for _ in range(SPLITS):
        term = rest.astype(jnp.bfloat16).astype(jnp.float32)
        terms.append(term)
        rest = rest - term
    packed[:, half:] = jnp.concatenate(terms, axis=0).T.astype(jnp.bfloat16)
    copies[2].wait()
    packed[:, :half] = tokens[...]


def pack(tokens, expert_ids, gate_probs, n_experts):
    rows, half = tokens.shape
    args = (tokens, expert_ids.T, gate_probs.T)
    return pl.pallas_call(
        functools.partial(pack_kernel, n_experts),
        out_shape=in_vmem((rows, half + SPLITS * n_experts)),
        in_specs=[pl.BlockSpec(memory_space=pltpu.HBM)] * 3,
        out_specs=pl.BlockSpec(memory_space=pltpu.VMEM),
        scratch_shapes=[pltpu.VMEM(a.shape, a.dtype) for a in args] + [pltpu.SemaphoreType.DMA((3,))],
        compiler_params=pltpu.CompilerParams(vmem_limit_bytes=8 << 20),
    )(*[pltpu.with_memory_space_constraint(a, pltpu.HBM) for a in args])


def turn_kernel(after_this, gate_in, up_in, gate, up, gate_buf, up_buf, sems):
    copies = [
        pltpu.make_async_copy(src, dst, sems.at[i])
        for i, (src, dst) in enumerate(((gate_in, gate_buf), (up_in, up_buf)))
    ]
    for copy in copies:
        copy.start()
    for copy, buf, out in zip(copies, (gate_buf, up_buf), (gate, up)):
        copy.wait()
        out[...] = buf[...].T


def turn_weights(after_this, *weights):
    hidden, width = weights[0].shape
    return pl.pallas_call(
        turn_kernel,
        out_shape=[in_vmem((width, hidden))] * 2,
        in_specs=[pl.BlockSpec(memory_space=pltpu.SMEM)] + [pl.BlockSpec(memory_space=pltpu.HBM)] * 2,
        out_specs=[pl.BlockSpec(memory_space=pltpu.VMEM)] * 2,
        scratch_shapes=[pltpu.VMEM((hidden, width), jnp.bfloat16)] * 2 + [pltpu.SemaphoreType.DMA((2,))],
        compiler_params=pltpu.CompilerParams(vmem_limit_bytes=32 << 20),
        cost_estimate=pl.CostEstimate(flops=0, bytes_accessed=8 * hidden * width, transcendentals=0),
    )(after_this, *[pltpu.with_memory_space_constraint(w, pltpu.HBM) for w in weights])


def halve_kernel(place, down_in, down_mine, down_theirs, down_buf, sem):
    lane = place[0]
    half = down_mine.shape[1]
    copy = pltpu.make_async_copy(down_in, down_buf, sem)
    copy.start()
    copy.wait()

    @pl.when(lane == 0)
    def _():
        down_mine[...] = down_buf[:, :half]
        down_theirs[...] = down_buf[:, half:]

    @pl.when(lane != 0)
    def _():
        down_mine[...] = down_buf[:, half:]
        down_theirs[...] = down_buf[:, :half]


def halve_weights(place, w_down):
    hidden, width = w_down.shape
    return pl.pallas_call(
        halve_kernel,
        out_shape=[in_vmem((hidden, width // 2))] * 2,
        in_specs=[pl.BlockSpec(memory_space=pltpu.SMEM), pl.BlockSpec(memory_space=pltpu.HBM)],
        out_specs=[pl.BlockSpec(memory_space=pltpu.VMEM)] * 2,
        scratch_shapes=[pltpu.VMEM((hidden, width), jnp.bfloat16), pltpu.SemaphoreType.DMA],
        compiler_params=pltpu.CompilerParams(vmem_limit_bytes=32 << 20),
        cost_estimate=pl.CostEstimate(flops=0, bytes_accessed=8 * hidden * width, transcendentals=0),
    )(place, pltpu.with_memory_space_constraint(w_down, pltpu.HBM))


def expert_kernel(n_blocks, n_experts, place, *refs):
    own, across = refs[:n_blocks], refs[n_blocks : 2 * n_blocks]
    w_gate, w_up, down_mine, down_theirs, mine, theirs, x_own, x_across = refs[2 * n_blocks :]
    lane, expert = place[0], place[1]
    half = mine.shape[1]
    spans, start = [], 0
    for a, b in zip(own, across):
        spans.append(slice(start, start + a.shape[0]))
        x_own[spans[-1], :] = a[:, :half]
        x_across[spans[-1], :] = b[:, :half]
        start += a.shape[0]
    here = pl.ds(pl.multiple_of(lane * half, 16), half)
    there = pl.ds(pl.multiple_of((1 - lane) * half, 16), half)

    def project(w):
        near = jnp.dot(x_own[...], w[here, :], preferred_element_type=jnp.float32)
        return near + jnp.dot(x_across[...], w[there, :], preferred_element_type=jnp.float32)

    gated = project(w_gate)
    lifted = project(w_up)
    hidden = (gated / (1.0 + jnp.exp(-gated)) * lifted).astype(jnp.bfloat16)
    weights = []
    for a in own:
        terms = a[:, half:].astype(jnp.float32)
        column = lax.broadcasted_iota(jnp.int32, terms.shape, 1)
        weights.append(jnp.sum(jnp.where(lax.rem(column, n_experts) == expert, terms, 0.0), axis=1, keepdims=True))
    for w, out in ((down_theirs, theirs), (down_mine, mine)):
        value = jnp.dot(hidden, w[...], preferred_element_type=jnp.float32)
        for span, weight in zip(spans, weights):
            out[span] = (value[span] * weight).astype(jnp.bfloat16)


def run_expert(place, own, across, weights, n_experts):
    width, hidden = weights[0].shape
    rows = sum(a.shape[0] for a in own)
    vmem = pl.BlockSpec(memory_space=pltpu.VMEM)
    return pl.pallas_call(
        functools.partial(expert_kernel, len(own), n_experts),
        out_shape=[in_vmem((rows, width // 2))] * 2,
        in_specs=[pl.BlockSpec(memory_space=pltpu.SMEM)] + [vmem] * (2 * len(own) + 4),
        out_specs=[vmem] * 2,
        scratch_shapes=[pltpu.VMEM((rows, width // 2), jnp.bfloat16)] * 2,
        compiler_params=pltpu.CompilerParams(vmem_limit_bytes=16 << 20),
        cost_estimate=pl.CostEstimate(flops=6 * rows * hidden * width, bytes_accessed=6 * hidden * width, transcendentals=0),
    )(place, *[hold(a) for a in own], *[hold(a) for a in across], *[hold(w) for w in weights])


def ring_body(tokens, expert_ids, gate_probs, w_gate, w_up, w_down):
    n = lax.axis_size("ep")
    rows = tokens.shape[0]
    order = list(range(0, n, 2)) + list(range(n - 1, 0, -2))
    ahead = [(order[i], order[(i + 1) % n]) for i in range(n)]
    back = [(b, a) for a, b in ahead]
    swap = functools.partial(lax.ppermute, axis_name="tp", perm=[(0, 1), (1, 0)])
    far = n // 2
    place = jnp.stack([lax.axis_index("tp"), lax.axis_index("ep")]).astype(jnp.int32)
    packed = pack(tokens, expert_ids, gate_probs, n)
    gate, up = turn_weights(after(place, packed), w_gate[0].T, w_up[0].T)

    came, across, value = {0: packed}, {}, {}

    def run(keys, wait_for=None):
        at = place if wait_for is None else after(place, wait_for)
        mine, theirs = run_expert(at, [came[k] for k in keys], [across[k] for k in keys], weights, n)
        done, theirs = theirs, swap(theirs)
        start = 0
        for k in keys:
            span = slice(start, start + came[k].shape[0])
            start = span.stop
            value[k] = mine[span].astype(jnp.float32) + theirs[span].astype(jnp.float32)
            mine, theirs = lax.optimization_barrier((mine, theirs))
        return done

    came[1] = lax.ppermute(packed, "ep", ahead)
    came[-1] = lax.ppermute(packed, "ep", back)
    across[0] = swap(packed)
    weights, done = [gate, up], up
    for k in range(2, far):
        came[k - 1], came[1 - k] = after(came[k - 1], done), after(came[1 - k], done)
        came[k] = lax.ppermute(came[k - 1], "ep", ahead)
        came[-k] = lax.ppermute(came[1 - k], "ep", back)
        across[k - 1], across[1 - k] = swap(came[k - 1]), swap(came[1 - k])
        if k == 2:
            weights += halve_weights(after(place, came[1]), w_down[0])
            done = weights[-1]
        else:
            done = run([k - 2, 2 - k])
    came[far - 1], came[1 - far] = after(came[far - 1], done), after(came[1 - far], done)
    came["low"] = lax.ppermute(came[far - 1][: rows // 2], "ep", ahead)
    came["high"] = lax.ppermute(came[1 - far][rows // 2 :], "ep", back)
    across[far - 1], across[1 - far] = swap(came[far - 1]), swap(came[1 - far])
    done = run([far - 1, 1 - far])
    came["low"], came["high"] = after((came["low"], came["high"]), done)
    across["low"], across["high"] = swap(came["low"]), swap(came["high"])
    run(["low", "high"])

    to_ahead = value["low"].astype(jnp.bfloat16)
    to_back = value["high"].astype(jnp.bfloat16)
    pad_low, pad_high = ((0, rows - rows // 2), (0, 0)), ((rows // 2, 0), (0, 0))
    for k in range(far - 1, -1, -1):
        behind = lax.ppermute(to_ahead, "ep", ahead)
        front = lax.ppermute(to_back, "ep", back)
        if k >= far - 2:
            done = run([far - 2, 2 - far] if k == far - 1 else [0], (to_ahead, to_back))
        behind, front = behind.astype(jnp.float32), front.astype(jnp.float32)
        if k == far - 1:
            behind, front = jnp.pad(behind, pad_low), jnp.pad(front, pad_high)
        if k:
            to_ahead = (value[-k] + behind).astype(jnp.bfloat16)
            to_back = (value[k] + front).astype(jnp.bfloat16)
        if k >= far - 2:
            to_ahead, to_back = after(to_ahead, done), after(to_back, done)
    return (value[0] + behind + front).astype(jnp.bfloat16)


def swiglu_expert(rows, gate_part, up_part, down_part):
    gated = jnp.dot(rows, gate_part, preferred_element_type=jnp.float32)
    lifted = jnp.dot(rows, up_part, preferred_element_type=jnp.float32)
    hidden = (jax.nn.silu(gated) * lifted).astype(jnp.bfloat16)
    return jnp.dot(hidden, down_part, preferred_element_type=jnp.float32)


def slot_table(expert_ids, n_experts):
    routed = expert_ids.reshape(-1)
    pair_count = routed.shape[0]
    onehot = (routed[:, None] == jnp.arange(n_experts, dtype=jnp.int32)[None, :]).astype(
        jnp.bfloat16
    )
    row_index = lax.broadcasted_iota(jnp.int32, (pair_count, pair_count), 0)
    col_index = lax.broadcasted_iota(jnp.int32, (pair_count, pair_count), 1)
    earlier = (row_index > col_index).astype(jnp.bfloat16)
    before = jnp.dot(earlier, onehot, preferred_element_type=jnp.float32)
    slots = jnp.sum(before * onehot.astype(jnp.float32), axis=1).astype(jnp.int32)
    return (routed, slots)


def slot_body(tokens, expert_ids, gate_probs, w_gate, w_up, w_down):
    n_experts = lax.axis_size("ep")
    tok_rows, top_count = expert_ids.shape
    capacity = 3 * tok_rows * top_count // (2 * n_experts)
    routed, slots = slot_table(expert_ids, n_experts)
    positions = routed * capacity + slots
    pair_token = jnp.repeat(jnp.arange(tok_rows, dtype=jnp.int32), top_count)
    buffer_rows = n_experts * capacity
    owners = jnp.full((buffer_rows,), tok_rows, jnp.int32).at[positions].set(pair_token)
    half_slots = capacity // 2
    whole_tokens = lax.all_gather(tokens, "tp", axis=1, tiled=True)
    width = whole_tokens.shape[1]
    gate_full, up_full = (
        lax.all_gather(w_gate, "tp", axis=2, tiled=True),
        lax.all_gather(w_up, "tp", axis=2, tiled=True),
    )
    down_full = lax.all_gather(w_down, "tp", axis=1, tiled=True)
    padded = jnp.concatenate([whole_tokens, jnp.zeros((1, width), whole_tokens.dtype)], 0)
    outgoing = padded[owners].reshape(n_experts, capacity, width)
    lane = lax.axis_index("tp")
    mine = lax.dynamic_slice_in_dim(outgoing, lane * half_slots, half_slots, 1)
    block = lax.all_to_all(mine, "ep", split_axis=0, concat_axis=0, tiled=True)
    sources, items, columns = block.shape
    result = swiglu_expert(
        block.reshape(sources * items, columns), gate_full[0], up_full[0], down_full[0]
    )
    result = result.astype(jnp.bfloat16).reshape(sources, items, columns)
    returned = lax.all_to_all(result, "ep", split_axis=0, concat_axis=0, tiled=True)
    received = returned.reshape(n_experts * half_slots, width)
    in_half = slots // half_slots == lane
    local_pos = routed * half_slots + slots % half_slots
    picked = received[local_pos].astype(jnp.float32).reshape(tok_rows, top_count, width)
    weighted = jnp.where(in_half.reshape(tok_rows, top_count), gate_probs, 0.0)
    partial_value = jnp.sum(weighted[:, :, None] * picked, axis=1)
    return lax.psum_scatter(partial_value, "tp", scatter_dimension=1, tiled=True).astype(
        jnp.bfloat16
    )


def solution(mesh):
    in_specs = (
        P(("groups", "ep"), "tp"),
        P(("groups", "ep"), None),
        P(("groups", "ep"), None),
        P("ep", None, "tp"),
        P("ep", None, "tp"),
        P("ep", "tp", None),
    )
    out_specs = P(("groups", "ep"), "tp")

    def body(tokens, expert_ids, *rest):
        n, top = lax.axis_size("ep"), expert_ids.shape[1]
        small = n <= 4 * top and n % 2 == 0 and n >= 6 and lax.axis_size("tp") == 2
        return (ring_body if small else slot_body)(tokens, expert_ids, *rest)

    return jax.shard_map(body, mesh=mesh, in_specs=in_specs, out_specs=out_specs, check_vma=False)
```

```python
import functools

import jax
import jax.numpy as jnp
from jax import lax
from jax.experimental import pallas as pl
from jax.experimental.pallas import tpu as pltpu
from jax.sharding import PartitionSpec as P

SPLITS = 3


def in_vmem(shape, dtype=jnp.bfloat16):
    return pltpu.MemorySpace.VMEM(shape, dtype)


def hold(x):
    return pltpu.with_memory_space_constraint(x, pltpu.VMEM)


def after(x, done):
    return lax.optimization_barrier((x, done))[0]


def pack_kernel(n_experts, tokens_in, ids_in, probs_in, packed, tokens, ids, probs, sems):
    copies = [
        pltpu.make_async_copy(src, dst, sems.at[i])
        for i, (src, dst) in enumerate(((ids_in, ids), (probs_in, probs), (tokens_in, tokens)))
    ]
    for copy in copies:
        copy.start()
    top, rows = ids.shape
    half = tokens.shape[1]
    copies[0].wait()
    copies[1].wait()
    expert = lax.broadcasted_iota(jnp.int32, (n_experts, rows), 0)
    rest = jnp.zeros((n_experts, rows), jnp.float32)
    for k in range(top):
        rest += jnp.where(ids[k : k + 1, :] == expert, probs[k : k + 1, :], 0.0)
    terms = []
    for _ in range(SPLITS):
        term = rest.astype(jnp.bfloat16).astype(jnp.float32)
        terms.append(term)
        rest = rest - term
    packed[:, half:] = jnp.concatenate(terms, axis=0).T.astype(jnp.bfloat16)
    copies[2].wait()
    packed[:, :half] = tokens[...]


def pack(tokens, expert_ids, gate_probs, n_experts):
    rows, half = tokens.shape
    args = (tokens, expert_ids.T, gate_probs.T)
    return pl.pallas_call(
        functools.partial(pack_kernel, n_experts),
        out_shape=in_vmem((rows, half + SPLITS * n_experts)),
        in_specs=[pl.BlockSpec(memory_space=pltpu.HBM)] * 3,
        out_specs=pl.BlockSpec(memory_space=pltpu.VMEM),
        scratch_shapes=[pltpu.VMEM(a.shape, a.dtype) for a in args] + [pltpu.SemaphoreType.DMA((3,))],
        compiler_params=pltpu.CompilerParams(vmem_limit_bytes=8 << 20),
    )(*[pltpu.with_memory_space_constraint(a, pltpu.HBM) for a in args])


def pieces(hidden):
    first = -(-hidden // 256) * 128
    return ((0, first), (first, hidden))


def turn_kernel(after_this, gate_in, up_in, gate, up, gate_buf, up_buf, sems):
    steps = []
    for i, (src, buf, out) in enumerate(((gate_in, gate_buf, gate), (up_in, up_buf, up))):
        for j, (start, stop) in enumerate(pieces(src.shape[0])):
            span = pl.ds(start, stop - start)
            steps.append((pltpu.make_async_copy(src.at[span], buf.at[span], sems.at[i, j]), buf, out, start, stop))
    for copy, *_ in steps:
        copy.start()
    for copy, buf, out, start, stop in steps:
        copy.wait()
        out[:, start:stop] = buf[start:stop, :].T


def turn_weights(after_this, *weights):
    hidden, width = weights[0].shape
    return pl.pallas_call(
        turn_kernel,
        out_shape=[in_vmem((width, hidden))] * 2,
        in_specs=[pl.BlockSpec(memory_space=pltpu.SMEM)] + [pl.BlockSpec(memory_space=pltpu.HBM)] * 2,
        out_specs=[pl.BlockSpec(memory_space=pltpu.VMEM)] * 2,
        scratch_shapes=[pltpu.VMEM((hidden, width), jnp.bfloat16)] * 2 + [pltpu.SemaphoreType.DMA((2, 2))],
        compiler_params=pltpu.CompilerParams(vmem_limit_bytes=32 << 20),
        cost_estimate=pl.CostEstimate(flops=0, bytes_accessed=8 * hidden * width, transcendentals=0),
    )(after_this, *[pltpu.with_memory_space_constraint(w, pltpu.HBM) for w in weights])


def halve_kernel(place, down_in, down_mine, down_theirs, down_buf, sems):
    lane = place[0]
    half = down_mine.shape[1]
    spans = [slice(start, stop) for start, stop in pieces(down_in.shape[0])]
    copies = [
        pltpu.make_async_copy(down_in.at[pl.ds(s.start, s.stop - s.start)], down_buf.at[pl.ds(s.start, s.stop - s.start)], sems.at[i])
        for i, s in enumerate(spans)
    ]
    for copy in copies:
        copy.start()
    for copy, s in zip(copies, spans):
        copy.wait()

        @pl.when(lane == 0)
        def _():
            down_mine[s, :] = down_buf[s, :half]
            down_theirs[s, :] = down_buf[s, half:]

        @pl.when(lane != 0)
        def _():
            down_mine[s, :] = down_buf[s, half:]
            down_theirs[s, :] = down_buf[s, :half]


def halve_weights(place, w_down):
    hidden, width = w_down.shape
    return pl.pallas_call(
        halve_kernel,
        out_shape=[in_vmem((hidden, width // 2))] * 2,
        in_specs=[pl.BlockSpec(memory_space=pltpu.SMEM), pl.BlockSpec(memory_space=pltpu.HBM)],
        out_specs=[pl.BlockSpec(memory_space=pltpu.VMEM)] * 2,
        scratch_shapes=[pltpu.VMEM((hidden, width), jnp.bfloat16), pltpu.SemaphoreType.DMA((2,))],
        compiler_params=pltpu.CompilerParams(vmem_limit_bytes=32 << 20),
        cost_estimate=pl.CostEstimate(flops=0, bytes_accessed=8 * hidden * width, transcendentals=0),
    )(place, pltpu.with_memory_space_constraint(w_down, pltpu.HBM))


def expert_kernel(n_blocks, n_experts, place, *refs):
    own, across = refs[:n_blocks], refs[n_blocks : 2 * n_blocks]
    w_gate, w_up, down_mine, down_theirs, mine, theirs, x_own, x_across = refs[2 * n_blocks :]
    lane, expert = place[0], place[1]
    half = mine.shape[1]
    spans, start = [], 0
    for a, b in zip(own, across):
        spans.append(slice(start, start + a.shape[0]))
        x_own[spans[-1], :] = a[:, :half]
        x_across[spans[-1], :] = b[:, :half]
        start += a.shape[0]
    here = pl.ds(pl.multiple_of(lane * half, 16), half)
    there = pl.ds(pl.multiple_of((1 - lane) * half, 16), half)

    def project(w):
        near = jnp.dot(x_own[...], w[here, :], preferred_element_type=jnp.float32)
        return near + jnp.dot(x_across[...], w[there, :], preferred_element_type=jnp.float32)

    gated = project(w_gate)
    lifted = project(w_up)
    hidden = (gated / (1.0 + jnp.exp(-gated)) * lifted).astype(jnp.bfloat16)
    weights = []
    for a in own:
        terms = a[:, half:].astype(jnp.float32)
        column = lax.broadcasted_iota(jnp.int32, terms.shape, 1)
        weights.append(jnp.sum(jnp.where(lax.rem(column, n_experts) == expert, terms, 0.0), axis=1, keepdims=True))
    for w, out in ((down_theirs, theirs), (down_mine, mine)):
        value = jnp.dot(hidden, w[...], preferred_element_type=jnp.float32)
        for span, weight in zip(spans, weights):
            out[span] = (value[span] * weight).astype(jnp.bfloat16)


def run_expert(place, own, across, weights, n_experts):
    width, hidden = weights[0].shape
    rows = sum(a.shape[0] for a in own)
    vmem = pl.BlockSpec(memory_space=pltpu.VMEM)
    return pl.pallas_call(
        functools.partial(expert_kernel, len(own), n_experts),
        out_shape=[in_vmem((rows, width // 2))] * 2,
        in_specs=[pl.BlockSpec(memory_space=pltpu.SMEM)] + [vmem] * (2 * len(own) + 4),
        out_specs=[vmem] * 2,
        scratch_shapes=[pltpu.VMEM((rows, width // 2), jnp.bfloat16)] * 2,
        compiler_params=pltpu.CompilerParams(vmem_limit_bytes=16 << 20),
        cost_estimate=pl.CostEstimate(flops=6 * rows * hidden * width, bytes_accessed=6 * hidden * width, transcendentals=0),
    )(place, *[hold(a) for a in own], *[hold(a) for a in across], *[hold(w) for w in weights])


def ring_body(tokens, expert_ids, gate_probs, w_gate, w_up, w_down):
    n = lax.axis_size("ep")
    rows = tokens.shape[0]
    order = list(range(0, n, 2)) + list(range(n - 1, 0, -2))
    ahead = [(order[i], order[(i + 1) % n]) for i in range(n)]
    back = [(b, a) for a, b in ahead]
    levels = n // 2
    middle = (levels // 2 - 1, levels // 2)
    opposite = [(i, i ^ 1 if i // 2 in middle else n - 1 - i) for i in range(n)]
    swap = functools.partial(lax.ppermute, axis_name="tp", perm=[(0, 1), (1, 0)])
    far = n // 2
    me = lax.axis_index("ep")
    level, side = me // 2, me % 2
    relays = (level == middle[0]) | (level == middle[1])
    relays_ahead = relays & ((level == middle[0]) == (side == 0))
    relays_back = relays & ~relays_ahead
    place = jnp.stack([lax.axis_index("tp"), me]).astype(jnp.int32)
    packed = pack(tokens, expert_ids, gate_probs, n)
    gate, up = turn_weights(after(place, packed), w_gate[0].T, w_up[0].T)

    came, across, value = {0: packed}, {}, {}

    def run(keys, wait_for=None):
        at = place if wait_for is None else after(place, wait_for)
        mine, theirs = run_expert(at, [came[k] for k in keys], [across[k] for k in keys], weights, n)
        done, theirs = theirs, swap(theirs)
        start = 0
        for k in keys:
            span = slice(start, start + came[k].shape[0])
            start = span.stop
            value[k] = mine[span].astype(jnp.float32) + theirs[span].astype(jnp.float32)
            mine, theirs = lax.optimization_barrier((mine, theirs))
        return done

    came[1] = lax.ppermute(packed, "ep", ahead)
    came[-1] = lax.ppermute(packed, "ep", back)
    across[0] = swap(packed)
    weights, done = [gate, up], up
    for k in range(2, far):
        came[k - 1], came[1 - k] = after(came[k - 1], done), after(came[1 - k], done)
        came[k] = lax.ppermute(came[k - 1], "ep", ahead)
        came[-k] = lax.ppermute(came[1 - k], "ep", back)
        across[k - 1], across[1 - k] = swap(came[k - 1]), swap(came[1 - k])
        if k == 2:
            passed = jnp.where(relays_ahead, came[-1], jnp.where(relays_back, came[1], packed))
            came[far] = lax.ppermute(passed, "ep", opposite)
            weights += halve_weights(after(place, came[1]), w_down[0])
            done = weights[-1]
        else:
            done = run([k - 1, 1 - k])
    came[far - 1], came[1 - far] = after(came[far - 1], done), after(came[1 - far], done)
    across[far - 1], across[1 - far] = swap(came[far - 1]), swap(came[1 - far])
    across[far] = swap(came[far])
    run([far - 1, 1 - far, far])
    returned = lax.ppermute(value[far].astype(jnp.bfloat16), "ep", opposite)

    to_ahead, to_back = value[1 - far].astype(jnp.bfloat16), value[far - 1].astype(jnp.bfloat16)
    for k in range(far - 1, 0, -1):
        behind = lax.ppermute(to_ahead, "ep", ahead)
        front = lax.ppermute(to_back, "ep", back)
        if k >= far - 2:
            done = run([1, -1] if k == far - 1 else [0], (to_ahead, to_back))
        if k > 1:
            to_ahead, to_back = value[1 - k] + behind.astype(jnp.float32), value[k - 1] + front.astype(jnp.float32)
            if k == 2:
                for_back = lax.optimization_barrier(returned).astype(jnp.float32)
                to_ahead += jnp.where(relays_ahead, returned.astype(jnp.float32), 0.0)
                to_back += jnp.where(relays_back, for_back, 0.0)
            to_ahead, to_back = after(to_ahead.astype(jnp.bfloat16), done), after(to_back.astype(jnp.bfloat16), done)
    total = value[0] + behind.astype(jnp.float32) + front.astype(jnp.float32)
    return (total + jnp.where(relays, 0.0, returned.astype(jnp.float32))).astype(jnp.bfloat16)


def swiglu_expert(rows, gate_part, up_part, down_part):
    gated = jnp.dot(rows, gate_part, preferred_element_type=jnp.float32)
    lifted = jnp.dot(rows, up_part, preferred_element_type=jnp.float32)
    hidden = (jax.nn.silu(gated) * lifted).astype(jnp.bfloat16)
    return jnp.dot(hidden, down_part, preferred_element_type=jnp.float32)


def slot_table(expert_ids, n_experts):
    routed = expert_ids.reshape(-1)
    pair_count = routed.shape[0]
    onehot = (routed[:, None] == jnp.arange(n_experts, dtype=jnp.int32)[None, :]).astype(
        jnp.bfloat16
    )
    row_index = lax.broadcasted_iota(jnp.int32, (pair_count, pair_count), 0)
    col_index = lax.broadcasted_iota(jnp.int32, (pair_count, pair_count), 1)
    earlier = (row_index > col_index).astype(jnp.bfloat16)
    before = jnp.dot(earlier, onehot, preferred_element_type=jnp.float32)
    slots = jnp.sum(before * onehot.astype(jnp.float32), axis=1).astype(jnp.int32)
    return (routed, slots)


def slot_body(tokens, expert_ids, gate_probs, w_gate, w_up, w_down):
    n_experts = lax.axis_size("ep")
    tok_rows, top_count = expert_ids.shape
    capacity = 3 * tok_rows * top_count // (2 * n_experts)
    routed, slots = slot_table(expert_ids, n_experts)
    positions = routed * capacity + slots
    pair_token = jnp.repeat(jnp.arange(tok_rows, dtype=jnp.int32), top_count)
    buffer_rows = n_experts * capacity
    owners = jnp.full((buffer_rows,), tok_rows, jnp.int32).at[positions].set(pair_token)
    half_slots = capacity // 2
    whole_tokens = lax.all_gather(tokens, "tp", axis=1, tiled=True)
    width = whole_tokens.shape[1]
    gate_full, up_full = (
        lax.all_gather(w_gate, "tp", axis=2, tiled=True),
        lax.all_gather(w_up, "tp", axis=2, tiled=True),
    )
    down_full = lax.all_gather(w_down, "tp", axis=1, tiled=True)
    padded = jnp.concatenate([whole_tokens, jnp.zeros((1, width), whole_tokens.dtype)], 0)
    outgoing = padded[owners].reshape(n_experts, capacity, width)
    lane = lax.axis_index("tp")
    mine = lax.dynamic_slice_in_dim(outgoing, lane * half_slots, half_slots, 1)
    block = lax.all_to_all(mine, "ep", split_axis=0, concat_axis=0, tiled=True)
    sources, items, columns = block.shape
    result = swiglu_expert(
        block.reshape(sources * items, columns), gate_full[0], up_full[0], down_full[0]
    )
    result = result.astype(jnp.bfloat16).reshape(sources, items, columns)
    returned = lax.all_to_all(result, "ep", split_axis=0, concat_axis=0, tiled=True)
    received = returned.reshape(n_experts * half_slots, width)
    in_half = slots // half_slots == lane
    local_pos = routed * half_slots + slots % half_slots
    picked = received[local_pos].astype(jnp.float32).reshape(tok_rows, top_count, width)
    weighted = jnp.where(in_half.reshape(tok_rows, top_count), gate_probs, 0.0)
    partial_value = jnp.sum(weighted[:, :, None] * picked, axis=1)
    return lax.psum_scatter(partial_value, "tp", scatter_dimension=1, tiled=True).astype(
        jnp.bfloat16
    )


def solution(mesh):
    in_specs = (
        P(("groups", "ep"), "tp"),
        P(("groups", "ep"), None),
        P(("groups", "ep"), None),
        P("ep", None, "tp"),
        P("ep", None, "tp"),
        P("ep", "tp", None),
    )
    out_specs = P(("groups", "ep"), "tp")

    def body(tokens, expert_ids, *rest):
        n, top = lax.axis_size("ep"), expert_ids.shape[1]
        small = n <= 4 * top and n % 4 == 0 and n >= 8 and lax.axis_size("tp") == 2
        return (ring_body if small else slot_body)(tokens, expert_ids, *rest)

    return jax.shard_map(body, mesh=mesh, in_specs=in_specs, out_specs=out_specs, check_vma=False)
```

```python
import functools

import jax
import jax.numpy as jnp
from jax import lax
from jax.experimental import pallas as pl
from jax.experimental.pallas import tpu as pltpu
from jax.sharding import PartitionSpec as P

SPLITS = 3


def in_vmem(shape, dtype=jnp.bfloat16):
    return pltpu.MemorySpace.VMEM(shape, dtype)


def hold(x):
    return pltpu.with_memory_space_constraint(x, pltpu.VMEM)


def after(x, done):
    return lax.optimization_barrier((x, done))[0]


def pack_kernel(n_experts, tokens_in, ids_in, probs_in, packed, tokens, ids, probs, sems):
    copies = [
        pltpu.make_async_copy(src, dst, sems.at[i])
        for i, (src, dst) in enumerate(((ids_in, ids), (probs_in, probs), (tokens_in, tokens)))
    ]
    for copy in copies:
        copy.start()
    top, rows = ids.shape
    half = tokens.shape[1]
    copies[0].wait()
    copies[1].wait()
    expert = lax.broadcasted_iota(jnp.int32, (n_experts, rows), 0)
    rest = jnp.zeros((n_experts, rows), jnp.float32)
    for k in range(top):
        rest += jnp.where(ids[k : k + 1, :] == expert, probs[k : k + 1, :], 0.0)
    terms = []
    for _ in range(SPLITS):
        term = rest.astype(jnp.bfloat16).astype(jnp.float32)
        terms.append(term)
        rest = rest - term
    packed[:, half:] = jnp.concatenate(terms, axis=0).T.astype(jnp.bfloat16)
    copies[2].wait()
    packed[:, :half] = tokens[...]


def pack(tokens, expert_ids, gate_probs, n_experts):
    rows, half = tokens.shape
    args = (tokens, expert_ids.T, gate_probs.T)
    return pl.pallas_call(
        functools.partial(pack_kernel, n_experts),
        out_shape=in_vmem((rows, half + SPLITS * n_experts)),
        in_specs=[pl.BlockSpec(memory_space=pltpu.HBM)] * 3,
        out_specs=pl.BlockSpec(memory_space=pltpu.VMEM),
        scratch_shapes=[pltpu.VMEM(a.shape, a.dtype) for a in args] + [pltpu.SemaphoreType.DMA((3,))],
        compiler_params=pltpu.CompilerParams(vmem_limit_bytes=8 << 20),
    )(*[pltpu.with_memory_space_constraint(a, pltpu.HBM) for a in args])


def pieces(hidden):
    first = -(-hidden // 256) * 128
    return ((0, first), (first, hidden))


def turn_kernel(after_this, gate_in, up_in, gate, up, gate_buf, up_buf, sems):
    steps = []
    for i, (src, buf, out) in enumerate(((gate_in, gate_buf, gate), (up_in, up_buf, up))):
        for j, (start, stop) in enumerate(pieces(src.shape[0])):
            span = pl.ds(start, stop - start)
            steps.append((pltpu.make_async_copy(src.at[span], buf.at[span], sems.at[i, j]), buf, out, start, stop))
    for copy, *_ in steps:
        copy.start()
    for copy, buf, out, start, stop in steps:
        copy.wait()
        out[:, start:stop] = buf[start:stop, :].T


def turn_weights(after_this, *weights):
    hidden, width = weights[0].shape
    return pl.pallas_call(
        turn_kernel,
        out_shape=[in_vmem((width, hidden))] * 2,
        in_specs=[pl.BlockSpec(memory_space=pltpu.SMEM)] + [pl.BlockSpec(memory_space=pltpu.HBM)] * 2,
        out_specs=[pl.BlockSpec(memory_space=pltpu.VMEM)] * 2,
        scratch_shapes=[pltpu.VMEM((hidden, width), jnp.bfloat16)] * 2 + [pltpu.SemaphoreType.DMA((2, 2))],
        compiler_params=pltpu.CompilerParams(vmem_limit_bytes=32 << 20),
        cost_estimate=pl.CostEstimate(flops=0, bytes_accessed=8 * hidden * width, transcendentals=0),
    )(after_this, *[pltpu.with_memory_space_constraint(w, pltpu.HBM) for w in weights])


def halve_kernel(place, down_in, down_mine, down_theirs, down_buf, sems):
    lane = place[0]
    half = down_mine.shape[1]
    spans = [slice(start, stop) for start, stop in pieces(down_in.shape[0])]
    copies = [
        pltpu.make_async_copy(down_in.at[pl.ds(s.start, s.stop - s.start)], down_buf.at[pl.ds(s.start, s.stop - s.start)], sems.at[i])
        for i, s in enumerate(spans)
    ]
    for copy in copies:
        copy.start()
    for copy, s in zip(copies, spans):
        copy.wait()

        @pl.when(lane == 0)
        def _():
            down_mine[s, :] = down_buf[s, :half]
            down_theirs[s, :] = down_buf[s, half:]

        @pl.when(lane != 0)
        def _():
            down_mine[s, :] = down_buf[s, half:]
            down_theirs[s, :] = down_buf[s, :half]


def halve_weights(place, w_down):
    hidden, width = w_down.shape
    return pl.pallas_call(
        halve_kernel,
        out_shape=[in_vmem((hidden, width // 2))] * 2,
        in_specs=[pl.BlockSpec(memory_space=pltpu.SMEM), pl.BlockSpec(memory_space=pltpu.HBM)],
        out_specs=[pl.BlockSpec(memory_space=pltpu.VMEM)] * 2,
        scratch_shapes=[pltpu.VMEM((hidden, width), jnp.bfloat16), pltpu.SemaphoreType.DMA((2,))],
        compiler_params=pltpu.CompilerParams(vmem_limit_bytes=32 << 20),
        cost_estimate=pl.CostEstimate(flops=0, bytes_accessed=8 * hidden * width, transcendentals=0),
    )(place, pltpu.with_memory_space_constraint(w_down, pltpu.HBM))


def gather_rows(blocks, x, width):
    start = 0
    for block in blocks:
        x[start : start + block.shape[0], :] = block[:, :width]
        start += block.shape[0]
    if start < x.shape[0]:
        x[start:, :] = jnp.zeros((x.shape[0] - start, width), x.dtype)


def project(x, lane, w):
    half = x.shape[1]
    return jnp.dot(x[...], w[pl.ds(pl.multiple_of(lane * half, 16), half), :], preferred_element_type=jnp.float32)


def activate(gated, lifted):
    return (gated / (1.0 + jnp.exp(-gated)) * lifted).astype(jnp.bfloat16)


def gate_weights(blocks, half, expert, n_experts):
    weights = []
    for block in blocks:
        terms = block[:, half:].astype(jnp.float32)
        column = lax.broadcasted_iota(jnp.int32, terms.shape, 1)
        weights.append(jnp.sum(jnp.where(lax.rem(column, n_experts) == expert, terms, 0.0), axis=1, keepdims=True))
    return weights


def lower(hidden, w, weights, out):
    value = jnp.dot(hidden, w[...], preferred_element_type=jnp.float32)
    start = 0
    for weight in weights:
        span = slice(start, start + weight.shape[0])
        start = span.stop
        out[span] = (value[span] * weight).astype(jnp.bfloat16)


def expert_kernel(n_blocks, n_experts, place, *refs):
    own, across = refs[:n_blocks], refs[n_blocks : 2 * n_blocks]
    w_gate, w_up, down_mine, down_theirs, mine, theirs, x_own, x_across = refs[2 * n_blocks :]
    lane, expert = place[0], place[1]
    half = mine.shape[1]
    gather_rows(own, x_own, half)
    gather_rows(across, x_across, half)
    gated = project(x_own, lane, w_gate) + project(x_across, 1 - lane, w_gate)
    lifted = project(x_own, lane, w_up) + project(x_across, 1 - lane, w_up)
    hidden = activate(gated, lifted)
    weights = gate_weights(own, half, expert, n_experts)
    lower(hidden, down_theirs, weights, theirs)
    lower(hidden, down_mine, weights, mine)


def first_kernel(n_blocks, place, *refs):
    own = refs[:n_blocks]
    w_gate, w_up, gated, lifted, x = refs[n_blocks:]
    gather_rows(own, x, x.shape[1])
    gated[...] = project(x, place[0], w_gate)
    lifted[...] = project(x, place[0], w_up)


def second_kernel(n_blocks, n_experts, place, *refs):
    own, across = refs[:n_blocks], refs[n_blocks : 2 * n_blocks]
    gated, lifted, w_gate, w_up, down_theirs, hidden, theirs, x = refs[2 * n_blocks :]
    half = x.shape[1]
    gather_rows(across, x, half)
    there = 1 - place[0]
    hidden[...] = activate(gated[...] + project(x, there, w_gate), lifted[...] + project(x, there, w_up))
    lower(hidden[...], down_theirs, gate_weights(own, half, place[1], n_experts), theirs)


def third_kernel(n_blocks, n_experts, place, *refs):
    own = refs[:n_blocks]
    hidden, down_mine, mine = refs[n_blocks:]
    lower(hidden[...], down_mine, gate_weights(own, mine.shape[1], place[1], n_experts), mine)


def call(kernel, place, args, out_shape, scratch_shapes, flops):
    vmem = pl.BlockSpec(memory_space=pltpu.VMEM)
    return pl.pallas_call(
        kernel,
        out_shape=out_shape,
        in_specs=[pl.BlockSpec(memory_space=pltpu.SMEM)] + [vmem] * len(args),
        out_specs=[vmem] * len(out_shape),
        scratch_shapes=scratch_shapes,
        compiler_params=pltpu.CompilerParams(vmem_limit_bytes=16 << 20),
        cost_estimate=pl.CostEstimate(flops=flops, bytes_accessed=flops // 128, transcendentals=0),
    )(place, *[hold(a) for a in args])


def padded(rows):
    return -(-rows // 128) * 128


def run_expert(place, own, across, weights, n_experts):
    width, hidden = weights[0].shape
    half = width // 2
    rows = sum(a.shape[0] for a in own)
    return call(
        functools.partial(expert_kernel, len(own), n_experts),
        place,
        (*own, *across, *weights),
        [in_vmem((rows, half))] * 2,
        [pltpu.VMEM((padded(rows), half), jnp.bfloat16)] * 2,
        6 * padded(rows) * hidden * width,
    )


def run_expert_in_stages(place, own, swap, weights, n_experts):
    gate, up, down_mine, down_theirs = weights
    width, hidden = gate.shape
    half = width // 2
    rows, n_blocks = sum(a.shape[0] for a in own), len(own)
    across = [swap(a) for a in own]
    products = [in_vmem((padded(rows), hidden), jnp.float32)] * 2
    x = [pltpu.VMEM((padded(rows), half), jnp.bfloat16)]
    flops = 2 * padded(rows) * hidden * width
    gated, lifted = call(functools.partial(first_kernel, n_blocks), place, (*own, gate, up), products, x, flops)
    units, theirs = call(
        functools.partial(second_kernel, n_blocks, n_experts),
        place,
        (*own, *across, gated, lifted, gate, up, down_theirs),
        [in_vmem((padded(rows), hidden)), in_vmem((rows, half))],
        x,
        flops + flops // 2,
    )
    theirs = swap(theirs)
    (mine,) = call(
        functools.partial(third_kernel, n_blocks, n_experts),
        place,
        (*own, units, down_mine),
        [in_vmem((rows, half))],
        [],
        flops // 2,
    )
    return mine, theirs


def ring_body(tokens, expert_ids, gate_probs, w_gate, w_up, w_down):
    n = lax.axis_size("ep")
    rows = tokens.shape[0]
    order = list(range(0, n, 2)) + list(range(n - 1, 0, -2))
    ahead = [(order[i], order[(i + 1) % n]) for i in range(n)]
    back = [(b, a) for a, b in ahead]
    swap = functools.partial(lax.ppermute, axis_name="tp", perm=[(0, 1), (1, 0)])
    far = n // 2
    place = jnp.stack([lax.axis_index("tp"), lax.axis_index("ep")]).astype(jnp.int32)
    packed = pack(tokens, expert_ids, gate_probs, n)
    gate, up = turn_weights(after(place, packed), w_gate[0].T, w_up[0].T)

    came, across, value = {0: packed}, {}, {}

    def run(keys, wait_for=None):
        at = place if wait_for is None else after(place, wait_for)
        mine, theirs = run_expert(at, [came[k] for k in keys], [across[k] for k in keys], weights, n)
        keep(keys, mine, swap(theirs))
        return theirs

    def keep(keys, mine, theirs):
        start = 0
        for k in keys:
            span = slice(start, start + came[k].shape[0])
            start = span.stop
            value[k] = mine[span].astype(jnp.float32) + theirs[span].astype(jnp.float32)
            mine, theirs = lax.optimization_barrier((mine, theirs))

    came[1] = lax.ppermute(packed, "ep", ahead)
    came[-1] = lax.ppermute(packed, "ep", back)
    across[0] = swap(packed)
    weights, done = [gate, up], up
    for k in range(2, far):
        came[k - 1], came[1 - k] = after(came[k - 1], done), after(came[1 - k], done)
        came[k] = lax.ppermute(came[k - 1], "ep", ahead)
        came[-k] = lax.ppermute(came[1 - k], "ep", back)
        across[k - 1], across[1 - k] = swap(came[k - 1]), swap(came[1 - k])
        if k == 2:
            weights += halve_weights(after(place, came[1]), w_down[0])
            done = weights[-1]
        else:
            done = run([k - 2, 2 - k], across[0] if k == 3 else None)
    came[far - 1], came[1 - far] = after(came[far - 1], done), after(came[1 - far], done)
    came["low"] = lax.ppermute(came[far - 1][: rows // 2], "ep", ahead)
    came["high"] = lax.ppermute(came[1 - far][rows // 2 :], "ep", back)
    across[far - 1], across[1 - far] = swap(came[far - 1]), swap(came[1 - far])
    done = run([far - 1, 1 - far], (across[far - 2], across[2 - far]))
    came["low"], came["high"] = after((came["low"], came["high"]), done)
    far_keys = ["low", "high"]
    keep(far_keys, *run_expert_in_stages(place, [came[k] for k in far_keys], swap, weights, n))

    to_ahead = value["low"].astype(jnp.bfloat16)
    to_back = value["high"].astype(jnp.bfloat16)
    pad_low, pad_high = ((0, rows - rows // 2), (0, 0)), ((rows // 2, 0), (0, 0))
    for k in range(far - 1, -1, -1):
        behind = lax.ppermute(to_ahead, "ep", ahead)
        front = lax.ppermute(to_back, "ep", back)
        if k >= far - 2:
            done = run([far - 2, 2 - far] if k == far - 1 else [0], (to_ahead, to_back))
        behind, front = behind.astype(jnp.float32), front.astype(jnp.float32)
        if k == far - 1:
            behind, front = jnp.pad(behind, pad_low), jnp.pad(front, pad_high)
        if k:
            to_ahead = (value[-k] + behind).astype(jnp.bfloat16)
            to_back = (value[k] + front).astype(jnp.bfloat16)
        if k >= far - 2:
            to_ahead, to_back = after(to_ahead, done), after(to_back, done)
    return (value[0] + behind + front).astype(jnp.bfloat16)


def swiglu_expert(rows, gate_part, up_part, down_part):
    gated = jnp.dot(rows, gate_part, preferred_element_type=jnp.float32)
    lifted = jnp.dot(rows, up_part, preferred_element_type=jnp.float32)
    hidden = (jax.nn.silu(gated) * lifted).astype(jnp.bfloat16)
    return jnp.dot(hidden, down_part, preferred_element_type=jnp.float32)


def slot_table(expert_ids, n_experts):
    routed = expert_ids.reshape(-1)
    pair_count = routed.shape[0]
    onehot = (routed[:, None] == jnp.arange(n_experts, dtype=jnp.int32)[None, :]).astype(
        jnp.bfloat16
    )
    row_index = lax.broadcasted_iota(jnp.int32, (pair_count, pair_count), 0)
    col_index = lax.broadcasted_iota(jnp.int32, (pair_count, pair_count), 1)
    earlier = (row_index > col_index).astype(jnp.bfloat16)
    before = jnp.dot(earlier, onehot, preferred_element_type=jnp.float32)
    slots = jnp.sum(before * onehot.astype(jnp.float32), axis=1).astype(jnp.int32)
    return (routed, slots)


def slot_body(tokens, expert_ids, gate_probs, w_gate, w_up, w_down):
    n_experts = lax.axis_size("ep")
    tok_rows, top_count = expert_ids.shape
    capacity = 3 * tok_rows * top_count // (2 * n_experts)
    routed, slots = slot_table(expert_ids, n_experts)
    positions = routed * capacity + slots
    pair_token = jnp.repeat(jnp.arange(tok_rows, dtype=jnp.int32), top_count)
    buffer_rows = n_experts * capacity
    owners = jnp.full((buffer_rows,), tok_rows, jnp.int32).at[positions].set(pair_token)
    half_slots = capacity // 2
    whole_tokens = lax.all_gather(tokens, "tp", axis=1, tiled=True)
    width = whole_tokens.shape[1]
    gate_full, up_full = (
        lax.all_gather(w_gate, "tp", axis=2, tiled=True),
        lax.all_gather(w_up, "tp", axis=2, tiled=True),
    )
    down_full = lax.all_gather(w_down, "tp", axis=1, tiled=True)
    padded = jnp.concatenate([whole_tokens, jnp.zeros((1, width), whole_tokens.dtype)], 0)
    outgoing = padded[owners].reshape(n_experts, capacity, width)
    lane = lax.axis_index("tp")
    mine = lax.dynamic_slice_in_dim(outgoing, lane * half_slots, half_slots, 1)
    block = lax.all_to_all(mine, "ep", split_axis=0, concat_axis=0, tiled=True)
    sources, items, columns = block.shape
    result = swiglu_expert(
        block.reshape(sources * items, columns), gate_full[0], up_full[0], down_full[0]
    )
    result = result.astype(jnp.bfloat16).reshape(sources, items, columns)
    returned = lax.all_to_all(result, "ep", split_axis=0, concat_axis=0, tiled=True)
    received = returned.reshape(n_experts * half_slots, width)
    in_half = slots // half_slots == lane
    local_pos = routed * half_slots + slots % half_slots
    picked = received[local_pos].astype(jnp.float32).reshape(tok_rows, top_count, width)
    weighted = jnp.where(in_half.reshape(tok_rows, top_count), gate_probs, 0.0)
    partial_value = jnp.sum(weighted[:, :, None] * picked, axis=1)
    return lax.psum_scatter(partial_value, "tp", scatter_dimension=1, tiled=True).astype(
        jnp.bfloat16
    )


def solution(mesh):
    in_specs = (
        P(("groups", "ep"), "tp"),
        P(("groups", "ep"), None),
        P(("groups", "ep"), None),
        P("ep", None, "tp"),
        P("ep", None, "tp"),
        P("ep", "tp", None),
    )
    out_specs = P(("groups", "ep"), "tp")

    def body(tokens, expert_ids, *rest):
        n, top = lax.axis_size("ep"), expert_ids.shape[1]
        small = n <= 4 * top and n % 2 == 0 and n >= 6 and lax.axis_size("tp") == 2
        return (ring_body if small else slot_body)(tokens, expert_ids, *rest)

    return jax.shard_map(body, mesh=mesh, in_specs=in_specs, out_specs=out_specs, check_vma=False)
```

```python
import functools

import jax
import jax.numpy as jnp
from jax import lax
from jax.experimental import pallas as pl
from jax.experimental.pallas import tpu as pltpu
from jax.sharding import PartitionSpec as P

SPLITS = 3


def in_vmem(shape, dtype=jnp.bfloat16):
    return pltpu.MemorySpace.VMEM(shape, dtype)


def hold(x):
    return pltpu.with_memory_space_constraint(x, pltpu.VMEM)


def after(x, done):
    return lax.optimization_barrier((x, done))[0]


def pack_kernel(n_experts, tokens_in, ids_in, probs_in, packed, tokens, ids, probs, sems):
    copies = [
        pltpu.make_async_copy(src, dst, sems.at[i])
        for i, (src, dst) in enumerate(((ids_in, ids), (probs_in, probs), (tokens_in, tokens)))
    ]
    for copy in copies:
        copy.start()
    top, rows = ids.shape
    half = tokens.shape[1]
    copies[0].wait()
    copies[1].wait()
    expert = lax.broadcasted_iota(jnp.int32, (n_experts, rows), 0)
    rest = jnp.zeros((n_experts, rows), jnp.float32)
    for k in range(top):
        rest += jnp.where(ids[k : k + 1, :] == expert, probs[k : k + 1, :], 0.0)
    terms = []
    for _ in range(SPLITS):
        term = rest.astype(jnp.bfloat16).astype(jnp.float32)
        terms.append(term)
        rest = rest - term
    packed[:, half:] = jnp.concatenate(terms, axis=0).T.astype(jnp.bfloat16)
    copies[2].wait()
    packed[:, :half] = tokens[...]


def pack(tokens, expert_ids, gate_probs, n_experts):
    rows, half = tokens.shape
    args = (tokens, expert_ids.T, gate_probs.T)
    return pl.pallas_call(
        functools.partial(pack_kernel, n_experts),
        out_shape=in_vmem((rows, half + SPLITS * n_experts)),
        in_specs=[pl.BlockSpec(memory_space=pltpu.HBM)] * 3,
        out_specs=pl.BlockSpec(memory_space=pltpu.VMEM),
        scratch_shapes=[pltpu.VMEM(a.shape, a.dtype) for a in args] + [pltpu.SemaphoreType.DMA((3,))],
        compiler_params=pltpu.CompilerParams(vmem_limit_bytes=8 << 20),
    )(*[pltpu.with_memory_space_constraint(a, pltpu.HBM) for a in args])


def pieces(hidden):
    first = -(-hidden // 256) * 128
    return ((0, first), (first, hidden))


def turn_kernel(after_this, gate_in, up_in, gate, up, gate_buf, up_buf, sems):
    steps = []
    for i, (src, buf, out) in enumerate(((gate_in, gate_buf, gate), (up_in, up_buf, up))):
        for j, (start, stop) in enumerate(pieces(src.shape[0])):
            span = pl.ds(start, stop - start)
            steps.append((pltpu.make_async_copy(src.at[span], buf.at[span], sems.at[i, j]), buf, out, start, stop))
    for copy, *_ in steps:
        copy.start()
    for copy, buf, out, start, stop in steps:
        copy.wait()
        out[:, start:stop] = buf[start:stop, :].T


def turn_weights(after_this, *weights):
    hidden, width = weights[0].shape
    return pl.pallas_call(
        turn_kernel,
        out_shape=[in_vmem((width, hidden))] * 2,
        in_specs=[pl.BlockSpec(memory_space=pltpu.SMEM)] + [pl.BlockSpec(memory_space=pltpu.HBM)] * 2,
        out_specs=[pl.BlockSpec(memory_space=pltpu.VMEM)] * 2,
        scratch_shapes=[pltpu.VMEM((hidden, width), jnp.bfloat16)] * 2 + [pltpu.SemaphoreType.DMA((2, 2))],
        compiler_params=pltpu.CompilerParams(vmem_limit_bytes=32 << 20),
        cost_estimate=pl.CostEstimate(flops=0, bytes_accessed=8 * hidden * width, transcendentals=0),
    )(after_this, *[pltpu.with_memory_space_constraint(w, pltpu.HBM) for w in weights])


def halve_kernel(place, down_in, down_mine, down_theirs, down_buf, sems):
    lane = place[0]
    half = down_mine.shape[1]
    spans = [slice(start, stop) for start, stop in pieces(down_in.shape[0])]
    copies = [
        pltpu.make_async_copy(down_in.at[pl.ds(s.start, s.stop - s.start)], down_buf.at[pl.ds(s.start, s.stop - s.start)], sems.at[i])
        for i, s in enumerate(spans)
    ]
    for copy in copies:
        copy.start()
    for copy, s in zip(copies, spans):
        copy.wait()

        @pl.when(lane == 0)
        def _():
            down_mine[s, :] = down_buf[s, :half]
            down_theirs[s, :] = down_buf[s, half:]

        @pl.when(lane != 0)
        def _():
            down_mine[s, :] = down_buf[s, half:]
            down_theirs[s, :] = down_buf[s, :half]


def halve_weights(place, w_down):
    hidden, width = w_down.shape
    return pl.pallas_call(
        halve_kernel,
        out_shape=[in_vmem((hidden, width // 2))] * 2,
        in_specs=[pl.BlockSpec(memory_space=pltpu.SMEM), pl.BlockSpec(memory_space=pltpu.HBM)],
        out_specs=[pl.BlockSpec(memory_space=pltpu.VMEM)] * 2,
        scratch_shapes=[pltpu.VMEM((hidden, width), jnp.bfloat16), pltpu.SemaphoreType.DMA((2,))],
        compiler_params=pltpu.CompilerParams(vmem_limit_bytes=32 << 20),
        cost_estimate=pl.CostEstimate(flops=0, bytes_accessed=8 * hidden * width, transcendentals=0),
    )(place, pltpu.with_memory_space_constraint(w_down, pltpu.HBM))


def gather_rows(blocks, x, width):
    start = 0
    for block in blocks:
        x[start : start + block.shape[0], :] = block[:, :width]
        start += block.shape[0]
    if start < x.shape[0]:
        x[start:, :] = jnp.zeros((x.shape[0] - start, width), x.dtype)


def project(x, lane, w):
    half = x.shape[1]
    return jnp.dot(x[...], w[pl.ds(pl.multiple_of(lane * half, 16), half), :], preferred_element_type=jnp.float32)


def activate(gated, lifted):
    return (gated / (1.0 + jnp.exp(-gated)) * lifted).astype(jnp.bfloat16)


def gate_weights(blocks, half, expert, n_experts):
    weights = []
    for block in blocks:
        terms = block[:, half:].astype(jnp.float32)
        column = lax.broadcasted_iota(jnp.int32, terms.shape, 1)
        weights.append(jnp.sum(jnp.where(lax.rem(column, n_experts) == expert, terms, 0.0), axis=1, keepdims=True))
    return weights


def lower(hidden, w, weights, *outs):
    value = jnp.dot(hidden, w[...], preferred_element_type=jnp.float32)
    start, rows = 0, outs[0].shape[0]
    for weight in weights:
        stop = start + weight.shape[0]
        out, at = outs[start // rows], start % rows
        out[at : at + weight.shape[0]] = (value[start:stop] * weight).astype(jnp.bfloat16)
        start = stop


def expert_kernel(n_blocks, n_experts, place, *refs):
    own, across = refs[:n_blocks], refs[n_blocks : 2 * n_blocks]
    w_gate, w_up, down_mine, down_theirs, *outs, x_own, x_across = refs[2 * n_blocks :]
    lane, expert = place[0], place[1]
    half = x_own.shape[1]
    gather_rows(own, x_own, half)
    gather_rows(across, x_across, half)
    gated = project(x_own, lane, w_gate) + project(x_across, 1 - lane, w_gate)
    lifted = project(x_own, lane, w_up) + project(x_across, 1 - lane, w_up)
    hidden = activate(gated, lifted)
    weights = gate_weights(own, half, expert, n_experts)
    mine, theirs = outs[: len(outs) // 2], outs[len(outs) // 2 :]
    lower(hidden, down_theirs, weights, *theirs)
    lower(hidden, down_mine, weights, *mine)


def first_kernel(n_blocks, place, *refs):
    own = refs[:n_blocks]
    w_gate, w_up, gated, lifted, x = refs[n_blocks:]
    gather_rows(own, x, x.shape[1])
    gated[...] = project(x, place[0], w_gate)
    lifted[...] = project(x, place[0], w_up)


def second_kernel(n_blocks, n_experts, place, *refs):
    own, across = refs[:n_blocks], refs[n_blocks : 2 * n_blocks]
    gated, lifted, w_gate, w_up, down_theirs, hidden, theirs, x = refs[2 * n_blocks :]
    half = x.shape[1]
    gather_rows(across, x, half)
    there = 1 - place[0]
    hidden[...] = activate(gated[...] + project(x, there, w_gate), lifted[...] + project(x, there, w_up))
    lower(hidden[...], down_theirs, gate_weights(own, half, place[1], n_experts), theirs)


def third_kernel(n_blocks, n_experts, place, *refs):
    own = refs[:n_blocks]
    hidden, down_mine, mine = refs[n_blocks:]
    lower(hidden[...], down_mine, gate_weights(own, mine.shape[1], place[1], n_experts), mine)


def call(kernel, place, args, out_shape, scratch_shapes, flops):
    vmem = pl.BlockSpec(memory_space=pltpu.VMEM)
    return pl.pallas_call(
        kernel,
        out_shape=out_shape,
        in_specs=[pl.BlockSpec(memory_space=pltpu.SMEM)] + [vmem] * len(args),
        out_specs=[vmem] * len(out_shape),
        scratch_shapes=scratch_shapes,
        compiler_params=pltpu.CompilerParams(vmem_limit_bytes=16 << 20),
        cost_estimate=pl.CostEstimate(flops=flops, bytes_accessed=flops // 128, transcendentals=0),
    )(place, *[hold(a) for a in args])


def padded(rows):
    return -(-rows // 128) * 128


def run_expert(place, own, across, weights, n_experts):
    width, hidden = weights[0].shape
    half = width // 2
    rows, pairs = sum(a.shape[0] for a in own), max(1, len(own) // 2)
    outs = call(
        functools.partial(expert_kernel, len(own), n_experts),
        place,
        (*own, *across, *weights),
        [in_vmem((rows // pairs, half))] * (2 * pairs),
        [pltpu.VMEM((padded(rows), half), jnp.bfloat16)] * 2,
        6 * padded(rows) * hidden * width,
    )
    return outs[:pairs], outs[pairs:]


def run_expert_in_stages(place, own, swap, weights, n_experts):
    gate, up, down_mine, down_theirs = weights
    width, hidden = gate.shape
    half = width // 2
    rows, n_blocks = sum(a.shape[0] for a in own), len(own)
    across = [swap(a) for a in own]
    products = [in_vmem((padded(rows), hidden), jnp.float32)] * 2
    x = [pltpu.VMEM((padded(rows), half), jnp.bfloat16)]
    flops = 2 * padded(rows) * hidden * width
    gated, lifted = call(functools.partial(first_kernel, n_blocks), place, (*own, gate, up), products, x, flops)
    units, theirs = call(
        functools.partial(second_kernel, n_blocks, n_experts),
        place,
        (*own, *across, gated, lifted, gate, up, down_theirs),
        [in_vmem((padded(rows), hidden)), in_vmem((rows, half))],
        x,
        flops + flops // 2,
    )
    theirs = swap(theirs)
    (mine,) = call(
        functools.partial(third_kernel, n_blocks, n_experts),
        place,
        (*own, units, down_mine),
        [in_vmem((rows, half))],
        [],
        flops // 2,
    )
    return mine, theirs


def ring_body(tokens, expert_ids, gate_probs, w_gate, w_up, w_down):
    n = lax.axis_size("ep")
    rows = tokens.shape[0]
    order = list(range(0, n, 2)) + list(range(n - 1, 0, -2))
    ahead = [(order[i], order[(i + 1) % n]) for i in range(n)]
    back = [(b, a) for a, b in ahead]
    swap = functools.partial(lax.ppermute, axis_name="tp", perm=[(0, 1), (1, 0)])
    far = n // 2
    place = jnp.stack([lax.axis_index("tp"), lax.axis_index("ep")]).astype(jnp.int32)
    packed = pack(tokens, expert_ids, gate_probs, n)
    gate, up = turn_weights(after(place, packed), w_gate[0].T, w_up[0].T)

    came, across, value = {0: packed}, {}, {}

    def run(keys, wait_for=None):
        at = place if wait_for is None else after(place, wait_for)
        mine, theirs = run_expert(at, [came[k] for k in keys], [across[k] for k in keys], weights, n)
        for i, pair in enumerate(zip(mine, theirs)):
            keep(keys[2 * i : 2 * i + 2], pair[0], swap(pair[1]))
        return theirs[0]

    def keep(keys, mine, theirs):
        pairs = ((mine, theirs), lax.optimization_barrier((mine, theirs)))
        start = 0
        for i, k in enumerate(keys):
            mine, theirs = pairs[i % 2]
            span = slice(start, start + came[k].shape[0])
            start = span.stop
            value[k] = mine[span].astype(jnp.float32) + theirs[span].astype(jnp.float32)

    came[1] = lax.ppermute(packed, "ep", ahead)
    came[-1] = lax.ppermute(packed, "ep", back)
    across[0] = swap(packed)
    weights, done = [gate, up], up
    for k in range(2, far):
        came[k - 1], came[1 - k] = after(came[k - 1], done), after(came[1 - k], done)
        came[k] = lax.ppermute(came[k - 1], "ep", ahead)
        came[-k] = lax.ppermute(came[1 - k], "ep", back)
        across[k - 1], across[1 - k] = swap(came[k - 1]), swap(came[1 - k])
        if k == 2:
            weights += halve_weights(after(place, came[1]), w_down[0])
            done = weights[-1]
    came[far - 1], came[1 - far] = after(came[far - 1], done), after(came[1 - far], done)
    came["low"] = lax.ppermute(came[far - 1][: rows // 2], "ep", ahead)
    came["high"] = lax.ppermute(came[1 - far][rows // 2 :], "ep", back)
    across[far - 1], across[1 - far] = swap(came[far - 1]), swap(came[1 - far])
    done = run([far - 1, 1 - far], [across[k] for k in range(2 - far, far - 1)])
    came["low"], came["high"] = after((came["low"], came["high"]), done)
    far_keys = ["low", "high"]
    keep(far_keys, *run_expert_in_stages(place, [came[k] for k in far_keys], swap, weights, n))

    to_ahead = value["low"].astype(jnp.bfloat16)
    to_back = value["high"].astype(jnp.bfloat16)
    pad_low, pad_high = ((0, rows - rows // 2), (0, 0)), ((rows // 2, 0), (0, 0))
    for k in range(far - 1, -1, -1):
        behind = lax.ppermute(to_ahead, "ep", ahead)
        front = lax.ppermute(to_back, "ep", back)
        if k == far - 1:
            done = run([j for i in range(1, far - 1) for j in (i, -i)], (to_ahead, to_back))
        elif k == 1:
            done = run([0], (to_ahead, to_back))
        behind, front = behind.astype(jnp.float32), front.astype(jnp.float32)
        if k == far - 1:
            behind, front = jnp.pad(behind, pad_low), jnp.pad(front, pad_high)
        if k:
            to_ahead = (value[-k] + behind).astype(jnp.bfloat16)
            to_back = (value[k] + front).astype(jnp.bfloat16)
        if k in (far - 1, 1):
            to_ahead, to_back = after(to_ahead, done), after(to_back, done)
    return (value[0] + behind + front).astype(jnp.bfloat16)


def swiglu_expert(rows, gate_part, up_part, down_part):
    gated = jnp.dot(rows, gate_part, preferred_element_type=jnp.float32)
    lifted = jnp.dot(rows, up_part, preferred_element_type=jnp.float32)
    hidden = (jax.nn.silu(gated) * lifted).astype(jnp.bfloat16)
    return jnp.dot(hidden, down_part, preferred_element_type=jnp.float32)


def slot_table(expert_ids, n_experts):
    routed = expert_ids.reshape(-1)
    pair_count = routed.shape[0]
    onehot = (routed[:, None] == jnp.arange(n_experts, dtype=jnp.int32)[None, :]).astype(
        jnp.bfloat16
    )
    row_index = lax.broadcasted_iota(jnp.int32, (pair_count, pair_count), 0)
    col_index = lax.broadcasted_iota(jnp.int32, (pair_count, pair_count), 1)
    earlier = (row_index > col_index).astype(jnp.bfloat16)
    before = jnp.dot(earlier, onehot, preferred_element_type=jnp.float32)
    slots = jnp.sum(before * onehot.astype(jnp.float32), axis=1).astype(jnp.int32)
    return (routed, slots)


def slot_body(tokens, expert_ids, gate_probs, w_gate, w_up, w_down):
    n_experts = lax.axis_size("ep")
    tok_rows, top_count = expert_ids.shape
    capacity = 3 * tok_rows * top_count // (2 * n_experts)
    routed, slots = slot_table(expert_ids, n_experts)
    positions = routed * capacity + slots
    pair_token = jnp.repeat(jnp.arange(tok_rows, dtype=jnp.int32), top_count)
    buffer_rows = n_experts * capacity
    owners = jnp.full((buffer_rows,), tok_rows, jnp.int32).at[positions].set(pair_token)
    half_slots = capacity // 2
    whole_tokens = lax.all_gather(tokens, "tp", axis=1, tiled=True)
    width = whole_tokens.shape[1]
    gate_full, up_full = (
        lax.all_gather(w_gate, "tp", axis=2, tiled=True),
        lax.all_gather(w_up, "tp", axis=2, tiled=True),
    )
    down_full = lax.all_gather(w_down, "tp", axis=1, tiled=True)
    padded = jnp.concatenate([whole_tokens, jnp.zeros((1, width), whole_tokens.dtype)], 0)
    outgoing = padded[owners].reshape(n_experts, capacity, width)
    lane = lax.axis_index("tp")
    mine = lax.dynamic_slice_in_dim(outgoing, lane * half_slots, half_slots, 1)
    block = lax.all_to_all(mine, "ep", split_axis=0, concat_axis=0, tiled=True)
    sources, items, columns = block.shape
    result = swiglu_expert(
        block.reshape(sources * items, columns), gate_full[0], up_full[0], down_full[0]
    )
    result = result.astype(jnp.bfloat16).reshape(sources, items, columns)
    returned = lax.all_to_all(result, "ep", split_axis=0, concat_axis=0, tiled=True)
    received = returned.reshape(n_experts * half_slots, width)
    in_half = slots // half_slots == lane
    local_pos = routed * half_slots + slots % half_slots
    picked = received[local_pos].astype(jnp.float32).reshape(tok_rows, top_count, width)
    weighted = jnp.where(in_half.reshape(tok_rows, top_count), gate_probs, 0.0)
    partial_value = jnp.sum(weighted[:, :, None] * picked, axis=1)
    return lax.psum_scatter(partial_value, "tp", scatter_dimension=1, tiled=True).astype(
        jnp.bfloat16
    )


def solution(mesh):
    in_specs = (
        P(("groups", "ep"), "tp"),
        P(("groups", "ep"), None),
        P(("groups", "ep"), None),
        P("ep", None, "tp"),
        P("ep", None, "tp"),
        P("ep", "tp", None),
    )
    out_specs = P(("groups", "ep"), "tp")

    def body(tokens, expert_ids, *rest):
        n, top = lax.axis_size("ep"), expert_ids.shape[1]
        small = n <= 4 * top and n % 2 == 0 and n >= 6 and lax.axis_size("tp") == 2
        return (ring_body if small else slot_body)(tokens, expert_ids, *rest)

    return jax.shard_map(body, mesh=mesh, in_specs=in_specs, out_specs=out_specs, check_vma=False)
```

```python
import functools

import jax
import jax.numpy as jnp
from jax import lax
from jax.experimental import pallas as pl
from jax.experimental.pallas import tpu as pltpu
from jax.sharding import PartitionSpec as P

SPLITS = 3


def in_vmem(shape, dtype=jnp.bfloat16):
    return pltpu.MemorySpace.VMEM(shape, dtype)


def hold(x):
    return pltpu.with_memory_space_constraint(x, pltpu.VMEM)


def after(x, done):
    return lax.optimization_barrier((x, done))[0]


def pack_kernel(n_experts, tokens_in, ids_in, probs_in, packed, tokens, ids, probs, sems):
    copies = [
        pltpu.make_async_copy(src, dst, sems.at[i])
        for i, (src, dst) in enumerate(((ids_in, ids), (probs_in, probs), (tokens_in, tokens)))
    ]
    for copy in copies:
        copy.start()
    top, rows = ids.shape
    half = tokens.shape[1]
    copies[0].wait()
    copies[1].wait()
    expert = lax.broadcasted_iota(jnp.int32, (n_experts, rows), 0)
    rest = jnp.zeros((n_experts, rows), jnp.float32)
    for k in range(top):
        rest += jnp.where(ids[k : k + 1, :] == expert, probs[k : k + 1, :], 0.0)
    terms = []
    for _ in range(SPLITS):
        term = rest.astype(jnp.bfloat16).astype(jnp.float32)
        terms.append(term)
        rest = rest - term
    packed[:, half:] = jnp.concatenate(terms, axis=0).T.astype(jnp.bfloat16)
    copies[2].wait()
    packed[:, :half] = tokens[...]


def pack(tokens, expert_ids, gate_probs, n_experts):
    rows, half = tokens.shape
    args = (tokens, expert_ids.T, gate_probs.T)
    return pl.pallas_call(
        functools.partial(pack_kernel, n_experts),
        out_shape=in_vmem((rows, half + SPLITS * n_experts)),
        in_specs=[pl.BlockSpec(memory_space=pltpu.HBM)] * 3,
        out_specs=pl.BlockSpec(memory_space=pltpu.VMEM),
        scratch_shapes=[pltpu.VMEM(a.shape, a.dtype) for a in args] + [pltpu.SemaphoreType.DMA((3,))],
        compiler_params=pltpu.CompilerParams(vmem_limit_bytes=8 << 20),
    )(*[pltpu.with_memory_space_constraint(a, pltpu.HBM) for a in args])


def pieces(hidden):
    first = -(-hidden // 256) * 128
    return ((0, first), (first, hidden))


def turn_kernel(after_this, gate_in, up_in, gate, up, gate_buf, up_buf, sems):
    steps = []
    for i, (src, buf, out) in enumerate(((gate_in, gate_buf, gate), (up_in, up_buf, up))):
        for j, (start, stop) in enumerate(pieces(src.shape[0])):
            span = pl.ds(start, stop - start)
            steps.append((pltpu.make_async_copy(src.at[span], buf.at[span], sems.at[i, j]), buf, out, start, stop))
    for copy, *_ in steps:
        copy.start()
    for copy, buf, out, start, stop in steps:
        copy.wait()
        out[:, start:stop] = buf[start:stop, :].T


def turn_weights(after_this, *weights):
    hidden, width = weights[0].shape
    return pl.pallas_call(
        turn_kernel,
        out_shape=[in_vmem((width, hidden))] * 2,
        in_specs=[pl.BlockSpec(memory_space=pltpu.SMEM)] + [pl.BlockSpec(memory_space=pltpu.HBM)] * 2,
        out_specs=[pl.BlockSpec(memory_space=pltpu.VMEM)] * 2,
        scratch_shapes=[pltpu.VMEM((hidden, width), jnp.bfloat16)] * 2 + [pltpu.SemaphoreType.DMA((2, 2))],
        compiler_params=pltpu.CompilerParams(vmem_limit_bytes=32 << 20),
        cost_estimate=pl.CostEstimate(flops=0, bytes_accessed=8 * hidden * width, transcendentals=0),
    )(after_this, *[pltpu.with_memory_space_constraint(w, pltpu.HBM) for w in weights])


def halve_kernel(place, down_in, down_mine, down_theirs, down_buf, sems):
    lane = place[0]
    half = down_mine.shape[1]
    spans = [slice(start, stop) for start, stop in pieces(down_in.shape[0])]
    copies = [
        pltpu.make_async_copy(down_in.at[pl.ds(s.start, s.stop - s.start)], down_buf.at[pl.ds(s.start, s.stop - s.start)], sems.at[i])
        for i, s in enumerate(spans)
    ]
    for copy in copies:
        copy.start()
    for copy, s in zip(copies, spans):
        copy.wait()

        @pl.when(lane == 0)
        def _():
            down_mine[s, :] = down_buf[s, :half]
            down_theirs[s, :] = down_buf[s, half:]

        @pl.when(lane != 0)
        def _():
            down_mine[s, :] = down_buf[s, half:]
            down_theirs[s, :] = down_buf[s, :half]


def halve_weights(place, w_down):
    hidden, width = w_down.shape
    return pl.pallas_call(
        halve_kernel,
        out_shape=[in_vmem((hidden, width // 2))] * 2,
        in_specs=[pl.BlockSpec(memory_space=pltpu.SMEM), pl.BlockSpec(memory_space=pltpu.HBM)],
        out_specs=[pl.BlockSpec(memory_space=pltpu.VMEM)] * 2,
        scratch_shapes=[pltpu.VMEM((hidden, width), jnp.bfloat16), pltpu.SemaphoreType.DMA((2,))],
        compiler_params=pltpu.CompilerParams(vmem_limit_bytes=32 << 20),
        cost_estimate=pl.CostEstimate(flops=0, bytes_accessed=8 * hidden * width, transcendentals=0),
    )(place, pltpu.with_memory_space_constraint(w_down, pltpu.HBM))


def gather_rows(blocks, x, width):
    start = 0
    for block in blocks:
        x[start : start + block.shape[0], :] = block[:, :width]
        start += block.shape[0]
    if start < x.shape[0]:
        x[start:, :] = jnp.zeros((x.shape[0] - start, width), x.dtype)


def project(x, lane, w):
    half = x.shape[1]
    return jnp.dot(x[...], w[pl.ds(pl.multiple_of(lane * half, 16), half), :], preferred_element_type=jnp.float32)


def activate(gated, lifted):
    return (gated / (1.0 + jnp.exp(-gated)) * lifted).astype(jnp.bfloat16)


def gate_weights(blocks, half, expert, n_experts):
    weights = []
    for block in blocks:
        terms = block[:, half:].astype(jnp.float32)
        column = lax.broadcasted_iota(jnp.int32, terms.shape, 1)
        weights.append(jnp.sum(jnp.where(lax.rem(column, n_experts) == expert, terms, 0.0), axis=1, keepdims=True))
    return weights


def lower(hidden, w, weights, *outs):
    value = jnp.dot(hidden, w[...], preferred_element_type=jnp.float32)
    places = [(out, at) for out in outs for at in range(0, out.shape[0], weights[0].shape[0])]
    start = 0
    for weight, (out, at) in zip(weights, places):
        rows = weight.shape[0]
        out[at : at + rows] = (value[start : start + rows] * weight).astype(jnp.bfloat16)
        start += rows


def expert_kernel(n_blocks, n_experts, place, *refs):
    own, across = refs[:n_blocks], refs[n_blocks : 2 * n_blocks]
    w_gate, w_up, down_mine, down_theirs, *outs, x_own, x_across = refs[2 * n_blocks :]
    lane, expert = place[0], place[1]
    half = x_own.shape[1]
    gather_rows(own, x_own, half)
    gather_rows(across, x_across, half)
    gated = project(x_own, lane, w_gate) + project(x_across, 1 - lane, w_gate)
    lifted = project(x_own, lane, w_up) + project(x_across, 1 - lane, w_up)
    hidden = activate(gated, lifted)
    weights = gate_weights(own, half, expert, n_experts)
    mine, theirs = outs[: len(outs) // 2], outs[len(outs) // 2 :]
    lower(hidden, down_theirs, weights, *theirs)
    lower(hidden, down_mine, weights, *mine)


def first_kernel(n_blocks, place, *refs):
    own = refs[:n_blocks]
    w_gate, w_up, gated, lifted, x = refs[n_blocks:]
    gather_rows(own, x, x.shape[1])
    gated[...] = project(x, place[0], w_gate)
    lifted[...] = project(x, place[0], w_up)


def second_kernel(n_blocks, n_experts, place, *refs):
    own, across = refs[:n_blocks], refs[n_blocks : 2 * n_blocks]
    gated, lifted, w_gate, w_up, down_theirs, hidden, *theirs, x = refs[2 * n_blocks :]
    half = x.shape[1]
    gather_rows(across, x, half)
    there = 1 - place[0]
    hidden[...] = activate(gated[...] + project(x, there, w_gate), lifted[...] + project(x, there, w_up))
    lower(hidden[...], down_theirs, gate_weights(own, half, place[1], n_experts), *theirs)


def third_kernel(n_blocks, n_experts, place, *refs):
    own = refs[:n_blocks]
    hidden, down_mine, *mine = refs[n_blocks:]
    lower(hidden[...], down_mine, gate_weights(own, mine[0].shape[1], place[1], n_experts), *mine)


def call(kernel, place, args, out_shape, scratch_shapes, flops):
    vmem = pl.BlockSpec(memory_space=pltpu.VMEM)
    return pl.pallas_call(
        kernel,
        out_shape=out_shape,
        in_specs=[pl.BlockSpec(memory_space=pltpu.SMEM)] + [vmem] * len(args),
        out_specs=[vmem] * len(out_shape),
        scratch_shapes=scratch_shapes,
        compiler_params=pltpu.CompilerParams(vmem_limit_bytes=16 << 20),
        cost_estimate=pl.CostEstimate(flops=flops, bytes_accessed=flops // 128, transcendentals=0),
    )(place, *[hold(a) for a in args])


def padded(rows):
    return max(rows, 128)


def run_expert(place, own, across, weights, n_experts):
    width, hidden = weights[0].shape
    half = width // 2
    rows, pairs = sum(a.shape[0] for a in own), max(1, len(own) // 2)
    outs = call(
        functools.partial(expert_kernel, len(own), n_experts),
        place,
        (*own, *across, *weights),
        [in_vmem((rows // pairs, half))] * (2 * pairs),
        [pltpu.VMEM((padded(rows), half), jnp.bfloat16)] * 2,
        6 * padded(rows) * hidden * width,
    )
    return outs[:pairs], outs[pairs:]


def run_expert_in_stages(place, own, across, swap, weights, n_experts):
    gate, up, down_mine, down_theirs = weights
    width, hidden = gate.shape
    half = width // 2
    rows, n_blocks = sum(a.shape[0] for a in own), len(own)
    first = own[0].shape[0]
    products = [in_vmem((padded(rows), hidden), jnp.float32)] * 2
    outs = [in_vmem((first, half)), in_vmem((rows - first, half))]
    x = [pltpu.VMEM((padded(rows), half), jnp.bfloat16)]
    flops = 2 * padded(rows) * hidden * width
    gated, lifted = call(functools.partial(first_kernel, n_blocks), place, (*own, gate, up), products, x, flops)
    units, *theirs = call(
        functools.partial(second_kernel, n_blocks, n_experts),
        place,
        (*own, *across, gated, lifted, gate, up, down_theirs),
        [in_vmem((padded(rows), hidden)), *outs],
        x,
        flops + flops // 2,
    )
    theirs = [swap(a) for a in theirs]
    mine = call(
        functools.partial(third_kernel, n_blocks, n_experts),
        place,
        (*own, units, down_mine),
        outs,
        [],
        flops // 2,
    )
    return mine, theirs


def ring_body(tokens, expert_ids, gate_probs, w_gate, w_up, w_down):
    n = lax.axis_size("ep")
    rows = tokens.shape[0]
    order = list(range(0, n, 2)) + list(range(n - 1, 0, -2))
    ahead = [(order[i], order[(i + 1) % n]) for i in range(n)]
    back = [(b, a) for a, b in ahead]
    swap = functools.partial(lax.ppermute, axis_name="tp", perm=[(0, 1), (1, 0)])
    far = n // 2
    place = jnp.stack([lax.axis_index("tp"), lax.axis_index("ep")]).astype(jnp.int32)
    packed = pack(tokens, expert_ids, gate_probs, n)
    gate, up = turn_weights(after(place, packed), w_gate[0].T, w_up[0].T)

    came, across, value = {0: packed}, {}, {}

    def run(keys, wait_for=None):
        at = place if wait_for is None else after(place, wait_for)
        mine, theirs = run_expert(at, [came[k] for k in keys], [across[k] for k in keys], weights, n)
        return [(keys[2 * i : 2 * i + 2], *pair) for i, pair in enumerate(zip(mine, theirs))]

    def keep(keys, mine, theirs):
        pairs = ((mine, theirs), lax.optimization_barrier((mine, theirs)))
        start = 0
        for i, k in enumerate(keys):
            mine, theirs = pairs[i % 2]
            span = slice(start, start + came[k].shape[0])
            start = span.stop
            value[k] = mine[span].astype(jnp.float32) + theirs[span].astype(jnp.float32)

    came[1] = lax.ppermute(packed, "ep", ahead)
    came[-1] = lax.ppermute(packed, "ep", back)
    across[0] = swap(packed)
    weights, done = [gate, up], [up]
    for k in range(2, far):
        came[k - 1], came[1 - k] = after(came[k - 1], done), after(came[1 - k], done)
        came[k] = lax.ppermute(came[k - 1], "ep", ahead)
        came[-k] = lax.ppermute(came[1 - k], "ep", back)
        across[k - 1], across[1 - k] = swap(came[k - 1]), swap(came[1 - k])
        done = [across[k - 1], across[1 - k]]
        if k == 2:
            weights += halve_weights(after(place, (came[1], across[0])), w_down[0])
            done.append(weights[-1])
    came[far - 1] = after(came[far - 1], done)
    came[far] = lax.ppermute(came[far - 1], "ep", ahead)
    across[far - 1] = swap(came[far - 1])
    near = run([j for i in range(1, far - 1) for j in (i, -i)])
    done = near[0][-1]
    came[far], came[1 - far] = after(came[far], done), after(came[1 - far], done)
    across[far], across[1 - far] = swap(came[far]), swap(came[1 - far])
    last = [far, far - 1, 1 - far]
    for keys, mine, theirs in zip(([far], last[1:]), *run_expert_in_stages(place, [came[k] for k in last], [across[k] for k in last], swap, weights, n)):
        keep(keys, mine, theirs)
    for keys, mine, theirs in near:
        keep(keys, mine, swap(after(theirs, value[far])))

    to_ahead, to_back = value[far].astype(jnp.bfloat16), None
    for k in range(far - 1, -1, -1):
        behind = lax.ppermute(to_ahead, "ep", ahead).astype(jnp.float32)
        front = 0.0 if to_back is None else lax.ppermute(to_back, "ep", back).astype(jnp.float32)
        done = None
        if k == 1:
            ((keys, mine, done),) = run([0], (to_ahead, to_back))
            keep(keys, mine, swap(done))
        if k:
            to_ahead = (value[-k] + behind).astype(jnp.bfloat16)
            to_back = (value[k] + front).astype(jnp.bfloat16)
        if done is not None:
            to_ahead, to_back = after(to_ahead, done), after(to_back, done)
    return (value[0] + behind + front).astype(jnp.bfloat16)


def swiglu_expert(rows, gate_part, up_part, down_part):
    gated = jnp.dot(rows, gate_part, preferred_element_type=jnp.float32)
    lifted = jnp.dot(rows, up_part, preferred_element_type=jnp.float32)
    hidden = (jax.nn.silu(gated) * lifted).astype(jnp.bfloat16)
    return jnp.dot(hidden, down_part, preferred_element_type=jnp.float32)


def slot_table(expert_ids, n_experts):
    routed = expert_ids.reshape(-1)
    pair_count = routed.shape[0]
    onehot = (routed[:, None] == jnp.arange(n_experts, dtype=jnp.int32)[None, :]).astype(
        jnp.bfloat16
    )
    row_index = lax.broadcasted_iota(jnp.int32, (pair_count, pair_count), 0)
    col_index = lax.broadcasted_iota(jnp.int32, (pair_count, pair_count), 1)
    earlier = (row_index > col_index).astype(jnp.bfloat16)
    before = jnp.dot(earlier, onehot, preferred_element_type=jnp.float32)
    slots = jnp.sum(before * onehot.astype(jnp.float32), axis=1).astype(jnp.int32)
    return (routed, slots)


def slot_body(tokens, expert_ids, gate_probs, w_gate, w_up, w_down):
    n_experts = lax.axis_size("ep")
    tok_rows, top_count = expert_ids.shape
    capacity = 3 * tok_rows * top_count // (2 * n_experts)
    routed, slots = slot_table(expert_ids, n_experts)
    positions = routed * capacity + slots
    pair_token = jnp.repeat(jnp.arange(tok_rows, dtype=jnp.int32), top_count)
    buffer_rows = n_experts * capacity
    owners = jnp.full((buffer_rows,), tok_rows, jnp.int32).at[positions].set(pair_token)
    half_slots = capacity // 2
    whole_tokens = lax.all_gather(tokens, "tp", axis=1, tiled=True)
    width = whole_tokens.shape[1]
    gate_full, up_full = (
        lax.all_gather(w_gate, "tp", axis=2, tiled=True),
        lax.all_gather(w_up, "tp", axis=2, tiled=True),
    )
    down_full = lax.all_gather(w_down, "tp", axis=1, tiled=True)
    padded = jnp.concatenate([whole_tokens, jnp.zeros((1, width), whole_tokens.dtype)], 0)
    outgoing = padded[owners].reshape(n_experts, capacity, width)
    lane = lax.axis_index("tp")
    mine = lax.dynamic_slice_in_dim(outgoing, lane * half_slots, half_slots, 1)
    block = lax.all_to_all(mine, "ep", split_axis=0, concat_axis=0, tiled=True)
    sources, items, columns = block.shape
    result = swiglu_expert(
        block.reshape(sources * items, columns), gate_full[0], up_full[0], down_full[0]
    )
    result = result.astype(jnp.bfloat16).reshape(sources, items, columns)
    returned = lax.all_to_all(result, "ep", split_axis=0, concat_axis=0, tiled=True)
    received = returned.reshape(n_experts * half_slots, width)
    in_half = slots // half_slots == lane
    local_pos = routed * half_slots + slots % half_slots
    picked = received[local_pos].astype(jnp.float32).reshape(tok_rows, top_count, width)
    weighted = jnp.where(in_half.reshape(tok_rows, top_count), gate_probs, 0.0)
    partial_value = jnp.sum(weighted[:, :, None] * picked, axis=1)
    return lax.psum_scatter(partial_value, "tp", scatter_dimension=1, tiled=True).astype(
        jnp.bfloat16
    )


def solution(mesh):
    in_specs = (
        P(("groups", "ep"), "tp"),
        P(("groups", "ep"), None),
        P(("groups", "ep"), None),
        P("ep", None, "tp"),
        P("ep", None, "tp"),
        P("ep", "tp", None),
    )
    out_specs = P(("groups", "ep"), "tp")

    def body(tokens, expert_ids, *rest):
        n, top = lax.axis_size("ep"), expert_ids.shape[1]
        small = n <= 4 * top and n % 2 == 0 and n >= 6 and lax.axis_size("tp") == 2
        return (ring_body if small else slot_body)(tokens, expert_ids, *rest)

    return jax.shard_map(body, mesh=mesh, in_specs=in_specs, out_specs=out_specs, check_vma=False)
```

```python
import functools

import jax
import jax.numpy as jnp
from jax import lax
from jax.experimental import pallas as pl
from jax.experimental.pallas import tpu as pltpu
from jax.sharding import PartitionSpec as P

SPLITS = 3


def in_vmem(shape, dtype=jnp.bfloat16):
    return pltpu.MemorySpace.VMEM(shape, dtype)


def hold(x):
    return pltpu.with_memory_space_constraint(x, pltpu.VMEM)


def after(x, done):
    return lax.optimization_barrier((x, done))[0]


def pack_kernel(n_experts, tokens_in, ids_in, probs_in, packed, tokens, ids, probs, sems):
    copies = [
        pltpu.make_async_copy(src, dst, sems.at[i])
        for i, (src, dst) in enumerate(((ids_in, ids), (probs_in, probs), (tokens_in, tokens)))
    ]
    for copy in copies:
        copy.start()
    top, rows = ids.shape
    half = tokens.shape[1]
    copies[0].wait()
    copies[1].wait()
    expert = lax.broadcasted_iota(jnp.int32, (n_experts, rows), 0)
    rest = jnp.zeros((n_experts, rows), jnp.float32)
    for k in range(top):
        rest += jnp.where(ids[k : k + 1, :] == expert, probs[k : k + 1, :], 0.0)
    terms = []
    for _ in range(SPLITS):
        term = rest.astype(jnp.bfloat16).astype(jnp.float32)
        terms.append(term)
        rest = rest - term
    packed[:, half:] = jnp.concatenate(terms, axis=0).T.astype(jnp.bfloat16)
    copies[2].wait()
    packed[:, :half] = tokens[...]


def pack(tokens, expert_ids, gate_probs, n_experts):
    rows, half = tokens.shape
    args = (tokens, expert_ids.T, gate_probs.T)
    return pl.pallas_call(
        functools.partial(pack_kernel, n_experts),
        out_shape=in_vmem((rows, half + SPLITS * n_experts)),
        in_specs=[pl.BlockSpec(memory_space=pltpu.HBM)] * 3,
        out_specs=pl.BlockSpec(memory_space=pltpu.VMEM),
        scratch_shapes=[pltpu.VMEM(a.shape, a.dtype) for a in args] + [pltpu.SemaphoreType.DMA((3,))],
        compiler_params=pltpu.CompilerParams(vmem_limit_bytes=8 << 20),
    )(*[pltpu.with_memory_space_constraint(a, pltpu.HBM) for a in args])


def pieces(hidden):
    first = -(-hidden // 256) * 128
    return ((0, first), (first, hidden))


def turn_kernel(after_this, gate_in, up_in, gate, up, gate_buf, up_buf, sems):
    steps = []
    for i, (src, buf, out) in enumerate(((gate_in, gate_buf, gate), (up_in, up_buf, up))):
        for j, (start, stop) in enumerate(pieces(src.shape[0])):
            span = pl.ds(start, stop - start)
            steps.append((pltpu.make_async_copy(src.at[span], buf.at[span], sems.at[i, j]), buf, out, start, stop))
    for copy, *_ in steps:
        copy.start()
    for copy, buf, out, start, stop in steps:
        copy.wait()
        out[:, start:stop] = buf[start:stop, :].T


def turn_weights(after_this, *weights):
    hidden, width = weights[0].shape
    return pl.pallas_call(
        turn_kernel,
        out_shape=[in_vmem((width, hidden))] * 2,
        in_specs=[pl.BlockSpec(memory_space=pltpu.SMEM)] + [pl.BlockSpec(memory_space=pltpu.HBM)] * 2,
        out_specs=[pl.BlockSpec(memory_space=pltpu.VMEM)] * 2,
        scratch_shapes=[pltpu.VMEM((hidden, width), jnp.bfloat16)] * 2 + [pltpu.SemaphoreType.DMA((2, 2))],
        compiler_params=pltpu.CompilerParams(vmem_limit_bytes=32 << 20),
        cost_estimate=pl.CostEstimate(flops=0, bytes_accessed=8 * hidden * width, transcendentals=0),
    )(after_this, *[pltpu.with_memory_space_constraint(w, pltpu.HBM) for w in weights])


def halve_kernel(place, down_in, down_mine, down_theirs, down_buf, sems):
    lane = place[0]
    half = down_mine.shape[1]
    spans = [slice(start, stop) for start, stop in pieces(down_in.shape[0])]
    copies = [
        pltpu.make_async_copy(down_in.at[pl.ds(s.start, s.stop - s.start)], down_buf.at[pl.ds(s.start, s.stop - s.start)], sems.at[i])
        for i, s in enumerate(spans)
    ]
    for copy in copies:
        copy.start()
    for copy, s in zip(copies, spans):
        copy.wait()

        @pl.when(lane == 0)
        def _():
            down_mine[s, :] = down_buf[s, :half]
            down_theirs[s, :] = down_buf[s, half:]

        @pl.when(lane != 0)
        def _():
            down_mine[s, :] = down_buf[s, half:]
            down_theirs[s, :] = down_buf[s, :half]


def halve_weights(place, w_down):
    hidden, width = w_down.shape
    return pl.pallas_call(
        halve_kernel,
        out_shape=[in_vmem((hidden, width // 2))] * 2,
        in_specs=[pl.BlockSpec(memory_space=pltpu.SMEM), pl.BlockSpec(memory_space=pltpu.HBM)],
        out_specs=[pl.BlockSpec(memory_space=pltpu.VMEM)] * 2,
        scratch_shapes=[pltpu.VMEM((hidden, width), jnp.bfloat16), pltpu.SemaphoreType.DMA((2,))],
        compiler_params=pltpu.CompilerParams(vmem_limit_bytes=32 << 20),
        cost_estimate=pl.CostEstimate(flops=0, bytes_accessed=8 * hidden * width, transcendentals=0),
    )(place, pltpu.with_memory_space_constraint(w_down, pltpu.HBM))


def gather_rows(blocks, x, width):
    start = 0
    for block in blocks:
        x[start : start + block.shape[0], :] = block[:, :width]
        start += block.shape[0]
    if start < x.shape[0]:
        x[start:, :] = jnp.zeros((x.shape[0] - start, width), x.dtype)


def project(x, lane, w):
    half = x.shape[1]
    return jnp.dot(x[...], w[pl.ds(pl.multiple_of(lane * half, 16), half), :], preferred_element_type=jnp.float32)


def activate(gated, lifted):
    return (gated / (1.0 + jnp.exp(-gated)) * lifted).astype(jnp.bfloat16)


def gate_weights(blocks, half, expert, n_experts):
    weights = []
    for block in blocks:
        terms = block[:, half:].astype(jnp.float32)
        column = lax.broadcasted_iota(jnp.int32, terms.shape, 1)
        weights.append(jnp.sum(jnp.where(lax.rem(column, n_experts) == expert, terms, 0.0), axis=1, keepdims=True))
    return weights


def lower(hidden, w, weights, *outs):
    value = jnp.dot(hidden, w[...], preferred_element_type=jnp.float32)
    places = [(out, at) for out in outs for at in range(0, out.shape[0], weights[0].shape[0])]
    start = 0
    for weight, (out, at) in zip(weights, places):
        rows = weight.shape[0]
        out[at : at + rows] = (value[start : start + rows] * weight).astype(jnp.bfloat16)
        start += rows


def expert_kernel(n_blocks, n_experts, place, *refs):
    own, across = refs[:n_blocks], refs[n_blocks : 2 * n_blocks]
    w_gate, w_up, down_mine, down_theirs, *outs, x_own, x_across = refs[2 * n_blocks :]
    lane, expert = place[0], place[1]
    half = x_own.shape[1]
    gather_rows(own, x_own, half)
    gather_rows(across, x_across, half)
    gated = project(x_own, lane, w_gate) + project(x_across, 1 - lane, w_gate)
    lifted = project(x_own, lane, w_up) + project(x_across, 1 - lane, w_up)
    hidden = activate(gated, lifted)
    weights = gate_weights(own, half, expert, n_experts)
    mine, theirs = outs[: len(outs) // 2], outs[len(outs) // 2 :]
    lower(hidden, down_theirs, weights, *theirs)
    lower(hidden, down_mine, weights, *mine)


def first_kernel(n_blocks, place, *refs):
    own = refs[:n_blocks]
    w_gate, w_up, gated, lifted, x = refs[n_blocks:]
    gather_rows(own, x, x.shape[1])
    gated[...] = project(x, place[0], w_gate)
    lifted[...] = project(x, place[0], w_up)


def second_kernel(n_blocks, n_experts, place, *refs):
    own, across = refs[:n_blocks], refs[n_blocks : 2 * n_blocks]
    gated, lifted, w_gate, w_up, down_theirs, hidden, *theirs, x = refs[2 * n_blocks :]
    half = x.shape[1]
    gather_rows(across, x, half)
    there = 1 - place[0]
    hidden[...] = activate(gated[...] + project(x, there, w_gate), lifted[...] + project(x, there, w_up))
    lower(hidden[...], down_theirs, gate_weights(own, half, place[1], n_experts), *theirs)


def third_kernel(n_blocks, n_experts, place, *refs):
    own = refs[:n_blocks]
    hidden, down_mine, *mine = refs[n_blocks:]
    lower(hidden[...], down_mine, gate_weights(own, mine[0].shape[1], place[1], n_experts), *mine)


def call(kernel, place, args, out_shape, scratch_shapes, flops):
    vmem = pl.BlockSpec(memory_space=pltpu.VMEM)
    return pl.pallas_call(
        kernel,
        out_shape=out_shape,
        in_specs=[pl.BlockSpec(memory_space=pltpu.SMEM)] + [vmem] * len(args),
        out_specs=[vmem] * len(out_shape),
        scratch_shapes=scratch_shapes,
        compiler_params=pltpu.CompilerParams(vmem_limit_bytes=16 << 20),
        cost_estimate=pl.CostEstimate(flops=flops, bytes_accessed=flops // 128, transcendentals=0),
    )(place, *[hold(a) for a in args])


def padded(rows):
    return max(rows, 128)


def run_expert(place, own, across, weights, n_experts):
    width, hidden = weights[0].shape
    half = width // 2
    rows, pairs = sum(a.shape[0] for a in own), max(1, len(own) // 2)
    outs = call(
        functools.partial(expert_kernel, len(own), n_experts),
        place,
        (*own, *across, *weights),
        [in_vmem((rows // pairs, half))] * (2 * pairs),
        [pltpu.VMEM((padded(rows), half), jnp.bfloat16)] * 2,
        6 * padded(rows) * hidden * width,
    )
    return outs[:pairs], outs[pairs:]


def run_expert_in_stages(place, own, across, swap, weights, n_experts):
    gate, up, down_mine, down_theirs = weights
    width, hidden = gate.shape
    half = width // 2
    rows, n_blocks = sum(a.shape[0] for a in own), len(own)
    first = own[0].shape[0]
    products = [in_vmem((padded(rows), hidden), jnp.float32)] * 2
    outs = [in_vmem((first, half)), in_vmem((rows - first, half))]
    x = [pltpu.VMEM((padded(rows), half), jnp.bfloat16)]
    flops = 2 * padded(rows) * hidden * width
    gated, lifted = call(functools.partial(first_kernel, n_blocks), place, (*own, gate, up), products, x, flops)
    units, *theirs = call(
        functools.partial(second_kernel, n_blocks, n_experts),
        place,
        (*own, *across, gated, lifted, gate, up, down_theirs),
        [in_vmem((padded(rows), hidden)), *outs],
        x,
        flops + flops // 2,
    )
    theirs = [swap(a) for a in theirs]
    mine = call(
        functools.partial(third_kernel, n_blocks, n_experts),
        place,
        (*own, units, down_mine),
        outs,
        [],
        flops // 2,
    )
    return mine, theirs


def ring_body(tokens, expert_ids, gate_probs, w_gate, w_up, w_down):
    n = lax.axis_size("ep")
    rows = tokens.shape[0]
    order = list(range(0, n, 2)) + list(range(n - 1, 0, -2))
    ahead = [(order[i], order[(i + 1) % n]) for i in range(n)]
    back = [(b, a) for a, b in ahead]
    swap = functools.partial(lax.ppermute, axis_name="tp", perm=[(0, 1), (1, 0)])
    far = n // 2
    place = jnp.stack([lax.axis_index("tp"), lax.axis_index("ep")]).astype(jnp.int32)
    packed = pack(tokens, expert_ids, gate_probs, n)
    gate, up = turn_weights(after(place, packed), w_gate[0].T, w_up[0].T)

    came, across, value = {0: packed}, {}, {}

    def run(keys, wait_for=None):
        at = place if wait_for is None else after(place, wait_for)
        mine, theirs = run_expert(at, [came[k] for k in keys], [across[k] for k in keys], weights, n)
        return [(keys[2 * i : 2 * i + 2], *pair) for i, pair in enumerate(zip(mine, theirs))]

    def keep(keys, mine, theirs):
        pairs = ((mine, theirs), lax.optimization_barrier((mine, theirs)))
        start = 0
        for i, k in enumerate(keys):
            mine, theirs = pairs[i % 2]
            span = slice(start, start + came[k].shape[0])
            start = span.stop
            value[k] = mine[span].astype(jnp.float32) + theirs[span].astype(jnp.float32)

    came[1] = lax.ppermute(packed, "ep", ahead)
    came[-1] = lax.ppermute(packed, "ep", back)
    across[0] = swap(packed)
    weights, done, near = [gate, up], up, []
    for k in range(2, far + 1):
        came[k - 1], came[1 - k] = after(came[k - 1], done), after(came[1 - k], done)
        came[k] = lax.ppermute(came[k - 1], "ep", ahead)
        if k < far:
            came[-k] = lax.ppermute(came[1 - k], "ep", back)
        across[k - 1], across[1 - k] = swap(came[k - 1]), swap(came[1 - k])
        if k == 2:
            weights += halve_weights(after(place, came[1]), w_down[0])
            done = weights[-1]
        else:
            near += run([k - 2, 2 - k])
            done = near[-1][-1]
    came[far] = after(came[far], done)
    across[far] = swap(came[far])
    last = [far, far - 1, 1 - far]
    for keys, mine, theirs in zip(([far], last[1:]), *run_expert_in_stages(place, [came[k] for k in last], [across[k] for k in last], swap, weights, n)):
        keep(keys, mine, theirs)
    for keys, mine, theirs in near:
        keep(keys, mine, swap(after(theirs, value[far])))

    to_ahead, to_back = value[far].astype(jnp.bfloat16), None
    for k in range(far - 1, -1, -1):
        behind = lax.ppermute(to_ahead, "ep", ahead).astype(jnp.float32)
        front = 0.0 if to_back is None else lax.ppermute(to_back, "ep", back).astype(jnp.float32)
        done = None
        if k == 1:
            ((keys, mine, done),) = run([0], (to_ahead, to_back))
            keep(keys, mine, swap(done))
        if k:
            to_ahead = (value[-k] + behind).astype(jnp.bfloat16)
            to_back = (value[k] + front).astype(jnp.bfloat16)
        if done is not None:
            to_ahead, to_back = after(to_ahead, done), after(to_back, done)
    return (value[0] + behind + front).astype(jnp.bfloat16)


def swiglu_expert(rows, gate_part, up_part, down_part):
    gated = jnp.dot(rows, gate_part, preferred_element_type=jnp.float32)
    lifted = jnp.dot(rows, up_part, preferred_element_type=jnp.float32)
    hidden = (jax.nn.silu(gated) * lifted).astype(jnp.bfloat16)
    return jnp.dot(hidden, down_part, preferred_element_type=jnp.float32)


def slot_table(expert_ids, n_experts):
    routed = expert_ids.reshape(-1)
    pair_count = routed.shape[0]
    onehot = (routed[:, None] == jnp.arange(n_experts, dtype=jnp.int32)[None, :]).astype(
        jnp.bfloat16
    )
    row_index = lax.broadcasted_iota(jnp.int32, (pair_count, pair_count), 0)
    col_index = lax.broadcasted_iota(jnp.int32, (pair_count, pair_count), 1)
    earlier = (row_index > col_index).astype(jnp.bfloat16)
    before = jnp.dot(earlier, onehot, preferred_element_type=jnp.float32)
    slots = jnp.sum(before * onehot.astype(jnp.float32), axis=1).astype(jnp.int32)
    return (routed, slots)


def slot_body(tokens, expert_ids, gate_probs, w_gate, w_up, w_down):
    n_experts = lax.axis_size("ep")
    tok_rows, top_count = expert_ids.shape
    capacity = 3 * tok_rows * top_count // (2 * n_experts)
    routed, slots = slot_table(expert_ids, n_experts)
    positions = routed * capacity + slots
    pair_token = jnp.repeat(jnp.arange(tok_rows, dtype=jnp.int32), top_count)
    buffer_rows = n_experts * capacity
    owners = jnp.full((buffer_rows,), tok_rows, jnp.int32).at[positions].set(pair_token)
    half_slots = capacity // 2
    whole_tokens = lax.all_gather(tokens, "tp", axis=1, tiled=True)
    width = whole_tokens.shape[1]
    gate_full, up_full = (
        lax.all_gather(w_gate, "tp", axis=2, tiled=True),
        lax.all_gather(w_up, "tp", axis=2, tiled=True),
    )
    down_full = lax.all_gather(w_down, "tp", axis=1, tiled=True)
    padded = jnp.concatenate([whole_tokens, jnp.zeros((1, width), whole_tokens.dtype)], 0)
    outgoing = padded[owners].reshape(n_experts, capacity, width)
    lane = lax.axis_index("tp")
    mine = lax.dynamic_slice_in_dim(outgoing, lane * half_slots, half_slots, 1)
    block = lax.all_to_all(mine, "ep", split_axis=0, concat_axis=0, tiled=True)
    sources, items, columns = block.shape
    result = swiglu_expert(
        block.reshape(sources * items, columns), gate_full[0], up_full[0], down_full[0]
    )
    result = result.astype(jnp.bfloat16).reshape(sources, items, columns)
    returned = lax.all_to_all(result, "ep", split_axis=0, concat_axis=0, tiled=True)
    received = returned.reshape(n_experts * half_slots, width)
    in_half = slots // half_slots == lane
    local_pos = routed * half_slots + slots % half_slots
    picked = received[local_pos].astype(jnp.float32).reshape(tok_rows, top_count, width)
    weighted = jnp.where(in_half.reshape(tok_rows, top_count), gate_probs, 0.0)
    partial_value = jnp.sum(weighted[:, :, None] * picked, axis=1)
    return lax.psum_scatter(partial_value, "tp", scatter_dimension=1, tiled=True).astype(
        jnp.bfloat16
    )


def solution(mesh):
    in_specs = (
        P(("groups", "ep"), "tp"),
        P(("groups", "ep"), None),
        P(("groups", "ep"), None),
        P("ep", None, "tp"),
        P("ep", None, "tp"),
        P("ep", "tp", None),
    )
    out_specs = P(("groups", "ep"), "tp")

    def body(tokens, expert_ids, *rest):
        n, top = lax.axis_size("ep"), expert_ids.shape[1]
        small = n <= 4 * top and n % 2 == 0 and n >= 6 and lax.axis_size("tp") == 2
        return (ring_body if small else slot_body)(tokens, expert_ids, *rest)

    return jax.shard_map(body, mesh=mesh, in_specs=in_specs, out_specs=out_specs, check_vma=False)
```

```python
import functools

import jax
import jax.numpy as jnp
from jax import lax
from jax.experimental import pallas as pl
from jax.experimental.pallas import tpu as pltpu
from jax.sharding import PartitionSpec as P

SPLITS = 3


def in_vmem(shape, dtype=jnp.bfloat16):
    return pltpu.MemorySpace.VMEM(shape, dtype)


def hold(x):
    return pltpu.with_memory_space_constraint(x, pltpu.VMEM)


def after(x, done):
    return lax.optimization_barrier((x, done))[0]


def pack_kernel(n_experts, tokens_in, ids_in, probs_in, packed, tokens, ids, probs, sems):
    copies = [
        pltpu.make_async_copy(src, dst, sems.at[i])
        for i, (src, dst) in enumerate(((ids_in, ids), (probs_in, probs), (tokens_in, tokens)))
    ]
    for copy in copies:
        copy.start()
    top, rows = ids.shape
    half = tokens.shape[1]
    copies[0].wait()
    copies[1].wait()
    expert = lax.broadcasted_iota(jnp.int32, (n_experts, rows), 0)
    rest = jnp.zeros((n_experts, rows), jnp.float32)
    for k in range(top):
        rest += jnp.where(ids[k : k + 1, :] == expert, probs[k : k + 1, :], 0.0)
    terms = []
    for _ in range(SPLITS):
        term = rest.astype(jnp.bfloat16).astype(jnp.float32)
        terms.append(term)
        rest = rest - term
    packed[:, half:] = jnp.concatenate(terms, axis=0).T.astype(jnp.bfloat16)
    copies[2].wait()
    packed[:, :half] = tokens[...]


def pack(tokens, expert_ids, gate_probs, n_experts):
    rows, half = tokens.shape
    args = (tokens, expert_ids.T, gate_probs.T)
    return pl.pallas_call(
        functools.partial(pack_kernel, n_experts),
        out_shape=in_vmem((rows, half + SPLITS * n_experts)),
        in_specs=[pl.BlockSpec(memory_space=pltpu.HBM)] * 3,
        out_specs=pl.BlockSpec(memory_space=pltpu.VMEM),
        scratch_shapes=[pltpu.VMEM(a.shape, a.dtype) for a in args] + [pltpu.SemaphoreType.DMA((3,))],
        compiler_params=pltpu.CompilerParams(vmem_limit_bytes=8 << 20),
    )(*[pltpu.with_memory_space_constraint(a, pltpu.HBM) for a in args])


def pieces(hidden):
    first = -(-hidden // 256) * 128
    return ((0, first), (first, hidden))


def turn_kernel(after_this, gate_in, up_in, gate, up, gate_buf, up_buf, sems):
    steps = []
    for i, (src, buf, out) in enumerate(((gate_in, gate_buf, gate), (up_in, up_buf, up))):
        for j, (start, stop) in enumerate(pieces(src.shape[0])):
            span = pl.ds(start, stop - start)
            steps.append((pltpu.make_async_copy(src.at[span], buf.at[span], sems.at[i, j]), buf, out, start, stop))
    for copy, *_ in steps:
        copy.start()
    for copy, buf, out, start, stop in steps:
        copy.wait()
        out[:, start:stop] = buf[start:stop, :].T


def turn_weights(after_this, *weights):
    hidden, width = weights[0].shape
    return pl.pallas_call(
        turn_kernel,
        out_shape=[in_vmem((width, hidden))] * 2,
        in_specs=[pl.BlockSpec(memory_space=pltpu.SMEM)] + [pl.BlockSpec(memory_space=pltpu.HBM)] * 2,
        out_specs=[pl.BlockSpec(memory_space=pltpu.VMEM)] * 2,
        scratch_shapes=[pltpu.VMEM((hidden, width), jnp.bfloat16)] * 2 + [pltpu.SemaphoreType.DMA((2, 2))],
        compiler_params=pltpu.CompilerParams(vmem_limit_bytes=32 << 20),
        cost_estimate=pl.CostEstimate(flops=0, bytes_accessed=8 * hidden * width, transcendentals=0),
    )(after_this, *[pltpu.with_memory_space_constraint(w, pltpu.HBM) for w in weights])


def halve_kernel(place, down_in, down_mine, down_theirs, down_buf, sems):
    lane = place[0]
    half = down_mine.shape[1]
    spans = [slice(start, stop) for start, stop in pieces(down_in.shape[0])]
    copies = [
        pltpu.make_async_copy(down_in.at[pl.ds(s.start, s.stop - s.start)], down_buf.at[pl.ds(s.start, s.stop - s.start)], sems.at[i])
        for i, s in enumerate(spans)
    ]
    for copy in copies:
        copy.start()
    for copy, s in zip(copies, spans):
        copy.wait()

        @pl.when(lane == 0)
        def _():
            down_mine[s, :] = down_buf[s, :half]
            down_theirs[s, :] = down_buf[s, half:]

        @pl.when(lane != 0)
        def _():
            down_mine[s, :] = down_buf[s, half:]
            down_theirs[s, :] = down_buf[s, :half]


def halve_weights(place, w_down):
    hidden, width = w_down.shape
    return pl.pallas_call(
        halve_kernel,
        out_shape=[in_vmem((hidden, width // 2))] * 2,
        in_specs=[pl.BlockSpec(memory_space=pltpu.SMEM), pl.BlockSpec(memory_space=pltpu.HBM)],
        out_specs=[pl.BlockSpec(memory_space=pltpu.VMEM)] * 2,
        scratch_shapes=[pltpu.VMEM((hidden, width), jnp.bfloat16), pltpu.SemaphoreType.DMA((2,))],
        compiler_params=pltpu.CompilerParams(vmem_limit_bytes=32 << 20),
        cost_estimate=pl.CostEstimate(flops=0, bytes_accessed=8 * hidden * width, transcendentals=0),
    )(place, pltpu.with_memory_space_constraint(w_down, pltpu.HBM))


def gather_rows(blocks, x, width):
    start = 0
    for block in blocks:
        x[start : start + block.shape[0], :] = block[:, :width]
        start += block.shape[0]
    if start < x.shape[0]:
        x[start:, :] = jnp.zeros((x.shape[0] - start, width), x.dtype)


def project(x, lane, w):
    half = x.shape[1]
    return jnp.dot(x[...], w[pl.ds(pl.multiple_of(lane * half, 16), half), :], preferred_element_type=jnp.float32)


def activate(gated, lifted):
    return (gated / (1.0 + jnp.exp(-gated)) * lifted).astype(jnp.bfloat16)


def gate_weights(blocks, half, expert, n_experts):
    weights = []
    for block in blocks:
        terms = block[:, half:].astype(jnp.float32)
        column = lax.broadcasted_iota(jnp.int32, terms.shape, 1)
        weights.append(jnp.sum(jnp.where(lax.rem(column, n_experts) == expert, terms, 0.0), axis=1, keepdims=True))
    return weights


def lower(hidden, w, weights, *outs):
    value = jnp.dot(hidden, w[...], preferred_element_type=jnp.float32)
    places = [(out, at) for out in outs for at in range(0, out.shape[0], weights[0].shape[0])]
    start = 0
    for weight, (out, at) in zip(weights, places):
        rows = weight.shape[0]
        out[at : at + rows] = (value[start : start + rows] * weight).astype(jnp.bfloat16)
        start += rows


def expert_kernel(n_blocks, n_experts, place, *refs):
    own, across = refs[:n_blocks], refs[n_blocks : 2 * n_blocks]
    w_gate, w_up, down_mine, down_theirs, *outs, x_own, x_across = refs[2 * n_blocks :]
    lane, expert = place[0], place[1]
    half = x_own.shape[1]
    gather_rows(own, x_own, half)
    gather_rows(across, x_across, half)
    gated = project(x_own, lane, w_gate) + project(x_across, 1 - lane, w_gate)
    lifted = project(x_own, lane, w_up) + project(x_across, 1 - lane, w_up)
    hidden = activate(gated, lifted)
    weights = gate_weights(own, half, expert, n_experts)
    mine, theirs = outs[: len(outs) // 2], outs[len(outs) // 2 :]
    lower(hidden, down_theirs, weights, *theirs)
    lower(hidden, down_mine, weights, *mine)


def first_kernel(n_blocks, place, *refs):
    own = refs[:n_blocks]
    w_gate, w_up, gated, lifted, x = refs[n_blocks:]
    gather_rows(own, x, x.shape[1])
    gated[...] = project(x, place[0], w_gate)
    lifted[...] = project(x, place[0], w_up)


def second_kernel(n_blocks, n_experts, place, *refs):
    own, across = refs[:n_blocks], refs[n_blocks : 2 * n_blocks]
    gated, lifted, w_gate, w_up, down_theirs, hidden, *theirs, x = refs[2 * n_blocks :]
    half = x.shape[1]
    gather_rows(across, x, half)
    there = 1 - place[0]
    hidden[...] = activate(gated[...] + project(x, there, w_gate), lifted[...] + project(x, there, w_up))
    lower(hidden[...], down_theirs, gate_weights(own, half, place[1], n_experts), *theirs)


def third_kernel(n_blocks, n_experts, place, *refs):
    own = refs[:n_blocks]
    hidden, down_mine, *mine = refs[n_blocks:]
    lower(hidden[...], down_mine, gate_weights(own, mine[0].shape[1], place[1], n_experts), *mine)


def call(kernel, place, args, out_shape, scratch_shapes, flops):
    vmem = pl.BlockSpec(memory_space=pltpu.VMEM)
    return pl.pallas_call(
        kernel,
        out_shape=out_shape,
        in_specs=[pl.BlockSpec(memory_space=pltpu.SMEM)] + [vmem] * len(args),
        out_specs=[vmem] * len(out_shape),
        scratch_shapes=scratch_shapes,
        compiler_params=pltpu.CompilerParams(vmem_limit_bytes=16 << 20),
        cost_estimate=pl.CostEstimate(flops=flops, bytes_accessed=flops // 128, transcendentals=0),
    )(place, *[hold(a) for a in args])


def padded(rows):
    return max(rows, 128)


def run_expert(place, own, across, weights, n_experts):
    width, hidden = weights[0].shape
    half = width // 2
    rows, pairs = sum(a.shape[0] for a in own), max(1, len(own) // 2)
    outs = call(
        functools.partial(expert_kernel, len(own), n_experts),
        place,
        (*own, *across, *weights),
        [in_vmem((rows // pairs, half))] * (2 * pairs),
        [pltpu.VMEM((padded(rows), half), jnp.bfloat16)] * 2,
        6 * padded(rows) * hidden * width,
    )
    return outs[:pairs], outs[pairs:]


def run_expert_in_stages(place, own, across, swap, weights, n_experts):
    gate, up, down_mine, down_theirs = weights
    width, hidden = gate.shape
    half = width // 2
    rows, n_blocks = sum(a.shape[0] for a in own), len(own)
    first = own[0].shape[0]
    products = [in_vmem((padded(rows), hidden), jnp.float32)] * 2
    outs = [in_vmem((first, half)), in_vmem((rows - first, half))]
    x = [pltpu.VMEM((padded(rows), half), jnp.bfloat16)]
    flops = 2 * padded(rows) * hidden * width
    gated, lifted = call(functools.partial(first_kernel, n_blocks), place, (*own, gate, up), products, x, flops)
    units, *theirs = call(
        functools.partial(second_kernel, n_blocks, n_experts),
        place,
        (*own, *across, gated, lifted, gate, up, down_theirs),
        [in_vmem((padded(rows), hidden)), *outs],
        x,
        flops + flops // 2,
    )
    theirs = [swap(a) for a in theirs]
    mine = call(
        functools.partial(third_kernel, n_blocks, n_experts),
        place,
        (*own, units, down_mine),
        outs,
        [],
        flops // 2,
    )
    return mine, theirs


def ring_body(tokens, expert_ids, gate_probs, w_gate, w_up, w_down):
    n = lax.axis_size("ep")
    rows = tokens.shape[0]
    order = list(range(0, n, 2)) + list(range(n - 1, 0, -2))
    ahead = [(order[i], order[(i + 1) % n]) for i in range(n)]
    back = [(b, a) for a, b in ahead]
    swap = functools.partial(lax.ppermute, axis_name="tp", perm=[(0, 1), (1, 0)])
    far = n // 2
    place = jnp.stack([lax.axis_index("tp"), lax.axis_index("ep")]).astype(jnp.int32)
    packed = pack(tokens, expert_ids, gate_probs, n)
    gate, up = turn_weights(after(place, packed), w_gate[0].T, w_up[0].T)

    came, across, value = {0: packed}, {}, {}

    def run(keys, wait_for=None):
        at = place if wait_for is None else after(place, wait_for)
        mine, theirs = run_expert(at, [came[k] for k in keys], [across[k] for k in keys], weights, n)
        return [(keys[2 * i : 2 * i + 2], *pair) for i, pair in enumerate(zip(mine, theirs))]

    def keep(keys, mine, theirs):
        pairs = ((mine, theirs), lax.optimization_barrier((mine, theirs)))
        start = 0
        for i, k in enumerate(keys):
            mine, theirs = pairs[i % 2]
            span = slice(start, start + came[k].shape[0])
            start = span.stop
            value[k] = mine[span].astype(jnp.float32) + theirs[span].astype(jnp.float32)

    across[0] = swap(packed)
    weights, done, near = [gate, up], up, []
    for k in range(1, far + 1):
        came[k - 1] = after(came[k - 1], done) if k > 1 else packed
        if k < far - 1:
            came[k] = lax.ppermute(came[k - 1], "ep", ahead)
        if k != far - 1:
            j = min(k, far - 1)
            came[1 - j] = after(came[1 - j], done if k < far else (done, came[k - 1])) if k > 1 else packed
            came[-j] = lax.ppermute(came[1 - j], "ep", back)
        if k >= far - 1:
            came[k] = lax.ppermute(came[k - 1], "ep", ahead)
        if k > 1:
            across[k - 1] = swap(came[k - 1])
        if 1 < k < far:
            across[1 - k] = swap(came[1 - k])
        if k == 2:
            weights += halve_weights(after(place, came[1]), w_down[0])
            done = weights[-1]
        elif k > 2:
            near += run([k - 2, 2 - k], across[0] if k == 3 else None)
            done = near[-1][-1]
    last = [far, 1 - far]
    for k in last:
        came[k] = after(came[k], done)
        across[k] = swap(came[k])
    mine, theirs = run_expert_in_stages(place, [came[k] for k in last], [across[k] for k in last], swap, weights, n)
    for k, m, t in zip(last, mine, theirs):
        keep([k], m, t)
    for keys, m, t in near:
        keep(keys, m, swap(after(t, value[far])))

    to_ahead, to_back = value[far].astype(jnp.bfloat16), None
    for k in range(far - 1, -1, -1):
        behind = lax.ppermute(to_ahead, "ep", ahead).astype(jnp.float32)
        front = 0.0 if to_back is None else lax.ppermute(to_back, "ep", back).astype(jnp.float32)
        done = None
        if k == far - 1:
            ((keys, mine, done),) = run([k, 0], to_ahead)
            keep(keys, mine, swap(done))
        if k:
            to_ahead = (value[-k] + behind).astype(jnp.bfloat16)
            to_back = (value[k] + front).astype(jnp.bfloat16)
        if done is not None:
            to_ahead, to_back = after(to_ahead, done), after(to_back, done)
    return (value[0] + behind + front).astype(jnp.bfloat16)


def swiglu_expert(rows, gate_part, up_part, down_part):
    gated = jnp.dot(rows, gate_part, preferred_element_type=jnp.float32)
    lifted = jnp.dot(rows, up_part, preferred_element_type=jnp.float32)
    hidden = (jax.nn.silu(gated) * lifted).astype(jnp.bfloat16)
    return jnp.dot(hidden, down_part, preferred_element_type=jnp.float32)


def slot_table(expert_ids, n_experts):
    routed = expert_ids.reshape(-1)
    pair_count = routed.shape[0]
    onehot = (routed[:, None] == jnp.arange(n_experts, dtype=jnp.int32)[None, :]).astype(
        jnp.bfloat16
    )
    row_index = lax.broadcasted_iota(jnp.int32, (pair_count, pair_count), 0)
    col_index = lax.broadcasted_iota(jnp.int32, (pair_count, pair_count), 1)
    earlier = (row_index > col_index).astype(jnp.bfloat16)
    before = jnp.dot(earlier, onehot, preferred_element_type=jnp.float32)
    slots = jnp.sum(before * onehot.astype(jnp.float32), axis=1).astype(jnp.int32)
    return (routed, slots)


def slot_body(tokens, expert_ids, gate_probs, w_gate, w_up, w_down):
    n_experts = lax.axis_size("ep")
    tok_rows, top_count = expert_ids.shape
    capacity = 3 * tok_rows * top_count // (2 * n_experts)
    routed, slots = slot_table(expert_ids, n_experts)
    positions = routed * capacity + slots
    pair_token = jnp.repeat(jnp.arange(tok_rows, dtype=jnp.int32), top_count)
    buffer_rows = n_experts * capacity
    owners = jnp.full((buffer_rows,), tok_rows, jnp.int32).at[positions].set(pair_token)
    half_slots = capacity // 2
    whole_tokens = lax.all_gather(tokens, "tp", axis=1, tiled=True)
    width = whole_tokens.shape[1]
    gate_full, up_full = (
        lax.all_gather(w_gate, "tp", axis=2, tiled=True),
        lax.all_gather(w_up, "tp", axis=2, tiled=True),
    )
    down_full = lax.all_gather(w_down, "tp", axis=1, tiled=True)
    padded = jnp.concatenate([whole_tokens, jnp.zeros((1, width), whole_tokens.dtype)], 0)
    outgoing = padded[owners].reshape(n_experts, capacity, width)
    lane = lax.axis_index("tp")
    mine = lax.dynamic_slice_in_dim(outgoing, lane * half_slots, half_slots, 1)
    block = lax.all_to_all(mine, "ep", split_axis=0, concat_axis=0, tiled=True)
    sources, items, columns = block.shape
    result = swiglu_expert(
        block.reshape(sources * items, columns), gate_full[0], up_full[0], down_full[0]
    )
    result = result.astype(jnp.bfloat16).reshape(sources, items, columns)
    returned = lax.all_to_all(result, "ep", split_axis=0, concat_axis=0, tiled=True)
    received = returned.reshape(n_experts * half_slots, width)
    in_half = slots // half_slots == lane
    local_pos = routed * half_slots + slots % half_slots
    picked = received[local_pos].astype(jnp.float32).reshape(tok_rows, top_count, width)
    weighted = jnp.where(in_half.reshape(tok_rows, top_count), gate_probs, 0.0)
    partial_value = jnp.sum(weighted[:, :, None] * picked, axis=1)
    return lax.psum_scatter(partial_value, "tp", scatter_dimension=1, tiled=True).astype(
        jnp.bfloat16
    )


def solution(mesh):
    in_specs = (
        P(("groups", "ep"), "tp"),
        P(("groups", "ep"), None),
        P(("groups", "ep"), None),
        P("ep", None, "tp"),
        P("ep", None, "tp"),
        P("ep", "tp", None),
    )
    out_specs = P(("groups", "ep"), "tp")

    def body(tokens, expert_ids, *rest):
        n, top = lax.axis_size("ep"), expert_ids.shape[1]
        small = n <= 4 * top and n % 2 == 0 and n >= 6 and lax.axis_size("tp") == 2
        return (ring_body if small else slot_body)(tokens, expert_ids, *rest)

    return jax.shard_map(body, mesh=mesh, in_specs=in_specs, out_specs=out_specs, check_vma=False)
```

```python
import functools

import jax
import jax.numpy as jnp
from jax import lax
from jax.experimental import pallas as pl
from jax.experimental.pallas import tpu as pltpu
from jax.sharding import PartitionSpec as P

SPLITS = 3


def in_vmem(shape, dtype=jnp.bfloat16):
    return pltpu.MemorySpace.VMEM(shape, dtype)


def hold(x):
    return pltpu.with_memory_space_constraint(x, pltpu.VMEM)


def after(x, done):
    return lax.optimization_barrier((x, done))[0]


def pack_kernel(n_experts, tokens_in, ids_in, probs_in, packed, tokens, ids, probs, sems):
    copies = [
        pltpu.make_async_copy(src, dst, sems.at[i])
        for i, (src, dst) in enumerate(((ids_in, ids), (probs_in, probs), (tokens_in, tokens)))
    ]
    for copy in copies:
        copy.start()
    top, rows = ids.shape
    half = tokens.shape[1]
    copies[0].wait()
    copies[1].wait()
    expert = lax.broadcasted_iota(jnp.int32, (n_experts, rows), 0)
    rest = jnp.zeros((n_experts, rows), jnp.float32)
    for k in range(top):
        rest += jnp.where(ids[k : k + 1, :] == expert, probs[k : k + 1, :], 0.0)
    terms = []
    for _ in range(SPLITS):
        term = rest.astype(jnp.bfloat16).astype(jnp.float32)
        terms.append(term)
        rest = rest - term
    packed[:, half:] = jnp.concatenate(terms, axis=0).T.astype(jnp.bfloat16)
    copies[2].wait()
    packed[:, :half] = tokens[...]


def pack(tokens, expert_ids, gate_probs, n_experts):
    rows, half = tokens.shape
    args = (tokens, expert_ids.T, gate_probs.T)
    return pl.pallas_call(
        functools.partial(pack_kernel, n_experts),
        out_shape=in_vmem((rows, half + SPLITS * n_experts)),
        in_specs=[pl.BlockSpec(memory_space=pltpu.HBM)] * 3,
        out_specs=pl.BlockSpec(memory_space=pltpu.VMEM),
        scratch_shapes=[pltpu.VMEM(a.shape, a.dtype) for a in args] + [pltpu.SemaphoreType.DMA((3,))],
        compiler_params=pltpu.CompilerParams(vmem_limit_bytes=8 << 20),
    )(*[pltpu.with_memory_space_constraint(a, pltpu.HBM) for a in args])


def pieces(hidden):
    first = -(-hidden // 256) * 128
    return ((0, first), (first, hidden))


def turn_kernel(after_this, gate_in, up_in, gate, up, gate_buf, up_buf, sems):
    steps = []
    for i, (src, buf, out) in enumerate(((gate_in, gate_buf, gate), (up_in, up_buf, up))):
        for j, (start, stop) in enumerate(pieces(src.shape[0])):
            span = pl.ds(start, stop - start)
            steps.append((pltpu.make_async_copy(src.at[span], buf.at[span], sems.at[i, j]), buf, out, start, stop))
    for copy, *_ in steps:
        copy.start()
    for copy, buf, out, start, stop in steps:
        copy.wait()
        out[:, start:stop] = buf[start:stop, :].T


def turn_weights(after_this, *weights):
    hidden, width = weights[0].shape
    return pl.pallas_call(
        turn_kernel,
        out_shape=[in_vmem((width, hidden))] * 2,
        in_specs=[pl.BlockSpec(memory_space=pltpu.SMEM)] + [pl.BlockSpec(memory_space=pltpu.HBM)] * 2,
        out_specs=[pl.BlockSpec(memory_space=pltpu.VMEM)] * 2,
        scratch_shapes=[pltpu.VMEM((hidden, width), jnp.bfloat16)] * 2 + [pltpu.SemaphoreType.DMA((2, 2))],
        compiler_params=pltpu.CompilerParams(vmem_limit_bytes=32 << 20),
        cost_estimate=pl.CostEstimate(flops=0, bytes_accessed=8 * hidden * width, transcendentals=0),
    )(after_this, *[pltpu.with_memory_space_constraint(w, pltpu.HBM) for w in weights])


def halve_kernel(place, down_in, down_mine, down_theirs, down_buf, sems):
    lane = place[0]
    half = down_mine.shape[1]
    spans = [slice(start, stop) for start, stop in pieces(down_in.shape[0])]
    copies = [
        pltpu.make_async_copy(down_in.at[pl.ds(s.start, s.stop - s.start)], down_buf.at[pl.ds(s.start, s.stop - s.start)], sems.at[i])
        for i, s in enumerate(spans)
    ]
    for copy in copies:
        copy.start()
    for copy, s in zip(copies, spans):
        copy.wait()

        @pl.when(lane == 0)
        def _():
            down_mine[s, :] = down_buf[s, :half]
            down_theirs[s, :] = down_buf[s, half:]

        @pl.when(lane != 0)
        def _():
            down_mine[s, :] = down_buf[s, half:]
            down_theirs[s, :] = down_buf[s, :half]


def halve_weights(place, w_down):
    hidden, width = w_down.shape
    return pl.pallas_call(
        halve_kernel,
        out_shape=[in_vmem((hidden, width // 2))] * 2,
        in_specs=[pl.BlockSpec(memory_space=pltpu.SMEM), pl.BlockSpec(memory_space=pltpu.HBM)],
        out_specs=[pl.BlockSpec(memory_space=pltpu.VMEM)] * 2,
        scratch_shapes=[pltpu.VMEM((hidden, width), jnp.bfloat16), pltpu.SemaphoreType.DMA((2,))],
        compiler_params=pltpu.CompilerParams(vmem_limit_bytes=32 << 20),
        cost_estimate=pl.CostEstimate(flops=0, bytes_accessed=8 * hidden * width, transcendentals=0),
    )(place, pltpu.with_memory_space_constraint(w_down, pltpu.HBM))


def gather_rows(blocks, x, width):
    start = 0
    for block in blocks:
        x[start : start + block.shape[0], :] = block[:, :width]
        start += block.shape[0]
    if start < x.shape[0]:
        x[start:, :] = jnp.zeros((x.shape[0] - start, width), x.dtype)


def project(x, lane, w):
    half = x.shape[1]
    return jnp.dot(x[...], w[pl.ds(pl.multiple_of(lane * half, 16), half), :], preferred_element_type=jnp.float32)


def activate(gated, lifted):
    return (gated / (1.0 + jnp.exp(-gated)) * lifted).astype(jnp.bfloat16)


def gate_weights(blocks, half, expert, n_experts):
    weights = []
    for block in blocks:
        terms = block[:, half:].astype(jnp.float32)
        column = lax.broadcasted_iota(jnp.int32, terms.shape, 1)
        weights.append(jnp.sum(jnp.where(lax.rem(column, n_experts) == expert, terms, 0.0), axis=1, keepdims=True))
    return weights


def lower(hidden, w, weights, *outs):
    value = jnp.dot(hidden, w[...], preferred_element_type=jnp.float32)
    places = [(out, at) for out in outs for at in range(0, out.shape[0], weights[0].shape[0])]
    start = 0
    for weight, (out, at) in zip(weights, places):
        rows = weight.shape[0]
        out[at : at + rows] = (value[start : start + rows] * weight).astype(jnp.bfloat16)
        start += rows


def expert_kernel(n_blocks, n_experts, place, *refs):
    own, across = refs[:n_blocks], refs[n_blocks : 2 * n_blocks]
    w_gate, w_up, down_mine, down_theirs, *outs, x_own, x_across = refs[2 * n_blocks :]
    lane, expert = place[0], place[1]
    half = x_own.shape[1]
    gather_rows(own, x_own, half)
    gather_rows(across, x_across, half)
    gated = project(x_own, lane, w_gate) + project(x_across, 1 - lane, w_gate)
    lifted = project(x_own, lane, w_up) + project(x_across, 1 - lane, w_up)
    hidden = activate(gated, lifted)
    weights = gate_weights(own, half, expert, n_experts)
    mine, theirs = outs[: len(outs) // 2], outs[len(outs) // 2 :]
    lower(hidden, down_theirs, weights, *theirs)
    lower(hidden, down_mine, weights, *mine)


def first_kernel(n_blocks, place, *refs):
    own = refs[:n_blocks]
    w_gate, w_up, gated, lifted, x = refs[n_blocks:]
    gather_rows(own, x, x.shape[1])
    gated[...] = project(x, place[0], w_gate)
    lifted[...] = project(x, place[0], w_up)


def second_kernel(n_blocks, n_experts, place, *refs):
    own, across = refs[:n_blocks], refs[n_blocks : 2 * n_blocks]
    gated, lifted, w_gate, w_up, down_theirs, hidden, *theirs, x = refs[2 * n_blocks :]
    half = x.shape[1]
    gather_rows(across, x, half)
    there = 1 - place[0]
    hidden[...] = activate(gated[...] + project(x, there, w_gate), lifted[...] + project(x, there, w_up))
    lower(hidden[...], down_theirs, gate_weights(own, half, place[1], n_experts), *theirs)


def third_kernel(n_blocks, n_experts, place, *refs):
    own = refs[:n_blocks]
    hidden, down_mine, *mine = refs[n_blocks:]
    lower(hidden[...], down_mine, gate_weights(own, mine[0].shape[1], place[1], n_experts), *mine)


def call(kernel, place, args, out_shape, scratch_shapes, flops):
    vmem = pl.BlockSpec(memory_space=pltpu.VMEM)
    return pl.pallas_call(
        kernel,
        out_shape=out_shape,
        in_specs=[pl.BlockSpec(memory_space=pltpu.SMEM)] + [vmem] * len(args),
        out_specs=[vmem] * len(out_shape),
        scratch_shapes=scratch_shapes,
        compiler_params=pltpu.CompilerParams(vmem_limit_bytes=16 << 20),
        cost_estimate=pl.CostEstimate(flops=flops, bytes_accessed=flops // 128, transcendentals=0),
    )(place, *[hold(a) for a in args])


def padded(rows):
    return max(rows, 128)


def run_expert(place, own, across, weights, n_experts):
    width, hidden = weights[0].shape
    half = width // 2
    rows, pairs = sum(a.shape[0] for a in own), max(1, len(own) // 2)
    outs = call(
        functools.partial(expert_kernel, len(own), n_experts),
        place,
        (*own, *across, *weights),
        [in_vmem((rows // pairs, half))] * (2 * pairs),
        [pltpu.VMEM((padded(rows), half), jnp.bfloat16)] * 2,
        6 * padded(rows) * hidden * width,
    )
    return outs[:pairs], outs[pairs:]


def run_expert_in_stages(place, own, across, swap, weights, n_experts):
    gate, up, down_mine, down_theirs = weights
    width, hidden = gate.shape
    half = width // 2
    rows, n_blocks = sum(a.shape[0] for a in own), len(own)
    first = own[0].shape[0]
    products = [in_vmem((padded(rows), hidden), jnp.float32)] * 2
    outs = [in_vmem((first, half)), in_vmem((rows - first, half))]
    x = [pltpu.VMEM((padded(rows), half), jnp.bfloat16)]
    flops = 2 * padded(rows) * hidden * width
    gated, lifted = call(functools.partial(first_kernel, n_blocks), place, (*own, gate, up), products, x, flops)
    units, *theirs = call(
        functools.partial(second_kernel, n_blocks, n_experts),
        place,
        (*own, *across, gated, lifted, gate, up, down_theirs),
        [in_vmem((padded(rows), hidden)), *outs],
        x,
        flops + flops // 2,
    )
    theirs = [swap(a) for a in theirs]
    mine = call(
        functools.partial(third_kernel, n_blocks, n_experts),
        place,
        (*own, units, down_mine),
        outs,
        [],
        flops // 2,
    )
    return mine, theirs


def add_kernel(*refs):
    *terms, out = refs
    out[...] = sum(t[...].astype(jnp.float32) for t in terms).astype(out.dtype)


def add(*terms):
    vmem = pl.BlockSpec(memory_space=pltpu.VMEM)
    return pl.pallas_call(
        add_kernel,
        out_shape=in_vmem(terms[0].shape),
        in_specs=[vmem] * len(terms),
        out_specs=vmem,
        cost_estimate=pl.CostEstimate(flops=0, bytes_accessed=12 << 20, transcendentals=0),
    )(*[hold(t) for t in terms])


def ring_body(tokens, expert_ids, gate_probs, w_gate, w_up, w_down):
    n = lax.axis_size("ep")
    rows = tokens.shape[0]
    order = list(range(0, n, 2)) + list(range(n - 1, 0, -2))
    ahead = [(order[i], order[(i + 1) % n]) for i in range(n)]
    back = [(b, a) for a, b in ahead]
    swap = functools.partial(lax.ppermute, axis_name="tp", perm=[(0, 1), (1, 0)])
    far = n // 2
    place = jnp.stack([lax.axis_index("tp"), lax.axis_index("ep")]).astype(jnp.int32)
    packed = pack(tokens, expert_ids, gate_probs, n)
    gate, up = turn_weights(after(place, packed), w_gate[0].T, w_up[0].T)

    came, across, value, parts = {0: packed}, {}, {}, {}

    def run(keys, wait_for=None):
        at = place if wait_for is None else after(place, wait_for)
        mine, theirs = run_expert(at, [came[k] for k in keys], [across[k] for k in keys], weights, n)
        return [(keys[2 * i : 2 * i + 2], *pair) for i, pair in enumerate(zip(mine, theirs))]

    def keep(keys, mine, theirs):
        pairs = ((mine, theirs), lax.optimization_barrier((mine, theirs)))
        start = 0
        for i, k in enumerate(keys):
            mine, theirs = pairs[i % 2]
            span = slice(start, start + came[k].shape[0])
            start = span.stop
            parts[k] = mine[span], theirs[span]
            value[k] = mine[span].astype(jnp.float32) + theirs[span].astype(jnp.float32)

    came[1] = lax.ppermute(packed, "ep", ahead)
    came[-1] = lax.ppermute(packed, "ep", back)
    across[0] = swap(packed)
    weights, done, near = [gate, up], up, []
    for k in range(2, far + 1):
        came[k - 1], came[1 - k] = after(came[k - 1], done), after(came[1 - k], done)
        came[k] = lax.ppermute(came[k - 1], "ep", ahead)
        if k < far:
            came[-k] = lax.ppermute(came[1 - k], "ep", back)
        across[k - 1], across[1 - k] = swap(came[k - 1]), swap(came[1 - k])
        if k == 2:
            weights += halve_weights(after(place, came[1]), w_down[0])
            done = weights[-1]
        else:
            near += run([k - 2, 2 - k], across[0] if k == 3 else None)
            done = near[-1][-1]
    came[far] = after(came[far], done)
    across[far] = swap(came[far])
    last = [far, far - 1, 1 - far]
    for keys, mine, theirs in zip(([far], last[1:]), *run_expert_in_stages(place, [came[k] for k in last], [across[k] for k in last], swap, weights, n)):
        keep(keys, mine, theirs)
    for keys, mine, theirs in near:
        keep(keys, mine, swap(after(theirs, value[far])))

    to_ahead = value[far].astype(jnp.bfloat16)
    to_back = (value[far - 1]).astype(jnp.bfloat16)
    for k in range(far - 1, -1, -1):
        behind = lax.ppermute(to_ahead, "ep", ahead)
        if k == far - 1:
            ((keys, mine, done),) = run([0], to_ahead)
            keep(keys, mine, swap(done))
        else:
            to_back = done = add(*parts[k], after(front, to_ahead))
        if k:
            front = lax.ppermute(to_back, "ep", back)
            to_ahead = (value[-k] + after(behind, done).astype(jnp.float32)).astype(jnp.bfloat16)
    return (to_back.astype(jnp.float32) + behind.astype(jnp.float32)).astype(jnp.bfloat16)


def swiglu_expert(rows, gate_part, up_part, down_part):
    gated = jnp.dot(rows, gate_part, preferred_element_type=jnp.float32)
    lifted = jnp.dot(rows, up_part, preferred_element_type=jnp.float32)
    hidden = (jax.nn.silu(gated) * lifted).astype(jnp.bfloat16)
    return jnp.dot(hidden, down_part, preferred_element_type=jnp.float32)


def slot_table(expert_ids, n_experts):
    routed = expert_ids.reshape(-1)
    pair_count = routed.shape[0]
    onehot = (routed[:, None] == jnp.arange(n_experts, dtype=jnp.int32)[None, :]).astype(
        jnp.bfloat16
    )
    row_index = lax.broadcasted_iota(jnp.int32, (pair_count, pair_count), 0)
    col_index = lax.broadcasted_iota(jnp.int32, (pair_count, pair_count), 1)
    earlier = (row_index > col_index).astype(jnp.bfloat16)
    before = jnp.dot(earlier, onehot, preferred_element_type=jnp.float32)
    slots = jnp.sum(before * onehot.astype(jnp.float32), axis=1).astype(jnp.int32)
    return (routed, slots)


def slot_body(tokens, expert_ids, gate_probs, w_gate, w_up, w_down):
    n_experts = lax.axis_size("ep")
    tok_rows, top_count = expert_ids.shape
    capacity = 3 * tok_rows * top_count // (2 * n_experts)
    routed, slots = slot_table(expert_ids, n_experts)
    positions = routed * capacity + slots
    pair_token = jnp.repeat(jnp.arange(tok_rows, dtype=jnp.int32), top_count)
    buffer_rows = n_experts * capacity
    owners = jnp.full((buffer_rows,), tok_rows, jnp.int32).at[positions].set(pair_token)
    half_slots = capacity // 2
    whole_tokens = lax.all_gather(tokens, "tp", axis=1, tiled=True)
    width = whole_tokens.shape[1]
    gate_full, up_full = (
        lax.all_gather(w_gate, "tp", axis=2, tiled=True),
        lax.all_gather(w_up, "tp", axis=2, tiled=True),
    )
    down_full = lax.all_gather(w_down, "tp", axis=1, tiled=True)
    padded = jnp.concatenate([whole_tokens, jnp.zeros((1, width), whole_tokens.dtype)], 0)
    outgoing = padded[owners].reshape(n_experts, capacity, width)
    lane = lax.axis_index("tp")
    mine = lax.dynamic_slice_in_dim(outgoing, lane * half_slots, half_slots, 1)
    block = lax.all_to_all(mine, "ep", split_axis=0, concat_axis=0, tiled=True)
    sources, items, columns = block.shape
    result = swiglu_expert(
        block.reshape(sources * items, columns), gate_full[0], up_full[0], down_full[0]
    )
    result = result.astype(jnp.bfloat16).reshape(sources, items, columns)
    returned = lax.all_to_all(result, "ep", split_axis=0, concat_axis=0, tiled=True)
    received = returned.reshape(n_experts * half_slots, width)
    in_half = slots // half_slots == lane
    local_pos = routed * half_slots + slots % half_slots
    picked = received[local_pos].astype(jnp.float32).reshape(tok_rows, top_count, width)
    weighted = jnp.where(in_half.reshape(tok_rows, top_count), gate_probs, 0.0)
    partial_value = jnp.sum(weighted[:, :, None] * picked, axis=1)
    return lax.psum_scatter(partial_value, "tp", scatter_dimension=1, tiled=True).astype(
        jnp.bfloat16
    )


def solution(mesh):
    in_specs = (
        P(("groups", "ep"), "tp"),
        P(("groups", "ep"), None),
        P(("groups", "ep"), None),
        P("ep", None, "tp"),
        P("ep", None, "tp"),
        P("ep", "tp", None),
    )
    out_specs = P(("groups", "ep"), "tp")

    def body(tokens, expert_ids, *rest):
        n, top = lax.axis_size("ep"), expert_ids.shape[1]
        small = n <= 4 * top and n % 2 == 0 and n >= 6 and lax.axis_size("tp") == 2
        return (ring_body if small else slot_body)(tokens, expert_ids, *rest)

    return jax.shard_map(body, mesh=mesh, in_specs=in_specs, out_specs=out_specs, check_vma=False)
```

```python
import functools

import jax
import jax.numpy as jnp
from jax import lax
from jax.experimental import pallas as pl
from jax.experimental.pallas import tpu as pltpu
from jax.sharding import PartitionSpec as P

SPLITS = 3


def in_vmem(shape, dtype=jnp.bfloat16):
    return pltpu.MemorySpace.VMEM(shape, dtype)


def hold(x):
    return pltpu.with_memory_space_constraint(x, pltpu.VMEM)


def after(x, done):
    return lax.optimization_barrier((x, done))[0]


def pack_kernel(n_experts, tokens_in, ids_in, probs_in, packed, tokens, ids, probs, sems):
    copies = [
        pltpu.make_async_copy(src, dst, sems.at[i])
        for i, (src, dst) in enumerate(((ids_in, ids), (probs_in, probs), (tokens_in, tokens)))
    ]
    for copy in copies:
        copy.start()
    top, rows = ids.shape
    half = tokens.shape[1]
    copies[0].wait()
    copies[1].wait()
    expert = lax.broadcasted_iota(jnp.int32, (n_experts, rows), 0)
    rest = jnp.zeros((n_experts, rows), jnp.float32)
    for k in range(top):
        rest += jnp.where(ids[k : k + 1, :] == expert, probs[k : k + 1, :], 0.0)
    terms = []
    for _ in range(SPLITS):
        term = rest.astype(jnp.bfloat16).astype(jnp.float32)
        terms.append(term)
        rest = rest - term
    packed[:, half:] = jnp.concatenate(terms, axis=0).T.astype(jnp.bfloat16)
    copies[2].wait()
    packed[:, :half] = tokens[...]


def pack(tokens, expert_ids, gate_probs, n_experts):
    rows, half = tokens.shape
    args = (tokens, expert_ids.T, gate_probs.T)
    return pl.pallas_call(
        functools.partial(pack_kernel, n_experts),
        out_shape=in_vmem((rows, half + SPLITS * n_experts)),
        in_specs=[pl.BlockSpec(memory_space=pltpu.HBM)] * 3,
        out_specs=pl.BlockSpec(memory_space=pltpu.VMEM),
        scratch_shapes=[pltpu.VMEM(a.shape, a.dtype) for a in args] + [pltpu.SemaphoreType.DMA((3,))],
        compiler_params=pltpu.CompilerParams(vmem_limit_bytes=8 << 20),
    )(*[pltpu.with_memory_space_constraint(a, pltpu.HBM) for a in args])


def pieces(hidden):
    first = -(-hidden // 256) * 128
    return ((0, first), (first, hidden))


def turn_kernel(after_this, gate_in, up_in, gate, up, gate_buf, up_buf, sems):
    steps = []
    for i, (src, buf, out) in enumerate(((gate_in, gate_buf, gate), (up_in, up_buf, up))):
        for j, (start, stop) in enumerate(pieces(src.shape[0])):
            span = pl.ds(start, stop - start)
            steps.append((pltpu.make_async_copy(src.at[span], buf.at[span], sems.at[i, j]), buf, out, start, stop))
    for copy, *_ in steps:
        copy.start()
    for copy, buf, out, start, stop in steps:
        copy.wait()
        out[:, start:stop] = buf[start:stop, :].T


def turn_weights(after_this, *weights):
    hidden, width = weights[0].shape
    return pl.pallas_call(
        turn_kernel,
        out_shape=[in_vmem((width, hidden))] * 2,
        in_specs=[pl.BlockSpec(memory_space=pltpu.SMEM)] + [pl.BlockSpec(memory_space=pltpu.HBM)] * 2,
        out_specs=[pl.BlockSpec(memory_space=pltpu.VMEM)] * 2,
        scratch_shapes=[pltpu.VMEM((hidden, width), jnp.bfloat16)] * 2 + [pltpu.SemaphoreType.DMA((2, 2))],
        compiler_params=pltpu.CompilerParams(vmem_limit_bytes=32 << 20),
        cost_estimate=pl.CostEstimate(flops=0, bytes_accessed=8 * hidden * width, transcendentals=0),
    )(after_this, *[pltpu.with_memory_space_constraint(w, pltpu.HBM) for w in weights])


def halve_kernel(place, down_in, down_mine, down_theirs, down_buf, sems):
    lane = place[0]
    half = down_mine.shape[1]
    spans = [slice(start, stop) for start, stop in pieces(down_in.shape[0])]
    copies = [
        pltpu.make_async_copy(down_in.at[pl.ds(s.start, s.stop - s.start)], down_buf.at[pl.ds(s.start, s.stop - s.start)], sems.at[i])
        for i, s in enumerate(spans)
    ]
    for copy in copies:
        copy.start()
    for copy, s in zip(copies, spans):
        copy.wait()

        @pl.when(lane == 0)
        def _():
            down_mine[s, :] = down_buf[s, :half]
            down_theirs[s, :] = down_buf[s, half:]

        @pl.when(lane != 0)
        def _():
            down_mine[s, :] = down_buf[s, half:]
            down_theirs[s, :] = down_buf[s, :half]


def halve_weights(place, w_down):
    hidden, width = w_down.shape
    return pl.pallas_call(
        halve_kernel,
        out_shape=[in_vmem((hidden, width // 2))] * 2,
        in_specs=[pl.BlockSpec(memory_space=pltpu.SMEM), pl.BlockSpec(memory_space=pltpu.HBM)],
        out_specs=[pl.BlockSpec(memory_space=pltpu.VMEM)] * 2,
        scratch_shapes=[pltpu.VMEM((hidden, width), jnp.bfloat16), pltpu.SemaphoreType.DMA((2,))],
        compiler_params=pltpu.CompilerParams(vmem_limit_bytes=32 << 20),
        cost_estimate=pl.CostEstimate(flops=0, bytes_accessed=8 * hidden * width, transcendentals=0),
    )(place, pltpu.with_memory_space_constraint(w_down, pltpu.HBM))


def gather_rows(blocks, x, width):
    start = 0
    for block in blocks:
        x[start : start + block.shape[0], :] = block[:, :width]
        start += block.shape[0]
    if start < x.shape[0]:
        x[start:, :] = jnp.zeros((x.shape[0] - start, width), x.dtype)


def project(x, lane, w):
    half = x.shape[1]
    return jnp.dot(x[...], w[pl.ds(pl.multiple_of(lane * half, 16), half), :], preferred_element_type=jnp.float32)


def activate(gated, lifted):
    return (gated / (1.0 + jnp.exp(-gated)) * lifted).astype(jnp.bfloat16)


def gate_weights(blocks, half, expert, n_experts):
    weights = []
    for block in blocks:
        terms = block[:, half:].astype(jnp.float32)
        column = lax.broadcasted_iota(jnp.int32, terms.shape, 1)
        weights.append(jnp.sum(jnp.where(lax.rem(column, n_experts) == expert, terms, 0.0), axis=1, keepdims=True))
    return weights


def lower(hidden, w, weights, *outs):
    value = jnp.dot(hidden, w[...], preferred_element_type=jnp.float32)
    places = [(out, at) for out in outs for at in range(0, out.shape[0], weights[0].shape[0])]
    start = 0
    for weight, (out, at) in zip(weights, places):
        rows = weight.shape[0]
        out[at : at + rows] = (value[start : start + rows] * weight).astype(jnp.bfloat16)
        start += rows


def expert_kernel(n_blocks, n_experts, place, *refs):
    own, across = refs[:n_blocks], refs[n_blocks : 2 * n_blocks]
    w_gate, w_up, down_mine, down_theirs, *outs, x_own, x_across = refs[2 * n_blocks :]
    lane, expert = place[0], place[1]
    half = x_own.shape[1]
    gather_rows(own, x_own, half)
    gather_rows(across, x_across, half)
    gated = project(x_own, lane, w_gate) + project(x_across, 1 - lane, w_gate)
    lifted = project(x_own, lane, w_up) + project(x_across, 1 - lane, w_up)
    hidden = activate(gated, lifted)
    weights = gate_weights(own, half, expert, n_experts)
    mine, theirs = outs[: len(outs) // 2], outs[len(outs) // 2 :]
    lower(hidden, down_theirs, weights, *theirs)
    lower(hidden, down_mine, weights, *mine)


def first_kernel(n_blocks, place, *refs):
    own = refs[:n_blocks]
    w_gate, w_up, gated, lifted, x = refs[n_blocks:]
    gather_rows(own, x, x.shape[1])
    gated[...] = project(x, place[0], w_gate)
    lifted[...] = project(x, place[0], w_up)


def second_kernel(n_blocks, n_experts, place, *refs):
    own, across = refs[:n_blocks], refs[n_blocks : 2 * n_blocks]
    gated, lifted, w_gate, w_up, down_theirs, hidden, *theirs, x = refs[2 * n_blocks :]
    half = x.shape[1]
    gather_rows(across, x, half)
    there = 1 - place[0]
    hidden[...] = activate(gated[...] + project(x, there, w_gate), lifted[...] + project(x, there, w_up))
    lower(hidden[...], down_theirs, gate_weights(own, half, place[1], n_experts), *theirs)


def third_kernel(n_blocks, n_experts, place, *refs):
    own = refs[:n_blocks]
    hidden, down_mine, *mine = refs[n_blocks:]
    lower(hidden[...], down_mine, gate_weights(own, mine[0].shape[1], place[1], n_experts), *mine)


def call(kernel, place, args, out_shape, scratch_shapes, flops):
    vmem = pl.BlockSpec(memory_space=pltpu.VMEM)
    return pl.pallas_call(
        kernel,
        out_shape=out_shape,
        in_specs=[pl.BlockSpec(memory_space=pltpu.SMEM)] + [vmem] * len(args),
        out_specs=[vmem] * len(out_shape),
        scratch_shapes=scratch_shapes,
        compiler_params=pltpu.CompilerParams(vmem_limit_bytes=16 << 20),
        cost_estimate=pl.CostEstimate(flops=flops, bytes_accessed=flops // 128, transcendentals=0),
    )(place, *[hold(a) for a in args])


def padded(rows):
    return max(rows, 128)


def run_expert(place, own, across, weights, n_experts):
    width, hidden = weights[0].shape
    half = width // 2
    rows, pairs = sum(a.shape[0] for a in own), max(1, len(own) // 2)
    outs = call(
        functools.partial(expert_kernel, len(own), n_experts),
        place,
        (*own, *across, *weights),
        [in_vmem((rows // pairs, half))] * (2 * pairs),
        [pltpu.VMEM((padded(rows), half), jnp.bfloat16)] * 2,
        6 * padded(rows) * hidden * width,
    )
    return outs[:pairs], outs[pairs:]


def run_expert_in_stages(place, own, across, swap, weights, n_experts, last_place):
    gate, up, down_mine, down_theirs = weights
    width, hidden = gate.shape
    half = width // 2
    rows, n_blocks = sum(a.shape[0] for a in own), len(own)
    first = own[0].shape[0]
    products = [in_vmem((padded(rows), hidden), jnp.float32)] * 2
    outs = [in_vmem((first, half)), in_vmem((rows - first, half))]
    x = [pltpu.VMEM((padded(rows), half), jnp.bfloat16)]
    flops = 2 * padded(rows) * hidden * width
    gated, lifted = call(functools.partial(first_kernel, n_blocks), place, (*own, gate, up), products, x, flops)
    units, *theirs = call(
        functools.partial(second_kernel, n_blocks, n_experts),
        place,
        (*own, *across, gated, lifted, gate, up, down_theirs),
        [in_vmem((padded(rows), hidden)), *outs],
        x,
        flops + flops // 2,
    )
    theirs = [swap(a) for a in theirs]
    mine = call(
        functools.partial(third_kernel, n_blocks, n_experts),
        last_place,
        (*own, units, down_mine),
        outs,
        [],
        flops // 2,
    )
    return mine, theirs


def add_kernel(*refs):
    *terms, out = refs
    out[...] = sum(t[...].astype(jnp.float32) for t in terms).astype(out.dtype)


def add(*terms):
    vmem = pl.BlockSpec(memory_space=pltpu.VMEM)
    return pl.pallas_call(
        add_kernel,
        out_shape=in_vmem(terms[0].shape),
        in_specs=[vmem] * len(terms),
        out_specs=vmem,
        cost_estimate=pl.CostEstimate(flops=0, bytes_accessed=12 << 20, transcendentals=0),
    )(*[hold(t) for t in terms])


def ring_body(tokens, expert_ids, gate_probs, w_gate, w_up, w_down):
    n = lax.axis_size("ep")
    rows = tokens.shape[0]
    order = list(range(0, n, 2)) + list(range(n - 1, 0, -2))
    ahead = [(order[i], order[(i + 1) % n]) for i in range(n)]
    back = [(b, a) for a, b in ahead]
    swap = functools.partial(lax.ppermute, axis_name="tp", perm=[(0, 1), (1, 0)])
    far = n // 2
    place = jnp.stack([lax.axis_index("tp"), lax.axis_index("ep")]).astype(jnp.int32)
    packed = pack(tokens, expert_ids, gate_probs, n)
    gate, up = turn_weights(after(place, packed), w_gate[0].T, w_up[0].T)

    came, across, value, parts = {0: packed}, {}, {}, {}

    def run(keys, wait_for=None):
        at = place if wait_for is None else after(place, wait_for)
        mine, theirs = run_expert(at, [came[k] for k in keys], [across[k] for k in keys], weights, n)
        return [(keys[2 * i : 2 * i + 2], *pair) for i, pair in enumerate(zip(mine, theirs))]

    def keep(keys, mine, theirs):
        pairs = ((mine, theirs), lax.optimization_barrier((mine, theirs)))
        start = 0
        for i, k in enumerate(keys):
            mine, theirs = pairs[i % 2]
            span = slice(start, start + came[k].shape[0])
            start = span.stop
            parts[k] = mine[span], theirs[span]
            value[k] = mine[span].astype(jnp.float32) + theirs[span].astype(jnp.float32)

    came[1] = lax.ppermute(packed, "ep", ahead)
    came[-1] = lax.ppermute(packed, "ep", back)
    across[0] = swap(packed)
    weights, done, near = [gate, up], up, []
    for k in range(2, far + 1):
        came[k - 1], came[1 - k] = after(came[k - 1], done), after(came[1 - k], done)
        came[k] = lax.ppermute(came[k - 1], "ep", ahead)
        if k < far:
            came[-k] = lax.ppermute(came[1 - k], "ep", back)
        across[k - 1], across[1 - k] = swap(came[k - 1]), swap(came[1 - k])
        if k == 2:
            weights += halve_weights(after(place, came[1]), w_down[0])
            done = weights[-1]
        else:
            near += run([k - 2, 2 - k], across[0] if k == 3 else None)
            done = near[-1][-1]
    came[far] = after(came[far], done)
    across[far] = swap(came[far])
    last = [far, far - 1, 1 - far]
    near = [(keys, mine, swap(after(theirs, came[far]))) for keys, mine, theirs in near]
    stages = run_expert_in_stages(
        place, [came[k] for k in last], [across[k] for k in last], swap, weights, n, after(place, [theirs for *_, theirs in near])
    )
    for keys, mine, theirs in (*zip(([far], last[1:]), *stages), *near):
        keep(keys, mine, theirs)

    to_ahead = value[far].astype(jnp.bfloat16)
    to_back = (value[far - 1]).astype(jnp.bfloat16)
    for k in range(far - 1, -1, -1):
        behind = lax.ppermute(to_ahead, "ep", ahead)
        if k == far - 1:
            ((keys, mine, done),) = run([0], to_ahead)
            keep(keys, mine, swap(done))
        else:
            to_back = done = add(*parts[k], after(front, to_ahead))
        if k:
            front = lax.ppermute(to_back, "ep", back)
            to_ahead = (value[-k] + after(behind, done).astype(jnp.float32)).astype(jnp.bfloat16)
    return (to_back.astype(jnp.float32) + behind.astype(jnp.float32)).astype(jnp.bfloat16)


def swiglu_expert(rows, gate_part, up_part, down_part):
    gated = jnp.dot(rows, gate_part, preferred_element_type=jnp.float32)
    lifted = jnp.dot(rows, up_part, preferred_element_type=jnp.float32)
    hidden = (jax.nn.silu(gated) * lifted).astype(jnp.bfloat16)
    return jnp.dot(hidden, down_part, preferred_element_type=jnp.float32)


def slot_table(expert_ids, n_experts):
    routed = expert_ids.reshape(-1)
    pair_count = routed.shape[0]
    onehot = (routed[:, None] == jnp.arange(n_experts, dtype=jnp.int32)[None, :]).astype(
        jnp.bfloat16
    )
    row_index = lax.broadcasted_iota(jnp.int32, (pair_count, pair_count), 0)
    col_index = lax.broadcasted_iota(jnp.int32, (pair_count, pair_count), 1)
    earlier = (row_index > col_index).astype(jnp.bfloat16)
    before = jnp.dot(earlier, onehot, preferred_element_type=jnp.float32)
    slots = jnp.sum(before * onehot.astype(jnp.float32), axis=1).astype(jnp.int32)
    return (routed, slots)


def slot_body(tokens, expert_ids, gate_probs, w_gate, w_up, w_down):
    n_experts = lax.axis_size("ep")
    tok_rows, top_count = expert_ids.shape
    capacity = 3 * tok_rows * top_count // (2 * n_experts)
    routed, slots = slot_table(expert_ids, n_experts)
    positions = routed * capacity + slots
    pair_token = jnp.repeat(jnp.arange(tok_rows, dtype=jnp.int32), top_count)
    buffer_rows = n_experts * capacity
    owners = jnp.full((buffer_rows,), tok_rows, jnp.int32).at[positions].set(pair_token)
    half_slots = capacity // 2
    whole_tokens = lax.all_gather(tokens, "tp", axis=1, tiled=True)
    width = whole_tokens.shape[1]
    gate_full, up_full = (
        lax.all_gather(w_gate, "tp", axis=2, tiled=True),
        lax.all_gather(w_up, "tp", axis=2, tiled=True),
    )
    down_full = lax.all_gather(w_down, "tp", axis=1, tiled=True)
    padded = jnp.concatenate([whole_tokens, jnp.zeros((1, width), whole_tokens.dtype)], 0)
    outgoing = padded[owners].reshape(n_experts, capacity, width)
    lane = lax.axis_index("tp")
    mine = lax.dynamic_slice_in_dim(outgoing, lane * half_slots, half_slots, 1)
    block = lax.all_to_all(mine, "ep", split_axis=0, concat_axis=0, tiled=True)
    sources, items, columns = block.shape
    result = swiglu_expert(
        block.reshape(sources * items, columns), gate_full[0], up_full[0], down_full[0]
    )
    result = result.astype(jnp.bfloat16).reshape(sources, items, columns)
    returned = lax.all_to_all(result, "ep", split_axis=0, concat_axis=0, tiled=True)
    received = returned.reshape(n_experts * half_slots, width)
    in_half = slots // half_slots == lane
    local_pos = routed * half_slots + slots % half_slots
    picked = received[local_pos].astype(jnp.float32).reshape(tok_rows, top_count, width)
    weighted = jnp.where(in_half.reshape(tok_rows, top_count), gate_probs, 0.0)
    partial_value = jnp.sum(weighted[:, :, None] * picked, axis=1)
    return lax.psum_scatter(partial_value, "tp", scatter_dimension=1, tiled=True).astype(
        jnp.bfloat16
    )


def solution(mesh):
    in_specs = (
        P(("groups", "ep"), "tp"),
        P(("groups", "ep"), None),
        P(("groups", "ep"), None),
        P("ep", None, "tp"),
        P("ep", None, "tp"),
        P("ep", "tp", None),
    )
    out_specs = P(("groups", "ep"), "tp")

    def body(tokens, expert_ids, *rest):
        n, top = lax.axis_size("ep"), expert_ids.shape[1]
        small = n <= 4 * top and n % 2 == 0 and n >= 6 and lax.axis_size("tp") == 2
        return (ring_body if small else slot_body)(tokens, expert_ids, *rest)

    return jax.shard_map(body, mesh=mesh, in_specs=in_specs, out_specs=out_specs, check_vma=False)
```

```python
import functools

import jax
import jax.numpy as jnp
from jax import lax
from jax.experimental import pallas as pl
from jax.experimental.pallas import tpu as pltpu
from jax.sharding import PartitionSpec as P

SPLITS = 3


def in_vmem(shape, dtype=jnp.bfloat16):
    return pltpu.MemorySpace.VMEM(shape, dtype)


def hold(x):
    return pltpu.with_memory_space_constraint(x, pltpu.VMEM)


def after(x, done):
    return lax.optimization_barrier((x, done))[0]


def pack_kernel(n_experts, tokens_in, ids_in, probs_in, packed, tokens, ids, probs, sems):
    copies = [
        pltpu.make_async_copy(src, dst, sems.at[i])
        for i, (src, dst) in enumerate(((ids_in, ids), (probs_in, probs), (tokens_in, tokens)))
    ]
    for copy in copies:
        copy.start()
    top, rows = ids.shape
    half = tokens.shape[1]
    copies[0].wait()
    copies[1].wait()
    expert = lax.broadcasted_iota(jnp.int32, (n_experts, rows), 0)
    rest = jnp.zeros((n_experts, rows), jnp.float32)
    for k in range(top):
        rest += jnp.where(ids[k : k + 1, :] == expert, probs[k : k + 1, :], 0.0)
    terms = []
    for _ in range(SPLITS):
        term = rest.astype(jnp.bfloat16).astype(jnp.float32)
        terms.append(term)
        rest = rest - term
    packed[:, half:] = jnp.concatenate(terms, axis=0).T.astype(jnp.bfloat16)
    copies[2].wait()
    packed[:, :half] = tokens[...]


def pack(tokens, expert_ids, gate_probs, n_experts):
    rows, half = tokens.shape
    args = (tokens, expert_ids.T, gate_probs.T)
    return pl.pallas_call(
        functools.partial(pack_kernel, n_experts),
        out_shape=in_vmem((rows, half + SPLITS * n_experts)),
        in_specs=[pl.BlockSpec(memory_space=pltpu.HBM)] * 3,
        out_specs=pl.BlockSpec(memory_space=pltpu.VMEM),
        scratch_shapes=[pltpu.VMEM(a.shape, a.dtype) for a in args] + [pltpu.SemaphoreType.DMA((3,))],
        compiler_params=pltpu.CompilerParams(vmem_limit_bytes=8 << 20),
    )(*[pltpu.with_memory_space_constraint(a, pltpu.HBM) for a in args])


def pieces(hidden):
    first = -(-hidden // 256) * 128
    return ((0, first), (first, hidden))


def turn_kernel(after_this, gate_in, up_in, gate, up, gate_buf, up_buf, sems):
    steps = []
    for i, (src, buf, out) in enumerate(((gate_in, gate_buf, gate), (up_in, up_buf, up))):
        for j, (start, stop) in enumerate(pieces(src.shape[0])):
            span = pl.ds(start, stop - start)
            steps.append((pltpu.make_async_copy(src.at[span], buf.at[span], sems.at[i, j]), buf, out, start, stop))
    for copy, *_ in steps:
        copy.start()
    for copy, buf, out, start, stop in steps:
        copy.wait()
        out[:, start:stop] = buf[start:stop, :].T


def turn_weights(after_this, *weights):
    hidden, width = weights[0].shape
    return pl.pallas_call(
        turn_kernel,
        out_shape=[in_vmem((width, hidden))] * 2,
        in_specs=[pl.BlockSpec(memory_space=pltpu.SMEM)] + [pl.BlockSpec(memory_space=pltpu.HBM)] * 2,
        out_specs=[pl.BlockSpec(memory_space=pltpu.VMEM)] * 2,
        scratch_shapes=[pltpu.VMEM((hidden, width), jnp.bfloat16)] * 2 + [pltpu.SemaphoreType.DMA((2, 2))],
        compiler_params=pltpu.CompilerParams(vmem_limit_bytes=32 << 20),
        cost_estimate=pl.CostEstimate(flops=0, bytes_accessed=8 * hidden * width, transcendentals=0),
    )(after_this, *[pltpu.with_memory_space_constraint(w, pltpu.HBM) for w in weights])


def halve_kernel(place, down_in, down_mine, down_theirs, down_buf, sems):
    lane = place[0]
    half = down_mine.shape[1]
    spans = [slice(start, stop) for start, stop in pieces(down_in.shape[0])]
    copies = [
        pltpu.make_async_copy(down_in.at[pl.ds(s.start, s.stop - s.start)], down_buf.at[pl.ds(s.start, s.stop - s.start)], sems.at[i])
        for i, s in enumerate(spans)
    ]
    for copy in copies:
        copy.start()
    for copy, s in zip(copies, spans):
        copy.wait()

        @pl.when(lane == 0)
        def _():
            down_mine[s, :] = down_buf[s, :half]
            down_theirs[s, :] = down_buf[s, half:]

        @pl.when(lane != 0)
        def _():
            down_mine[s, :] = down_buf[s, half:]
            down_theirs[s, :] = down_buf[s, :half]


def halve_weights(place, w_down):
    hidden, width = w_down.shape
    return pl.pallas_call(
        halve_kernel,
        out_shape=[in_vmem((hidden, width // 2))] * 2,
        in_specs=[pl.BlockSpec(memory_space=pltpu.SMEM), pl.BlockSpec(memory_space=pltpu.HBM)],
        out_specs=[pl.BlockSpec(memory_space=pltpu.VMEM)] * 2,
        scratch_shapes=[pltpu.VMEM((hidden, width), jnp.bfloat16), pltpu.SemaphoreType.DMA((2,))],
        compiler_params=pltpu.CompilerParams(vmem_limit_bytes=32 << 20),
        cost_estimate=pl.CostEstimate(flops=0, bytes_accessed=8 * hidden * width, transcendentals=0),
    )(place, pltpu.with_memory_space_constraint(w_down, pltpu.HBM))


def gather_rows(blocks, x, width):
    start = 0
    for block in blocks:
        x[start : start + block.shape[0], :] = block[:, :width]
        start += block.shape[0]
    if start < x.shape[0]:
        x[start:, :] = jnp.zeros((x.shape[0] - start, width), x.dtype)


def project(x, lane, w):
    half = x.shape[1]
    return jnp.dot(x[...], w[pl.ds(pl.multiple_of(lane * half, 16), half), :], preferred_element_type=jnp.float32)


def activate(gated, lifted):
    return (gated / (1.0 + jnp.exp(-gated)) * lifted).astype(jnp.bfloat16)


def gate_weights(blocks, half, expert, n_experts):
    weights = []
    for block in blocks:
        terms = block[:, half:].astype(jnp.float32)
        column = lax.broadcasted_iota(jnp.int32, terms.shape, 1)
        weights.append(jnp.sum(jnp.where(lax.rem(column, n_experts) == expert, terms, 0.0), axis=1, keepdims=True))
    return weights


def lower(hidden, w, weights, *outs):
    value = jnp.dot(hidden, w[...], preferred_element_type=jnp.float32)
    places = [(out, at) for out in outs for at in range(0, out.shape[0], weights[0].shape[0])]
    start = 0
    for weight, (out, at) in zip(weights, places):
        rows = weight.shape[0]
        out[at : at + rows] = (value[start : start + rows] * weight).astype(jnp.bfloat16)
        start += rows


def expert_kernel(n_blocks, n_experts, place, *refs):
    own, across = refs[:n_blocks], refs[n_blocks : 2 * n_blocks]
    w_gate, w_up, down_mine, down_theirs, *outs, x_own, x_across = refs[2 * n_blocks :]
    lane, expert = place[0], place[1]
    half = x_own.shape[1]
    gather_rows(own, x_own, half)
    gather_rows(across, x_across, half)
    gated = project(x_own, lane, w_gate) + project(x_across, 1 - lane, w_gate)
    lifted = project(x_own, lane, w_up) + project(x_across, 1 - lane, w_up)
    hidden = activate(gated, lifted)
    weights = gate_weights(own, half, expert, n_experts)
    mine, theirs = outs[: len(outs) // 2], outs[len(outs) // 2 :]
    lower(hidden, down_theirs, weights, *theirs)
    lower(hidden, down_mine, weights, *mine)


def first_kernel(n_blocks, place, *refs):
    own = refs[:n_blocks]
    w_gate, w_up, gated, lifted, x = refs[n_blocks:]
    gather_rows(own, x, x.shape[1])
    gated[...] = project(x, place[0], w_gate)
    lifted[...] = project(x, place[0], w_up)


def second_kernel(n_blocks, n_experts, place, *refs):
    own, across = refs[:n_blocks], refs[n_blocks : 2 * n_blocks]
    gated, lifted, w_gate, w_up, down_theirs, hidden, *theirs, x = refs[2 * n_blocks :]
    half = x.shape[1]
    gather_rows(across, x, half)
    there = 1 - place[0]
    hidden[...] = activate(gated[...] + project(x, there, w_gate), lifted[...] + project(x, there, w_up))
    lower(hidden[...], down_theirs, gate_weights(own, half, place[1], n_experts), *theirs)


def third_kernel(n_blocks, n_experts, place, *refs):
    own = refs[:n_blocks]
    hidden, down_mine, *mine = refs[n_blocks:]
    lower(hidden[...], down_mine, gate_weights(own, mine[0].shape[1], place[1], n_experts), *mine)


def call(kernel, place, args, out_shape, scratch_shapes, flops):
    vmem = pl.BlockSpec(memory_space=pltpu.VMEM)
    return pl.pallas_call(
        kernel,
        out_shape=out_shape,
        in_specs=[pl.BlockSpec(memory_space=pltpu.SMEM)] + [vmem] * len(args),
        out_specs=[vmem] * len(out_shape),
        scratch_shapes=scratch_shapes,
        compiler_params=pltpu.CompilerParams(vmem_limit_bytes=16 << 20),
        cost_estimate=pl.CostEstimate(flops=flops, bytes_accessed=flops // 128, transcendentals=0),
    )(place, *[hold(a) for a in args])


def padded(rows):
    return max(rows, 128)


def run_expert(place, own, across, weights, n_experts):
    width, hidden = weights[0].shape
    half = width // 2
    rows, pairs = sum(a.shape[0] for a in own), max(1, len(own) // 2)
    outs = call(
        functools.partial(expert_kernel, len(own), n_experts),
        place,
        (*own, *across, *weights),
        [in_vmem((rows // pairs, half))] * (2 * pairs),
        [pltpu.VMEM((padded(rows), half), jnp.bfloat16)] * 2,
        6 * padded(rows) * hidden * width,
    )
    return outs[:pairs], outs[pairs:]


def run_expert_in_stages(place, own, across, swap, weights, n_experts):
    gate, up, down_mine, down_theirs = weights
    width, hidden = gate.shape
    half = width // 2
    rows, n_blocks = sum(a.shape[0] for a in own), len(own)
    first = own[0].shape[0]
    products = [in_vmem((padded(rows), hidden), jnp.float32)] * 2
    outs = [in_vmem((first, half)), in_vmem((rows - first, half))]
    x = [pltpu.VMEM((padded(rows), half), jnp.bfloat16)]
    flops = 2 * padded(rows) * hidden * width
    gated, lifted = call(functools.partial(first_kernel, n_blocks), place, (*own, gate, up), products, x, flops)
    units, *theirs = call(
        functools.partial(second_kernel, n_blocks, n_experts),
        place,
        (*own, *across, gated, lifted, gate, up, down_theirs),
        [in_vmem((padded(rows), hidden)), *outs],
        x,
        flops + flops // 2,
    )
    theirs = [swap(a) for a in theirs]
    mine = call(
        functools.partial(third_kernel, n_blocks, n_experts),
        place,
        (*own, units, down_mine),
        outs,
        [],
        flops // 2,
    )
    return mine, theirs


def add_kernel(*refs):
    *terms, out = refs
    out[...] = sum(t[...].astype(jnp.float32) for t in terms).astype(out.dtype)


def add(*terms):
    vmem = pl.BlockSpec(memory_space=pltpu.VMEM)
    return pl.pallas_call(
        add_kernel,
        out_shape=in_vmem(terms[0].shape),
        in_specs=[vmem] * len(terms),
        out_specs=vmem,
        cost_estimate=pl.CostEstimate(flops=0, bytes_accessed=12 << 20, transcendentals=0),
    )(*[hold(t) for t in terms])


def ring_body(tokens, expert_ids, gate_probs, w_gate, w_up, w_down):
    n = lax.axis_size("ep")
    rows = tokens.shape[0]
    order = list(range(0, n, 2)) + list(range(n - 1, 0, -2))
    ahead = [(order[i], order[(i + 1) % n]) for i in range(n)]
    back = [(b, a) for a, b in ahead]
    swap = functools.partial(lax.ppermute, axis_name="tp", perm=[(0, 1), (1, 0)])
    far = n // 2
    place = jnp.stack([lax.axis_index("tp"), lax.axis_index("ep")]).astype(jnp.int32)
    packed = pack(tokens, expert_ids, gate_probs, n)
    gate, up = turn_weights(after(place, packed), w_gate[0].T, w_up[0].T)

    came, across, value, parts = {0: packed}, {}, {}, {}

    def run(keys, wait_for=None):
        at = place if wait_for is None else after(place, wait_for)
        mine, theirs = run_expert(at, [came[k] for k in keys], [across[k] for k in keys], weights, n)
        return [(keys[2 * i : 2 * i + 2], *pair) for i, pair in enumerate(zip(mine, theirs))]

    def keep(keys, mine, theirs):
        pairs = ((mine, theirs), lax.optimization_barrier((mine, theirs)))
        start = 0
        for i, k in enumerate(keys):
            mine, theirs = pairs[i % 2]
            span = slice(start, start + came[k].shape[0])
            start = span.stop
            parts[k] = mine[span], theirs[span]
            value[k] = mine[span].astype(jnp.float32) + theirs[span].astype(jnp.float32)

    came[1] = lax.ppermute(packed, "ep", ahead)
    came[-1] = lax.ppermute(packed, "ep", back)
    weights, done, near = [gate, up], up, []
    for k in range(2, far + 1):
        came[k - 1], came[1 - k] = after(came[k - 1], done), after(came[1 - k], done)
        came[k] = lax.ppermute(came[k - 1], "ep", ahead)
        if k < far:
            came[-k] = lax.ppermute(came[1 - k], "ep", back)
        across[k - 1], across[1 - k] = swap(came[k - 1]), swap(came[1 - k])
        if k == 2:
            weights += halve_weights(after(place, came[1]), w_down[0])
            done = weights[-1]
        else:
            near += run([k - 2, 2 - k])
            done = near[-1][-1]
    came[far] = after(came[far], done)
    across[far] = swap(came[far])
    last = [far, far - 1, 1 - far]
    for keys, mine, theirs in zip(([far], last[1:]), *run_expert_in_stages(place, [came[k] for k in last], [across[k] for k in last], swap, weights, n)):
        keep(keys, mine, theirs)
    for keys, mine, theirs in near:
        keep(keys, mine, swap(after(theirs, value[far])))

    to_ahead = value[far].astype(jnp.bfloat16)
    to_back = (value[far - 1]).astype(jnp.bfloat16)
    for k in range(far - 1, -1, -1):
        behind = lax.ppermute(to_ahead, "ep", ahead)
        done = to_ahead
        if k < far - 1:
            to_back = done = add(*parts[k], after(front, to_ahead))
        if k:
            front = lax.ppermute(to_back, "ep", back)
        if k == 2:
            across[0] = swap(after(packed, to_ahead))
        if k == 1:
            ((keys, mine, done),) = run([0], done)
            keep(keys, mine, swap(done))
        if k:
            to_ahead = (value[-k] + after(behind, done).astype(jnp.float32)).astype(jnp.bfloat16)
    return (to_back.astype(jnp.float32) + behind.astype(jnp.float32)).astype(jnp.bfloat16)


def swiglu_expert(rows, gate_part, up_part, down_part):
    gated = jnp.dot(rows, gate_part, preferred_element_type=jnp.float32)
    lifted = jnp.dot(rows, up_part, preferred_element_type=jnp.float32)
    hidden = (jax.nn.silu(gated) * lifted).astype(jnp.bfloat16)
    return jnp.dot(hidden, down_part, preferred_element_type=jnp.float32)


def slot_table(expert_ids, n_experts):
    routed = expert_ids.reshape(-1)
    pair_count = routed.shape[0]
    onehot = (routed[:, None] == jnp.arange(n_experts, dtype=jnp.int32)[None, :]).astype(
        jnp.bfloat16
    )
    row_index = lax.broadcasted_iota(jnp.int32, (pair_count, pair_count), 0)
    col_index = lax.broadcasted_iota(jnp.int32, (pair_count, pair_count), 1)
    earlier = (row_index > col_index).astype(jnp.bfloat16)
    before = jnp.dot(earlier, onehot, preferred_element_type=jnp.float32)
    slots = jnp.sum(before * onehot.astype(jnp.float32), axis=1).astype(jnp.int32)
    return (routed, slots)


def slot_body(tokens, expert_ids, gate_probs, w_gate, w_up, w_down):
    n_experts = lax.axis_size("ep")
    tok_rows, top_count = expert_ids.shape
    capacity = 3 * tok_rows * top_count // (2 * n_experts)
    routed, slots = slot_table(expert_ids, n_experts)
    positions = routed * capacity + slots
    pair_token = jnp.repeat(jnp.arange(tok_rows, dtype=jnp.int32), top_count)
    buffer_rows = n_experts * capacity
    owners = jnp.full((buffer_rows,), tok_rows, jnp.int32).at[positions].set(pair_token)
    half_slots = capacity // 2
    whole_tokens = lax.all_gather(tokens, "tp", axis=1, tiled=True)
    width = whole_tokens.shape[1]
    gate_full, up_full = (
        lax.all_gather(w_gate, "tp", axis=2, tiled=True),
        lax.all_gather(w_up, "tp", axis=2, tiled=True),
    )
    down_full = lax.all_gather(w_down, "tp", axis=1, tiled=True)
    padded = jnp.concatenate([whole_tokens, jnp.zeros((1, width), whole_tokens.dtype)], 0)
    outgoing = padded[owners].reshape(n_experts, capacity, width)
    lane = lax.axis_index("tp")
    mine = lax.dynamic_slice_in_dim(outgoing, lane * half_slots, half_slots, 1)
    block = lax.all_to_all(mine, "ep", split_axis=0, concat_axis=0, tiled=True)
    sources, items, columns = block.shape
    result = swiglu_expert(
        block.reshape(sources * items, columns), gate_full[0], up_full[0], down_full[0]
    )
    result = result.astype(jnp.bfloat16).reshape(sources, items, columns)
    returned = lax.all_to_all(result, "ep", split_axis=0, concat_axis=0, tiled=True)
    received = returned.reshape(n_experts * half_slots, width)
    in_half = slots // half_slots == lane
    local_pos = routed * half_slots + slots % half_slots
    picked = received[local_pos].astype(jnp.float32).reshape(tok_rows, top_count, width)
    weighted = jnp.where(in_half.reshape(tok_rows, top_count), gate_probs, 0.0)
    partial_value = jnp.sum(weighted[:, :, None] * picked, axis=1)
    return lax.psum_scatter(partial_value, "tp", scatter_dimension=1, tiled=True).astype(
        jnp.bfloat16
    )


def solution(mesh):
    in_specs = (
        P(("groups", "ep"), "tp"),
        P(("groups", "ep"), None),
        P(("groups", "ep"), None),
        P("ep", None, "tp"),
        P("ep", None, "tp"),
        P("ep", "tp", None),
    )
    out_specs = P(("groups", "ep"), "tp")

    def body(tokens, expert_ids, *rest):
        n, top = lax.axis_size("ep"), expert_ids.shape[1]
        small = n <= 4 * top and n % 2 == 0 and n >= 6 and lax.axis_size("tp") == 2
        return (ring_body if small else slot_body)(tokens, expert_ids, *rest)

    return jax.shard_map(body, mesh=mesh, in_specs=in_specs, out_specs=out_specs, check_vma=False)
```

```python
import functools

import jax
import jax.numpy as jnp
from jax import lax
from jax.experimental import pallas as pl
from jax.experimental.pallas import tpu as pltpu
from jax.sharding import PartitionSpec as P

SPLITS = 3


def in_vmem(shape, dtype=jnp.bfloat16):
    return pltpu.MemorySpace.VMEM(shape, dtype)


def hold(x):
    return pltpu.with_memory_space_constraint(x, pltpu.VMEM)


def after(x, done):
    return lax.optimization_barrier((x, done))[0]


def pack_kernel(n_experts, tokens_in, ids_in, probs_in, packed, tokens, ids, probs, sems):
    copies = [
        pltpu.make_async_copy(src, dst, sems.at[i])
        for i, (src, dst) in enumerate(((ids_in, ids), (probs_in, probs), (tokens_in, tokens)))
    ]
    for copy in copies:
        copy.start()
    top, rows = ids.shape
    half = tokens.shape[1]
    copies[0].wait()
    copies[1].wait()
    expert = lax.broadcasted_iota(jnp.int32, (n_experts, rows), 0)
    rest = jnp.zeros((n_experts, rows), jnp.float32)
    for k in range(top):
        rest += jnp.where(ids[k : k + 1, :] == expert, probs[k : k + 1, :], 0.0)
    terms = []
    for _ in range(SPLITS):
        term = rest.astype(jnp.bfloat16).astype(jnp.float32)
        terms.append(term)
        rest = rest - term
    packed[:, half:] = jnp.concatenate(terms, axis=0).T.astype(jnp.bfloat16)
    copies[2].wait()
    packed[:, :half] = tokens[...]


def pack(tokens, expert_ids, gate_probs, n_experts):
    rows, half = tokens.shape
    args = (tokens, expert_ids.T, gate_probs.T)
    return pl.pallas_call(
        functools.partial(pack_kernel, n_experts),
        out_shape=in_vmem((rows, half + SPLITS * n_experts)),
        in_specs=[pl.BlockSpec(memory_space=pltpu.HBM)] * 3,
        out_specs=pl.BlockSpec(memory_space=pltpu.VMEM),
        scratch_shapes=[pltpu.VMEM(a.shape, a.dtype) for a in args] + [pltpu.SemaphoreType.DMA((3,))],
        compiler_params=pltpu.CompilerParams(vmem_limit_bytes=8 << 20),
    )(*[pltpu.with_memory_space_constraint(a, pltpu.HBM) for a in args])


def pieces(hidden):
    first = -(-hidden // 256) * 128
    return ((0, first), (first, hidden))


def turn_kernel(after_this, gate_in, up_in, gate, up, gate_buf, up_buf, sems):
    steps = []
    for i, (src, buf, out) in enumerate(((gate_in, gate_buf, gate), (up_in, up_buf, up))):
        for j, (start, stop) in enumerate(pieces(src.shape[0])):
            span = pl.ds(start, stop - start)
            steps.append((pltpu.make_async_copy(src.at[span], buf.at[span], sems.at[i, j]), buf, out, start, stop))
    for copy, *_ in steps:
        copy.start()
    for copy, buf, out, start, stop in steps:
        copy.wait()
        out[:, start:stop] = buf[start:stop, :].T


def turn_weights(after_this, *weights):
    hidden, width = weights[0].shape
    return pl.pallas_call(
        turn_kernel,
        out_shape=[in_vmem((width, hidden))] * 2,
        in_specs=[pl.BlockSpec(memory_space=pltpu.SMEM)] + [pl.BlockSpec(memory_space=pltpu.HBM)] * 2,
        out_specs=[pl.BlockSpec(memory_space=pltpu.VMEM)] * 2,
        scratch_shapes=[pltpu.VMEM((hidden, width), jnp.bfloat16)] * 2 + [pltpu.SemaphoreType.DMA((2, 2))],
        compiler_params=pltpu.CompilerParams(vmem_limit_bytes=32 << 20),
        cost_estimate=pl.CostEstimate(flops=0, bytes_accessed=8 * hidden * width, transcendentals=0),
    )(after_this, *[pltpu.with_memory_space_constraint(w, pltpu.HBM) for w in weights])


def halve_kernel(place, down_in, down_mine, down_theirs, down_buf, sems):
    lane = place[0]
    half = down_mine.shape[1]
    spans = [slice(start, stop) for start, stop in pieces(down_in.shape[0])]
    copies = [
        pltpu.make_async_copy(down_in.at[pl.ds(s.start, s.stop - s.start)], down_buf.at[pl.ds(s.start, s.stop - s.start)], sems.at[i])
        for i, s in enumerate(spans)
    ]
    for copy in copies:
        copy.start()
    for copy, s in zip(copies, spans):
        copy.wait()

        @pl.when(lane == 0)
        def _():
            down_mine[s, :] = down_buf[s, :half]
            down_theirs[s, :] = down_buf[s, half:]

        @pl.when(lane != 0)
        def _():
            down_mine[s, :] = down_buf[s, half:]
            down_theirs[s, :] = down_buf[s, :half]


def halve_weights(place, w_down):
    hidden, width = w_down.shape
    return pl.pallas_call(
        halve_kernel,
        out_shape=[in_vmem((hidden, width // 2))] * 2,
        in_specs=[pl.BlockSpec(memory_space=pltpu.SMEM), pl.BlockSpec(memory_space=pltpu.HBM)],
        out_specs=[pl.BlockSpec(memory_space=pltpu.VMEM)] * 2,
        scratch_shapes=[pltpu.VMEM((hidden, width), jnp.bfloat16), pltpu.SemaphoreType.DMA((2,))],
        compiler_params=pltpu.CompilerParams(vmem_limit_bytes=32 << 20),
        cost_estimate=pl.CostEstimate(flops=0, bytes_accessed=8 * hidden * width, transcendentals=0),
    )(place, pltpu.with_memory_space_constraint(w_down, pltpu.HBM))


def gather_rows(blocks, x, width):
    start = 0
    for block in blocks:
        x[start : start + block.shape[0], :] = block[:, :width]
        start += block.shape[0]
    if start < x.shape[0]:
        x[start:, :] = jnp.zeros((x.shape[0] - start, width), x.dtype)


def project(x, lane, w):
    half = x.shape[1]
    return jnp.dot(x[...], w[pl.ds(pl.multiple_of(lane * half, 16), half), :], preferred_element_type=jnp.float32)


def activate(gated, lifted):
    return (gated / (1.0 + jnp.exp(-gated)) * lifted).astype(jnp.bfloat16)


def gate_weights(blocks, half, expert, n_experts):
    weights = []
    for block in blocks:
        terms = block[:, half:].astype(jnp.float32)
        column = lax.broadcasted_iota(jnp.int32, terms.shape, 1)
        weights.append(jnp.sum(jnp.where(lax.rem(column, n_experts) == expert, terms, 0.0), axis=1, keepdims=True))
    return weights


def lower(hidden, w, weights, *outs):
    value = jnp.dot(hidden, w[...], preferred_element_type=jnp.float32)
    places = [(out, at) for out in outs for at in range(0, out.shape[0], weights[0].shape[0])]
    start = 0
    for weight, (out, at) in zip(weights, places):
        rows = weight.shape[0]
        out[at : at + rows] = (value[start : start + rows] * weight).astype(jnp.bfloat16)
        start += rows


def expert_kernel(n_blocks, n_experts, place, *refs):
    own, across = refs[:n_blocks], refs[n_blocks : 2 * n_blocks]
    w_gate, w_up, down_mine, down_theirs, *outs, x_own, x_across = refs[2 * n_blocks :]
    lane, expert = place[0], place[1]
    half = x_own.shape[1]
    gather_rows(own, x_own, half)
    gather_rows(across, x_across, half)
    gated = project(x_own, lane, w_gate) + project(x_across, 1 - lane, w_gate)
    lifted = project(x_own, lane, w_up) + project(x_across, 1 - lane, w_up)
    hidden = activate(gated, lifted)
    weights = gate_weights(own, half, expert, n_experts)
    mine, theirs = outs[: len(outs) // 2], outs[len(outs) // 2 :]
    lower(hidden, down_theirs, weights, *theirs)
    lower(hidden, down_mine, weights, *mine)


def first_kernel(n_blocks, place, *refs):
    own = refs[:n_blocks]
    w_gate, w_up, gated, lifted, x = refs[n_blocks:]
    gather_rows(own, x, x.shape[1])
    gated[...] = project(x, place[0], w_gate)
    lifted[...] = project(x, place[0], w_up)


def second_kernel(n_blocks, n_experts, place, *refs):
    own, across = refs[:n_blocks], refs[n_blocks : 2 * n_blocks]
    gated, lifted, w_gate, w_up, down_theirs, hidden, *theirs, x = refs[2 * n_blocks :]
    half = x.shape[1]
    gather_rows(across, x, half)
    there = 1 - place[0]
    hidden[...] = activate(gated[...] + project(x, there, w_gate), lifted[...] + project(x, there, w_up))
    lower(hidden[...], down_theirs, gate_weights(own, half, place[1], n_experts), *theirs)


def third_kernel(n_blocks, n_experts, place, *refs):
    own = refs[:n_blocks]
    hidden, down_mine, *mine = refs[n_blocks:]
    lower(hidden[...], down_mine, gate_weights(own, mine[0].shape[1], place[1], n_experts), *mine)


def call(kernel, place, args, out_shape, scratch_shapes, flops):
    vmem = pl.BlockSpec(memory_space=pltpu.VMEM)
    return pl.pallas_call(
        kernel,
        out_shape=out_shape,
        in_specs=[pl.BlockSpec(memory_space=pltpu.SMEM)] + [vmem] * len(args),
        out_specs=[vmem] * len(out_shape),
        scratch_shapes=scratch_shapes,
        compiler_params=pltpu.CompilerParams(vmem_limit_bytes=16 << 20),
        cost_estimate=pl.CostEstimate(flops=flops, bytes_accessed=flops // 128, transcendentals=0),
    )(place, *[hold(a) for a in args])


def padded(rows):
    return max(rows, 128)


def run_expert(place, own, across, weights, n_experts):
    width, hidden = weights[0].shape
    half = width // 2
    rows, pairs = sum(a.shape[0] for a in own), max(1, len(own) // 2)
    outs = call(
        functools.partial(expert_kernel, len(own), n_experts),
        place,
        (*own, *across, *weights),
        [in_vmem((rows // pairs, half))] * (2 * pairs),
        [pltpu.VMEM((padded(rows), half), jnp.bfloat16)] * 2,
        6 * padded(rows) * hidden * width,
    )
    return outs[:pairs], outs[pairs:]


def run_expert_in_stages(place, own, across, swap, weights, n_experts):
    gate, up, down_mine, down_theirs = weights
    width, hidden = gate.shape
    half = width // 2
    rows, n_blocks = sum(a.shape[0] for a in own), len(own)
    first = own[0].shape[0]
    products = [in_vmem((padded(rows), hidden), jnp.float32)] * 2
    outs = [in_vmem((first, half)), in_vmem((rows - first, half))]
    x = [pltpu.VMEM((padded(rows), half), jnp.bfloat16)]
    flops = 2 * padded(rows) * hidden * width
    gated, lifted = call(functools.partial(first_kernel, n_blocks), place, (*own, gate, up), products, x, flops)
    units, *theirs = call(
        functools.partial(second_kernel, n_blocks, n_experts),
        place,
        (*own, *across, gated, lifted, gate, up, down_theirs),
        [in_vmem((padded(rows), hidden)), *outs],
        x,
        flops + flops // 2,
    )
    theirs = [swap(a) for a in theirs]
    mine = call(
        functools.partial(third_kernel, n_blocks, n_experts),
        place,
        (*own, units, down_mine),
        outs,
        [],
        flops // 2,
    )
    return mine, theirs


def add_kernel(*refs):
    *terms, out = refs
    out[...] = sum(t[...].astype(jnp.float32) for t in terms).astype(out.dtype)


def add(*terms):
    vmem = pl.BlockSpec(memory_space=pltpu.VMEM)
    return pl.pallas_call(
        add_kernel,
        out_shape=in_vmem(terms[0].shape),
        in_specs=[vmem] * len(terms),
        out_specs=vmem,
        cost_estimate=pl.CostEstimate(flops=0, bytes_accessed=12 << 20, transcendentals=0),
    )(*[hold(t) for t in terms])


def ring_body(tokens, expert_ids, gate_probs, w_gate, w_up, w_down):
    n = lax.axis_size("ep")
    rows = tokens.shape[0]
    order = list(range(0, n, 2)) + list(range(n - 1, 0, -2))
    ahead = [(order[i], order[(i + 1) % n]) for i in range(n)]
    back = [(b, a) for a, b in ahead]
    swap = functools.partial(lax.ppermute, axis_name="tp", perm=[(0, 1), (1, 0)])
    far = n // 2
    place = jnp.stack([lax.axis_index("tp"), lax.axis_index("ep")]).astype(jnp.int32)
    packed = pack(tokens, expert_ids, gate_probs, n)
    gate, up = turn_weights(after(place, packed), w_gate[0].T, w_up[0].T)

    came, across, value, parts = {0: packed}, {}, {}, {}

    def run(keys, wait_for=None):
        at = place if wait_for is None else after(place, wait_for)
        mine, theirs = run_expert(at, [came[k] for k in keys], [across[k] for k in keys], weights, n)
        return [(keys[2 * i : 2 * i + 2], *pair) for i, pair in enumerate(zip(mine, theirs))]

    def keep(keys, mine, theirs):
        pairs = ((mine, theirs), lax.optimization_barrier((mine, theirs)))
        start = 0
        for i, k in enumerate(keys):
            mine, theirs = pairs[i % 2]
            span = slice(start, start + came[k].shape[0])
            start = span.stop
            parts[k] = mine[span], theirs[span]
            value[k] = mine[span].astype(jnp.float32) + theirs[span].astype(jnp.float32)

    came[1] = lax.ppermute(packed, "ep", ahead)
    came[-1] = lax.ppermute(packed, "ep", back)
    weights, done, near = [gate, up], up, []
    for k in range(2, far + 1):
        came[k - 1], came[1 - k] = after(came[k - 1], done), after(came[1 - k], done)
        came[k] = lax.ppermute(came[k - 1], "ep", ahead)
        if k < far:
            came[-k] = lax.ppermute(came[1 - k], "ep", back)
        across[k - 1], across[1 - k] = swap(came[k - 1]), swap(came[1 - k])
        if k == 2:
            weights += halve_weights(after(place, came[1]), w_down[0])
            done = weights[-1]
        else:
            near += run([k - 2, 2 - k])
            done = near[-1][-1]
    came[far] = after(came[far], done)
    across[far] = swap(came[far])
    across[0] = swap(after(packed, came[far]))
    last = [far, far - 1, 1 - far]
    for keys, mine, theirs in zip(([far], last[1:]), *run_expert_in_stages(place, [came[k] for k in last], [across[k] for k in last], swap, weights, n)):
        keep(keys, mine, theirs)
    for keys, mine, theirs in near:
        keep(keys, mine, swap(after(theirs, value[far])))

    to_ahead = value[far].astype(jnp.bfloat16)
    to_back = (value[far - 1]).astype(jnp.bfloat16)
    for k in range(far - 1, -1, -1):
        behind = lax.ppermute(to_ahead, "ep", ahead)
        if k == far - 1:
            ((keys, mine, done),) = run([0], to_ahead)
            keep(keys, mine, swap(done))
        else:
            to_back = done = add(*parts[k], after(front, to_ahead))
        if k:
            front = lax.ppermute(to_back, "ep", back)
            to_ahead = (value[-k] + after(behind, done).astype(jnp.float32)).astype(jnp.bfloat16)
    return (to_back.astype(jnp.float32) + behind.astype(jnp.float32)).astype(jnp.bfloat16)


def swiglu_expert(rows, gate_part, up_part, down_part):
    gated = jnp.dot(rows, gate_part, preferred_element_type=jnp.float32)
    lifted = jnp.dot(rows, up_part, preferred_element_type=jnp.float32)
    hidden = (jax.nn.silu(gated) * lifted).astype(jnp.bfloat16)
    return jnp.dot(hidden, down_part, preferred_element_type=jnp.float32)


def slot_table(expert_ids, n_experts):
    routed = expert_ids.reshape(-1)
    pair_count = routed.shape[0]
    onehot = (routed[:, None] == jnp.arange(n_experts, dtype=jnp.int32)[None, :]).astype(
        jnp.bfloat16
    )
    row_index = lax.broadcasted_iota(jnp.int32, (pair_count, pair_count), 0)
    col_index = lax.broadcasted_iota(jnp.int32, (pair_count, pair_count), 1)
    earlier = (row_index > col_index).astype(jnp.bfloat16)
    before = jnp.dot(earlier, onehot, preferred_element_type=jnp.float32)
    slots = jnp.sum(before * onehot.astype(jnp.float32), axis=1).astype(jnp.int32)
    return (routed, slots)


def slot_body(tokens, expert_ids, gate_probs, w_gate, w_up, w_down):
    n_experts = lax.axis_size("ep")
    tok_rows, top_count = expert_ids.shape
    capacity = 3 * tok_rows * top_count // (2 * n_experts)
    routed, slots = slot_table(expert_ids, n_experts)
    positions = routed * capacity + slots
    pair_token = jnp.repeat(jnp.arange(tok_rows, dtype=jnp.int32), top_count)
    buffer_rows = n_experts * capacity
    owners = jnp.full((buffer_rows,), tok_rows, jnp.int32).at[positions].set(pair_token)
    half_slots = capacity // 2
    whole_tokens = lax.all_gather(tokens, "tp", axis=1, tiled=True)
    width = whole_tokens.shape[1]
    gate_full, up_full = (
        lax.all_gather(w_gate, "tp", axis=2, tiled=True),
        lax.all_gather(w_up, "tp", axis=2, tiled=True),
    )
    down_full = lax.all_gather(w_down, "tp", axis=1, tiled=True)
    padded = jnp.concatenate([whole_tokens, jnp.zeros((1, width), whole_tokens.dtype)], 0)
    outgoing = padded[owners].reshape(n_experts, capacity, width)
    lane = lax.axis_index("tp")
    mine = lax.dynamic_slice_in_dim(outgoing, lane * half_slots, half_slots, 1)
    block = lax.all_to_all(mine, "ep", split_axis=0, concat_axis=0, tiled=True)
    sources, items, columns = block.shape
    result = swiglu_expert(
        block.reshape(sources * items, columns), gate_full[0], up_full[0], down_full[0]
    )
    result = result.astype(jnp.bfloat16).reshape(sources, items, columns)
    returned = lax.all_to_all(result, "ep", split_axis=0, concat_axis=0, tiled=True)
    received = returned.reshape(n_experts * half_slots, width)
    in_half = slots // half_slots == lane
    local_pos = routed * half_slots + slots % half_slots
    picked = received[local_pos].astype(jnp.float32).reshape(tok_rows, top_count, width)
    weighted = jnp.where(in_half.reshape(tok_rows, top_count), gate_probs, 0.0)
    partial_value = jnp.sum(weighted[:, :, None] * picked, axis=1)
    return lax.psum_scatter(partial_value, "tp", scatter_dimension=1, tiled=True).astype(
        jnp.bfloat16
    )


def solution(mesh):
    in_specs = (
        P(("groups", "ep"), "tp"),
        P(("groups", "ep"), None),
        P(("groups", "ep"), None),
        P("ep", None, "tp"),
        P("ep", None, "tp"),
        P("ep", "tp", None),
    )
    out_specs = P(("groups", "ep"), "tp")

    def body(tokens, expert_ids, *rest):
        n, top = lax.axis_size("ep"), expert_ids.shape[1]
        small = n <= 4 * top and n % 2 == 0 and n >= 6 and lax.axis_size("tp") == 2
        return (ring_body if small else slot_body)(tokens, expert_ids, *rest)

    return jax.shard_map(body, mesh=mesh, in_specs=in_specs, out_specs=out_specs, check_vma=False)
```

```python
import functools

import jax
import jax.numpy as jnp
from jax import lax
from jax.experimental import pallas as pl
from jax.experimental.pallas import tpu as pltpu
from jax.sharding import PartitionSpec as P

SPLITS = 3


def in_vmem(shape, dtype=jnp.bfloat16):
    return pltpu.MemorySpace.VMEM(shape, dtype)


def hold(x):
    return pltpu.with_memory_space_constraint(x, pltpu.VMEM)


def after(x, done):
    return lax.optimization_barrier((x, done))[0]


def tiles_of(rows, columns):
    whole, rest = divmod(columns, 128)
    parts = 1
    while rest and 128 // (2 * parts) >= rest and rows % (32 * parts) == 0:
        parts *= 2
    return whole, rest, parts, whole * rows + (rows // parts if rest else 0)


def tile_places(rows, columns):
    whole, rest, parts, size = tiles_of(rows, columns)
    for j in range(whole):
        yield slice(0, rows), slice(128 * j, 128 * j + 128), slice(j * rows, (j + 1) * rows), slice(0, 128)
    for q in range(parts if rest else 0):
        share, lane = rows // parts, q * (128 // parts)
        yield slice(q * share, (q + 1) * share), slice(128 * whole, columns), slice(whole * rows, size), slice(lane, lane + rest)


def pack_kernel(n_experts, tokens_in, ids_in, probs_in, packed, tokens, ids, probs, sems):
    copies = [
        pltpu.make_async_copy(src, dst, sems.at[i])
        for i, (src, dst) in enumerate(((ids_in, ids), (probs_in, probs), (tokens_in, tokens)))
    ]
    for copy in copies:
        copy.start()
    top, rows = ids.shape
    half = tokens.shape[1]
    copies[0].wait()
    copies[1].wait()
    expert = lax.broadcasted_iota(jnp.int32, (n_experts, rows), 0)
    rest = jnp.zeros((n_experts, rows), jnp.float32)
    for k in range(top):
        rest += jnp.where(ids[k : k + 1, :] == expert, probs[k : k + 1, :], 0.0)
    terms = []
    for _ in range(SPLITS):
        term = rest.astype(jnp.bfloat16).astype(jnp.float32)
        terms.append(term)
        rest = rest - term
    terms = jnp.concatenate(terms, axis=0).T.astype(jnp.bfloat16)
    copies[2].wait()
    for r, c, at, lanes in tile_places(rows, half + terms.shape[1]):
        if c.stop <= half:
            packed[at, lanes] = tokens[r, c]
        else:
            split = lanes.start + half - c.start
            packed[at, lanes.start : split] = tokens[r, c.start : half]
            packed[at, split : lanes.stop] = terms[r, :]


def pack(tokens, expert_ids, gate_probs, n_experts):
    rows, half = tokens.shape
    args = (tokens, expert_ids.T, gate_probs.T)
    return pl.pallas_call(
        functools.partial(pack_kernel, n_experts),
        out_shape=in_vmem((tiles_of(rows, half + SPLITS * n_experts)[-1], 128)),
        in_specs=[pl.BlockSpec(memory_space=pltpu.HBM)] * 3,
        out_specs=pl.BlockSpec(memory_space=pltpu.VMEM),
        scratch_shapes=[pltpu.VMEM(a.shape, a.dtype) for a in args] + [pltpu.SemaphoreType.DMA((3,))],
        compiler_params=pltpu.CompilerParams(vmem_limit_bytes=8 << 20),
    )(*[pltpu.with_memory_space_constraint(a, pltpu.HBM) for a in args])


def pieces(hidden):
    first = -(-hidden // 256) * 128
    return ((0, first), (first, hidden))


def turn_kernel(after_this, gate_in, up_in, gate, up, gate_buf, up_buf, sems):
    steps = []
    for i, (src, buf, out) in enumerate(((gate_in, gate_buf, gate), (up_in, up_buf, up))):
        for j, (start, stop) in enumerate(pieces(src.shape[0])):
            span = pl.ds(start, stop - start)
            steps.append((pltpu.make_async_copy(src.at[span], buf.at[span], sems.at[i, j]), buf, out, start, stop))
    for copy, *_ in steps:
        copy.start()
    for copy, buf, out, start, stop in steps:
        copy.wait()
        out[:, start:stop] = buf[start:stop, :].T


def turn_weights(after_this, *weights):
    hidden, width = weights[0].shape
    return pl.pallas_call(
        turn_kernel,
        out_shape=[in_vmem((width, hidden))] * 2,
        in_specs=[pl.BlockSpec(memory_space=pltpu.SMEM)] + [pl.BlockSpec(memory_space=pltpu.HBM)] * 2,
        out_specs=[pl.BlockSpec(memory_space=pltpu.VMEM)] * 2,
        scratch_shapes=[pltpu.VMEM((hidden, width), jnp.bfloat16)] * 2 + [pltpu.SemaphoreType.DMA((2, 2))],
        compiler_params=pltpu.CompilerParams(vmem_limit_bytes=32 << 20),
        cost_estimate=pl.CostEstimate(flops=0, bytes_accessed=8 * hidden * width, transcendentals=0),
    )(after_this, *[pltpu.with_memory_space_constraint(w, pltpu.HBM) for w in weights])


def halve_kernel(place, down_in, down_mine, down_theirs, down_buf, sems):
    lane = place[0]
    half = down_mine.shape[1]
    spans = [slice(start, stop) for start, stop in pieces(down_in.shape[0])]
    copies = [
        pltpu.make_async_copy(down_in.at[pl.ds(s.start, s.stop - s.start)], down_buf.at[pl.ds(s.start, s.stop - s.start)], sems.at[i])
        for i, s in enumerate(spans)
    ]
    for copy in copies:
        copy.start()
    for copy, s in zip(copies, spans):
        copy.wait()

        @pl.when(lane == 0)
        def _():
            down_mine[s, :] = down_buf[s, :half]
            down_theirs[s, :] = down_buf[s, half:]

        @pl.when(lane != 0)
        def _():
            down_mine[s, :] = down_buf[s, half:]
            down_theirs[s, :] = down_buf[s, :half]


def halve_weights(place, w_down):
    hidden, width = w_down.shape
    return pl.pallas_call(
        halve_kernel,
        out_shape=[in_vmem((hidden, width // 2))] * 2,
        in_specs=[pl.BlockSpec(memory_space=pltpu.SMEM), pl.BlockSpec(memory_space=pltpu.HBM)],
        out_specs=[pl.BlockSpec(memory_space=pltpu.VMEM)] * 2,
        scratch_shapes=[pltpu.VMEM((hidden, width), jnp.bfloat16), pltpu.SemaphoreType.DMA((2,))],
        compiler_params=pltpu.CompilerParams(vmem_limit_bytes=32 << 20),
        cost_estimate=pl.CostEstimate(flops=0, bytes_accessed=8 * hidden * width, transcendentals=0),
    )(place, pltpu.with_memory_space_constraint(w_down, pltpu.HBM))


def gather_rows(blocks, x, rows, columns):
    half = x.shape[1]
    for i, block in enumerate(blocks):
        for r, c, at, lanes in tile_places(rows, columns):
            stop = min(c.stop, half)
            x[i * rows + r.start : i * rows + r.stop, c.start : stop] = block[at, lanes.start : lanes.start + stop - c.start]
    start = len(blocks) * rows
    if start < x.shape[0]:
        x[start:, :] = jnp.zeros((x.shape[0] - start, half), x.dtype)


def project(x, lane, w):
    half = x.shape[1]
    return jnp.dot(x[...], w[pl.ds(pl.multiple_of(lane * half, 16), half), :], preferred_element_type=jnp.float32)


def activate(gated, lifted):
    return (gated / (1.0 + jnp.exp(-gated)) * lifted).astype(jnp.bfloat16)


def gate_weights(blocks, half, expert, n_experts, rows):
    columns = half + SPLITS * n_experts
    weights = []
    for block in blocks:
        pieces = []
        for _, c, at, lanes in tile_places(rows, columns):
            if c.stop == columns:
                terms = block[at, lanes.start + half - c.start : lanes.stop].astype(jnp.float32)
                column = lax.broadcasted_iota(jnp.int32, terms.shape, 1)
                pieces.append(jnp.sum(jnp.where(lax.rem(column, n_experts) == expert, terms, 0.0), axis=1, keepdims=True))
        weights.append(jnp.concatenate(pieces, axis=0))
    return weights


def lower(hidden, w, weights, *outs):
    value = jnp.dot(hidden, w[...], preferred_element_type=jnp.float32)
    rows, half = weights[0].shape[0], w.shape[1]
    size = tiles_of(rows, half)[-1]
    places = [(out, start) for out in outs for start in range(0, out.shape[0], size)]
    for i, (weight, (out, start)) in enumerate(zip(weights, places)):
        scaled = (value[i * rows : (i + 1) * rows] * weight).astype(jnp.bfloat16)
        for r, c, at, lanes in tile_places(rows, half):
            out[start + at.start : start + at.stop, lanes] = scaled[r, c]


def expert_kernel(n_blocks, n_experts, rows, place, *refs):
    own, across = refs[:n_blocks], refs[n_blocks : 2 * n_blocks]
    w_gate, w_up, down_mine, down_theirs, *outs, x_own, x_across = refs[2 * n_blocks :]
    lane, expert = place[0], place[1]
    half = x_own.shape[1]
    columns = half + SPLITS * n_experts
    gather_rows(own, x_own, rows, columns)
    gather_rows(across, x_across, rows, columns)
    gated = project(x_own, lane, w_gate) + project(x_across, 1 - lane, w_gate)
    lifted = project(x_own, lane, w_up) + project(x_across, 1 - lane, w_up)
    hidden = activate(gated, lifted)
    weights = gate_weights(own, half, expert, n_experts, rows)
    mine, theirs = outs[: len(outs) // 2], outs[len(outs) // 2 :]
    lower(hidden, down_theirs, weights, *theirs)
    lower(hidden, down_mine, weights, *mine)


def first_kernel(n_blocks, n_experts, rows, place, *refs):
    own = refs[:n_blocks]
    w_gate, w_up, gated, lifted, x = refs[n_blocks:]
    gather_rows(own, x, rows, x.shape[1] + SPLITS * n_experts)
    gated[...] = project(x, place[0], w_gate)
    lifted[...] = project(x, place[0], w_up)


def second_kernel(n_blocks, n_experts, rows, place, *refs):
    own, across = refs[:n_blocks], refs[n_blocks : 2 * n_blocks]
    gated, lifted, w_gate, w_up, down_theirs, hidden, *theirs, x = refs[2 * n_blocks :]
    half = x.shape[1]
    gather_rows(across, x, rows, half + SPLITS * n_experts)
    there = 1 - place[0]
    hidden[...] = activate(gated[...] + project(x, there, w_gate), lifted[...] + project(x, there, w_up))
    lower(hidden[...], down_theirs, gate_weights(own, half, place[1], n_experts, rows), *theirs)


def third_kernel(n_blocks, n_experts, rows, place, *refs):
    own = refs[:n_blocks]
    hidden, down_mine, *mine = refs[n_blocks:]
    lower(hidden[...], down_mine, gate_weights(own, down_mine.shape[1], place[1], n_experts, rows), *mine)


def call(kernel, place, args, out_shape, scratch_shapes, flops):
    vmem = pl.BlockSpec(memory_space=pltpu.VMEM)
    return pl.pallas_call(
        kernel,
        out_shape=out_shape,
        in_specs=[pl.BlockSpec(memory_space=pltpu.SMEM)] + [vmem] * len(args),
        out_specs=[vmem] * len(out_shape),
        scratch_shapes=scratch_shapes,
        compiler_params=pltpu.CompilerParams(vmem_limit_bytes=16 << 20),
        cost_estimate=pl.CostEstimate(flops=flops, bytes_accessed=flops // 128, transcendentals=0),
    )(place, *[hold(a) for a in args])


def padded(rows):
    return max(rows, 128)


def run_expert(place, own, across, weights, n_experts, block_rows):
    width, hidden = weights[0].shape
    half = width // 2
    rows, pairs = len(own) * block_rows, max(1, len(own) // 2)
    outs = call(
        functools.partial(expert_kernel, len(own), n_experts, block_rows),
        place,
        (*own, *across, *weights),
        [in_vmem((len(own) // pairs * tiles_of(block_rows, half)[-1], 128))] * (2 * pairs),
        [pltpu.VMEM((padded(rows), half), jnp.bfloat16)] * 2,
        6 * padded(rows) * hidden * width,
    )
    return outs[:pairs], outs[pairs:]


def run_expert_in_stages(place, own, across, swap, weights, n_experts, block_rows):
    gate, up, down_mine, down_theirs = weights
    width, hidden = gate.shape
    half = width // 2
    n_blocks = len(own)
    rows, size = n_blocks * block_rows, tiles_of(block_rows, half)[-1]
    products = [in_vmem((padded(rows), hidden), jnp.float32)] * 2
    outs = [in_vmem((size, 128)), in_vmem(((n_blocks - 1) * size, 128))]
    x = [pltpu.VMEM((padded(rows), half), jnp.bfloat16)]
    flops = 2 * padded(rows) * hidden * width
    gated, lifted = call(functools.partial(first_kernel, n_blocks, n_experts, block_rows), place, (*own, gate, up), products, x, flops)
    units, *theirs = call(
        functools.partial(second_kernel, n_blocks, n_experts, block_rows),
        place,
        (*own, *across, gated, lifted, gate, up, down_theirs),
        [in_vmem((padded(rows), hidden)), *outs],
        x,
        flops + flops // 2,
    )
    theirs = [swap(a) for a in theirs]
    mine = call(
        functools.partial(third_kernel, n_blocks, n_experts, block_rows),
        place,
        (*own, units, down_mine),
        outs,
        [],
        flops // 2,
    )
    return mine, theirs


def add_kernel(*refs):
    *terms, out = refs
    out[...] = sum(t[...].astype(jnp.float32) for t in terms).astype(out.dtype)


def add(*terms):
    vmem = pl.BlockSpec(memory_space=pltpu.VMEM)
    return pl.pallas_call(
        add_kernel,
        out_shape=in_vmem(terms[0].shape),
        in_specs=[vmem] * len(terms),
        out_specs=vmem,
        cost_estimate=pl.CostEstimate(flops=0, bytes_accessed=12 << 20, transcendentals=0),
    )(*[hold(t) for t in terms])


def finish_kernel(a, b, out):
    rows, half = out.shape
    for r, c, at, lanes in tile_places(rows, half):
        total = a[at, lanes].astype(jnp.float32) + b[at, lanes].astype(jnp.float32)
        out[r, c] = total.astype(out.dtype)


def finish(a, b, rows, half):
    vmem = pl.BlockSpec(memory_space=pltpu.VMEM)
    return pl.pallas_call(
        finish_kernel,
        out_shape=jax.ShapeDtypeStruct((rows, half), jnp.bfloat16),
        in_specs=[vmem] * 2,
        out_specs=vmem,
    )(hold(a), hold(b))


def ring_body(tokens, expert_ids, gate_probs, w_gate, w_up, w_down):
    n = lax.axis_size("ep")
    rows, half = tokens.shape
    size = tiles_of(rows, half)[-1]
    order = list(range(0, n, 2)) + list(range(n - 1, 0, -2))
    ahead = [(order[i], order[(i + 1) % n]) for i in range(n)]
    back = [(b, a) for a, b in ahead]
    swap = functools.partial(lax.ppermute, axis_name="tp", perm=[(0, 1), (1, 0)])
    far = n // 2
    place = jnp.stack([lax.axis_index("tp"), lax.axis_index("ep")]).astype(jnp.int32)
    packed = pack(tokens, expert_ids, gate_probs, n)
    gate, up = turn_weights(after(place, packed), w_gate[0].T, w_up[0].T)

    came, across, value, parts = {0: packed}, {}, {}, {}

    def run(keys, wait_for=None):
        at = place if wait_for is None else after(place, wait_for)
        mine, theirs = run_expert(at, [came[k] for k in keys], [across[k] for k in keys], weights, n, rows)
        return [(keys[2 * i : 2 * i + 2], *pair) for i, pair in enumerate(zip(mine, theirs))]

    def keep(keys, mine, theirs):
        pairs = ((mine, theirs), lax.optimization_barrier((mine, theirs)))
        start = 0
        for i, k in enumerate(keys):
            mine, theirs = pairs[i % 2]
            span = slice(start, start + size)
            start = span.stop
            parts[k] = mine[span], theirs[span]
            value[k] = mine[span].astype(jnp.float32) + theirs[span].astype(jnp.float32)

    came[1] = lax.ppermute(packed, "ep", ahead)
    came[-1] = lax.ppermute(packed, "ep", back)
    weights, done, near = [gate, up], up, []
    for k in range(2, far + 1):
        came[k - 1], came[1 - k] = after(came[k - 1], done), after(came[1 - k], done)
        came[k] = lax.ppermute(came[k - 1], "ep", ahead)
        if k < far:
            came[-k] = lax.ppermute(came[1 - k], "ep", back)
        across[k - 1], across[1 - k] = swap(came[k - 1]), swap(came[1 - k])
        if k == 2:
            weights += halve_weights(after(place, came[1]), w_down[0])
            done = weights[-1]
        else:
            near += run([k - 2, 2 - k])
            done = near[-1][-1]
    came[far] = after(came[far], done)
    across[far] = swap(came[far])
    across[0] = swap(after(packed, came[far]))
    last = [far, far - 1, 1 - far]
    for keys, mine, theirs in zip(([far], last[1:]), *run_expert_in_stages(place, [came[k] for k in last], [across[k] for k in last], swap, weights, n, rows)):
        keep(keys, mine, theirs)
    for keys, mine, theirs in near:
        keep(keys, mine, swap(after(theirs, value[far])))

    to_ahead = value[far].astype(jnp.bfloat16)
    to_back = (value[far - 1]).astype(jnp.bfloat16)
    for k in range(far - 1, -1, -1):
        behind = lax.ppermute(to_ahead, "ep", ahead)
        if k == far - 1:
            ((keys, mine, done),) = run([0], to_ahead)
            keep(keys, mine, swap(done))
        else:
            to_back = done = add(*parts[k], after(front, to_ahead))
        if k:
            front = lax.ppermute(to_back, "ep", back)
            to_ahead = (value[-k] + after(behind, done).astype(jnp.float32)).astype(jnp.bfloat16)
    return finish(to_back, behind, rows, half)


def swiglu_expert(rows, gate_part, up_part, down_part):
    gated = jnp.dot(rows, gate_part, preferred_element_type=jnp.float32)
    lifted = jnp.dot(rows, up_part, preferred_element_type=jnp.float32)
    hidden = (jax.nn.silu(gated) * lifted).astype(jnp.bfloat16)
    return jnp.dot(hidden, down_part, preferred_element_type=jnp.float32)


def slot_table(expert_ids, n_experts):
    routed = expert_ids.reshape(-1)
    pair_count = routed.shape[0]
    onehot = (routed[:, None] == jnp.arange(n_experts, dtype=jnp.int32)[None, :]).astype(
        jnp.bfloat16
    )
    row_index = lax.broadcasted_iota(jnp.int32, (pair_count, pair_count), 0)
    col_index = lax.broadcasted_iota(jnp.int32, (pair_count, pair_count), 1)
    earlier = (row_index > col_index).astype(jnp.bfloat16)
    before = jnp.dot(earlier, onehot, preferred_element_type=jnp.float32)
    slots = jnp.sum(before * onehot.astype(jnp.float32), axis=1).astype(jnp.int32)
    return (routed, slots)


def slot_body(tokens, expert_ids, gate_probs, w_gate, w_up, w_down):
    n_experts = lax.axis_size("ep")
    tok_rows, top_count = expert_ids.shape
    capacity = 3 * tok_rows * top_count // (2 * n_experts)
    routed, slots = slot_table(expert_ids, n_experts)
    positions = routed * capacity + slots
    pair_token = jnp.repeat(jnp.arange(tok_rows, dtype=jnp.int32), top_count)
    buffer_rows = n_experts * capacity
    owners = jnp.full((buffer_rows,), tok_rows, jnp.int32).at[positions].set(pair_token)
    half_slots = capacity // 2
    whole_tokens = lax.all_gather(tokens, "tp", axis=1, tiled=True)
    width = whole_tokens.shape[1]
    gate_full, up_full = (
        lax.all_gather(w_gate, "tp", axis=2, tiled=True),
        lax.all_gather(w_up, "tp", axis=2, tiled=True),
    )
    down_full = lax.all_gather(w_down, "tp", axis=1, tiled=True)
    padded = jnp.concatenate([whole_tokens, jnp.zeros((1, width), whole_tokens.dtype)], 0)
    outgoing = padded[owners].reshape(n_experts, capacity, width)
    lane = lax.axis_index("tp")
    mine = lax.dynamic_slice_in_dim(outgoing, lane * half_slots, half_slots, 1)
    block = lax.all_to_all(mine, "ep", split_axis=0, concat_axis=0, tiled=True)
    sources, items, columns = block.shape
    result = swiglu_expert(
        block.reshape(sources * items, columns), gate_full[0], up_full[0], down_full[0]
    )
    result = result.astype(jnp.bfloat16).reshape(sources, items, columns)
    returned = lax.all_to_all(result, "ep", split_axis=0, concat_axis=0, tiled=True)
    received = returned.reshape(n_experts * half_slots, width)
    in_half = slots // half_slots == lane
    local_pos = routed * half_slots + slots % half_slots
    picked = received[local_pos].astype(jnp.float32).reshape(tok_rows, top_count, width)
    weighted = jnp.where(in_half.reshape(tok_rows, top_count), gate_probs, 0.0)
    partial_value = jnp.sum(weighted[:, :, None] * picked, axis=1)
    return lax.psum_scatter(partial_value, "tp", scatter_dimension=1, tiled=True).astype(
        jnp.bfloat16
    )


def solution(mesh):
    in_specs = (
        P(("groups", "ep"), "tp"),
        P(("groups", "ep"), None),
        P(("groups", "ep"), None),
        P("ep", None, "tp"),
        P("ep", None, "tp"),
        P("ep", "tp", None),
    )
    out_specs = P(("groups", "ep"), "tp")

    def body(tokens, expert_ids, *rest):
        n, top = lax.axis_size("ep"), expert_ids.shape[1]
        small = n <= 4 * top and n % 2 == 0 and n >= 8 and lax.axis_size("tp") == 2 and tokens.shape[1] % 128 + SPLITS * n <= 128
        return (ring_body if small else slot_body)(tokens, expert_ids, *rest)

    return jax.shard_map(body, mesh=mesh, in_specs=in_specs, out_specs=out_specs, check_vma=False)
```

```python
import functools

import jax
import jax.numpy as jnp
from jax import lax
from jax.experimental import pallas as pl
from jax.experimental.pallas import tpu as pltpu
from jax.sharding import PartitionSpec as P

SPLITS = 3


def in_vmem(shape, dtype=jnp.bfloat16):
    return pltpu.MemorySpace.VMEM(shape, dtype)


def hold(x):
    return pltpu.with_memory_space_constraint(x, pltpu.VMEM)


def after(x, done):
    return lax.optimization_barrier((x, done))[0]


def tiles_of(rows, columns):
    whole, rest = divmod(columns, 128)
    parts = 1
    while rest and 128 // (2 * parts) >= rest and rows % (32 * parts) == 0:
        parts *= 2
    return whole, rest, parts, whole * rows + (rows // parts if rest else 0)


def tile_places(rows, columns):
    whole, rest, parts, size = tiles_of(rows, columns)
    for j in range(whole):
        yield slice(0, rows), slice(128 * j, 128 * j + 128), slice(j * rows, (j + 1) * rows), slice(0, 128)
    for q in range(parts if rest else 0):
        share, lane = rows // parts, q * (128 // parts)
        yield slice(q * share, (q + 1) * share), slice(128 * whole, columns), slice(whole * rows, size), slice(lane, lane + rest)


def pack_kernel(n_experts, tokens_in, ids_in, probs_in, packed, tokens, ids, probs, sems):
    copies = [
        pltpu.make_async_copy(src, dst, sems.at[i])
        for i, (src, dst) in enumerate(((ids_in, ids), (probs_in, probs), (tokens_in, tokens)))
    ]
    for copy in copies:
        copy.start()
    top, rows = ids.shape
    half = tokens.shape[1]
    copies[0].wait()
    copies[1].wait()
    expert = lax.broadcasted_iota(jnp.int32, (n_experts, rows), 0)
    rest = jnp.zeros((n_experts, rows), jnp.float32)
    for k in range(top):
        rest += jnp.where(ids[k : k + 1, :] == expert, probs[k : k + 1, :], 0.0)
    terms = []
    for _ in range(SPLITS):
        term = rest.astype(jnp.bfloat16).astype(jnp.float32)
        terms.append(term)
        rest = rest - term
    terms = jnp.concatenate(terms, axis=0).T.astype(jnp.bfloat16)
    copies[2].wait()
    for r, c, at, lanes in tile_places(rows, half + terms.shape[1]):
        if c.stop <= half:
            packed[at, lanes] = tokens[r, c]
        else:
            split = lanes.start + half - c.start
            packed[at, lanes.start : split] = tokens[r, c.start : half]
            packed[at, split : lanes.stop] = terms[r, :]


def pack(tokens, expert_ids, gate_probs, n_experts):
    rows, half = tokens.shape
    args = (tokens, expert_ids.T, gate_probs.T)
    return pl.pallas_call(
        functools.partial(pack_kernel, n_experts),
        out_shape=in_vmem((tiles_of(rows, half + SPLITS * n_experts)[-1], 128)),
        in_specs=[pl.BlockSpec(memory_space=pltpu.HBM)] * 3,
        out_specs=pl.BlockSpec(memory_space=pltpu.VMEM),
        scratch_shapes=[pltpu.VMEM(a.shape, a.dtype) for a in args] + [pltpu.SemaphoreType.DMA((3,))],
        compiler_params=pltpu.CompilerParams(vmem_limit_bytes=8 << 20),
    )(*[pltpu.with_memory_space_constraint(a, pltpu.HBM) for a in args])


def pieces(hidden):
    first = -(-hidden // 256) * 128
    return ((0, first), (first, hidden))


def turn_kernel(after_this, gate_in, up_in, gate, up, gate_buf, up_buf, sems):
    steps = []
    for i, (src, buf, out) in enumerate(((gate_in, gate_buf, gate), (up_in, up_buf, up))):
        for j, (start, stop) in enumerate(pieces(src.shape[0])):
            span = pl.ds(start, stop - start)
            steps.append((pltpu.make_async_copy(src.at[span], buf.at[span], sems.at[i, j]), buf, out, start, stop))
    for copy, *_ in steps:
        copy.start()
    for copy, buf, out, start, stop in steps:
        copy.wait()
        out[:, start:stop] = buf[start:stop, :].T


def turn_weights(after_this, *weights):
    hidden, width = weights[0].shape
    return pl.pallas_call(
        turn_kernel,
        out_shape=[in_vmem((width, hidden))] * 2,
        in_specs=[pl.BlockSpec(memory_space=pltpu.SMEM)] + [pl.BlockSpec(memory_space=pltpu.HBM)] * 2,
        out_specs=[pl.BlockSpec(memory_space=pltpu.VMEM)] * 2,
        scratch_shapes=[pltpu.VMEM((hidden, width), jnp.bfloat16)] * 2 + [pltpu.SemaphoreType.DMA((2, 2))],
        compiler_params=pltpu.CompilerParams(vmem_limit_bytes=32 << 20),
        cost_estimate=pl.CostEstimate(flops=0, bytes_accessed=8 * hidden * width, transcendentals=0),
    )(after_this, *[pltpu.with_memory_space_constraint(w, pltpu.HBM) for w in weights])


def halve_kernel(place, down_in, down_mine, down_theirs, down_buf, sems):
    lane = place[0]
    half = down_mine.shape[1]
    spans = [slice(start, stop) for start, stop in pieces(down_in.shape[0])]
    copies = [
        pltpu.make_async_copy(down_in.at[pl.ds(s.start, s.stop - s.start)], down_buf.at[pl.ds(s.start, s.stop - s.start)], sems.at[i])
        for i, s in enumerate(spans)
    ]
    for copy in copies:
        copy.start()
    for copy, s in zip(copies, spans):
        copy.wait()

        @pl.when(lane == 0)
        def _():
            down_mine[s, :] = down_buf[s, :half]
            down_theirs[s, :] = down_buf[s, half:]

        @pl.when(lane != 0)
        def _():
            down_mine[s, :] = down_buf[s, half:]
            down_theirs[s, :] = down_buf[s, :half]


def halve_weights(place, w_down):
    hidden, width = w_down.shape
    return pl.pallas_call(
        halve_kernel,
        out_shape=[in_vmem((hidden, width // 2))] * 2,
        in_specs=[pl.BlockSpec(memory_space=pltpu.SMEM), pl.BlockSpec(memory_space=pltpu.HBM)],
        out_specs=[pl.BlockSpec(memory_space=pltpu.VMEM)] * 2,
        scratch_shapes=[pltpu.VMEM((hidden, width), jnp.bfloat16), pltpu.SemaphoreType.DMA((2,))],
        compiler_params=pltpu.CompilerParams(vmem_limit_bytes=32 << 20),
        cost_estimate=pl.CostEstimate(flops=0, bytes_accessed=8 * hidden * width, transcendentals=0),
    )(place, pltpu.with_memory_space_constraint(w_down, pltpu.HBM))


def gather_rows(blocks, x, rows, columns):
    half = x.shape[1]
    for i, block in enumerate(blocks):
        for r, c, at, lanes in tile_places(rows, columns):
            stop = min(c.stop, half)
            x[i * rows + r.start : i * rows + r.stop, c.start : stop] = block[at, lanes.start : lanes.start + stop - c.start]
    start = len(blocks) * rows
    if start < x.shape[0]:
        x[start:, :] = jnp.zeros((x.shape[0] - start, half), x.dtype)


def project(x, lane, w):
    half = x.shape[1]
    return jnp.dot(x[...], w[pl.ds(pl.multiple_of(lane * half, 16), half), :], preferred_element_type=jnp.float32)


def activate(gated, lifted):
    return (gated / (1.0 + jnp.exp(-gated)) * lifted).astype(jnp.bfloat16)


def gate_weights(blocks, half, expert, n_experts, rows):
    columns = half + SPLITS * n_experts
    weights = []
    for block in blocks:
        pieces = []
        for _, c, at, lanes in tile_places(rows, columns):
            if c.stop == columns:
                terms = block[at, lanes.start + half - c.start : lanes.stop].astype(jnp.float32)
                column = lax.broadcasted_iota(jnp.int32, terms.shape, 1)
                pieces.append(jnp.sum(jnp.where(lax.rem(column, n_experts) == expert, terms, 0.0), axis=1, keepdims=True))
        weights.append(jnp.concatenate(pieces, axis=0))
    return weights


def lower(hidden, w, weights, *outs):
    value = jnp.dot(hidden, w[...], preferred_element_type=jnp.float32)
    rows, half = weights[0].shape[0], w.shape[1]
    size = tiles_of(rows, half)[-1]
    places = [(out, start) for out in outs for start in range(0, out.shape[0], size)]
    for i, (weight, (out, start)) in enumerate(zip(weights, places)):
        scaled = (value[i * rows : (i + 1) * rows] * weight).astype(jnp.bfloat16)
        for r, c, at, lanes in tile_places(rows, half):
            out[start + at.start : start + at.stop, lanes] = scaled[r, c]


def expert_kernel(n_blocks, n_experts, rows, place, *refs):
    own, across = refs[:n_blocks], refs[n_blocks : 2 * n_blocks]
    w_gate, w_up, down_mine, down_theirs, *outs, x_own, x_across = refs[2 * n_blocks :]
    lane, expert = place[0], place[1]
    half = x_own.shape[1]
    columns = half + SPLITS * n_experts
    gather_rows(own, x_own, rows, columns)
    gather_rows(across, x_across, rows, columns)
    gated = project(x_own, lane, w_gate) + project(x_across, 1 - lane, w_gate)
    lifted = project(x_own, lane, w_up) + project(x_across, 1 - lane, w_up)
    hidden = activate(gated, lifted)
    weights = gate_weights(own, half, expert, n_experts, rows)
    mine, theirs = outs[: len(outs) // 2], outs[len(outs) // 2 :]
    lower(hidden, down_theirs, weights, *theirs)
    lower(hidden, down_mine, weights, *mine)


def first_kernel(n_blocks, n_experts, rows, place, *refs):
    own = refs[:n_blocks]
    w_gate, w_up, gated, lifted, x = refs[n_blocks:]
    gather_rows(own, x, rows, x.shape[1] + SPLITS * n_experts)
    gated[...] = project(x, place[0], w_gate)
    lifted[...] = project(x, place[0], w_up)


def second_kernel(n_blocks, n_experts, rows, place, *refs):
    own, across = refs[:n_blocks], refs[n_blocks : 2 * n_blocks]
    gated, lifted, w_gate, w_up, down_theirs, hidden, theirs, x = refs[2 * n_blocks :]
    half = x.shape[1]
    gather_rows(across, x, rows, half + SPLITS * n_experts)
    there = 1 - place[0]
    hidden[...] = activate(gated[...] + project(x, there, w_gate), lifted[...] + project(x, there, w_up))
    lower(hidden[:rows], down_theirs, gate_weights(own[:1], half, place[1], n_experts, rows), theirs)


def last_kernel(n_blocks, n_experts, rows, skipped, place, *refs):
    own, hidden = refs[:n_blocks], refs[n_blocks]
    after_downs = n_blocks + 1 + (len(refs) - n_blocks - 1) // 2
    downs, outs = refs[n_blocks + 1 : after_downs], refs[after_downs:]
    units = hidden[skipped * rows : (skipped + n_blocks) * rows]
    for down, out in zip(downs, outs):
        lower(units, down, gate_weights(own, down.shape[1], place[1], n_experts, rows), out)


def call(kernel, place, args, out_shape, scratch_shapes, flops):
    vmem = pl.BlockSpec(memory_space=pltpu.VMEM)
    return pl.pallas_call(
        kernel,
        out_shape=out_shape,
        in_specs=[pl.BlockSpec(memory_space=pltpu.SMEM)] + [vmem] * len(args),
        out_specs=[vmem] * len(out_shape),
        scratch_shapes=scratch_shapes,
        compiler_params=pltpu.CompilerParams(vmem_limit_bytes=16 << 20),
        cost_estimate=pl.CostEstimate(flops=flops, bytes_accessed=flops // 128, transcendentals=0),
    )(place, *[hold(a) for a in args])


def padded(rows):
    return max(rows, 128)


def run_expert(place, own, across, weights, n_experts, block_rows):
    width, hidden = weights[0].shape
    half = width // 2
    rows, pairs = len(own) * block_rows, max(1, len(own) // 2)
    outs = call(
        functools.partial(expert_kernel, len(own), n_experts, block_rows),
        place,
        (*own, *across, *weights),
        [in_vmem((len(own) // pairs * tiles_of(block_rows, half)[-1], 128))] * (2 * pairs),
        [pltpu.VMEM((padded(rows), half), jnp.bfloat16)] * 2,
        6 * padded(rows) * hidden * width,
    )
    return outs[:pairs], outs[pairs:]


def run_expert_in_stages(place, own, across, swap, weights, n_experts, block_rows):
    gate, up, down_mine, down_theirs = weights
    width, hidden = gate.shape
    half = width // 2
    n_blocks = len(own)
    rows, size = n_blocks * block_rows, tiles_of(block_rows, half)[-1]
    products = [in_vmem((padded(rows), hidden), jnp.float32)] * 2
    x = [pltpu.VMEM((padded(rows), half), jnp.bfloat16)]
    flops = 2 * padded(rows) * hidden * width
    gated, lifted = call(functools.partial(first_kernel, n_blocks, n_experts, block_rows), place, (*own, gate, up), products, x, flops)
    units, theirs = call(
        functools.partial(second_kernel, n_blocks, n_experts, block_rows),
        place,
        (*own, *across, gated, lifted, gate, up, down_theirs),
        [in_vmem((padded(rows), hidden)), in_vmem((size, 128))],
        x,
        flops + flops // 2,
    )
    theirs = swap(theirs)
    (mine,) = call(
        functools.partial(last_kernel, 1, n_experts, block_rows, 0), place, (own[0], units, down_mine), [in_vmem((size, 128))], [], flops // 6
    )

    def others(place):
        rest = n_blocks - 1
        return call(
            functools.partial(last_kernel, rest, n_experts, block_rows, 1),
            place,
            (*own[1:], units, down_theirs, down_mine),
            [in_vmem((rest * size, 128))] * 2,
            [],
            flops // 2,
        )

    return mine, theirs, others


def add_kernel(*refs):
    *terms, out = refs
    out[...] = sum(t[...].astype(jnp.float32) for t in terms).astype(out.dtype)


def add(*terms):
    vmem = pl.BlockSpec(memory_space=pltpu.VMEM)
    return pl.pallas_call(
        add_kernel,
        out_shape=in_vmem(terms[0].shape),
        in_specs=[vmem] * len(terms),
        out_specs=vmem,
        cost_estimate=pl.CostEstimate(flops=0, bytes_accessed=12 << 20, transcendentals=0),
    )(*[hold(t) for t in terms])


def finish_kernel(a, b, out):
    rows, half = out.shape
    for r, c, at, lanes in tile_places(rows, half):
        total = a[at, lanes].astype(jnp.float32) + b[at, lanes].astype(jnp.float32)
        out[r, c] = total.astype(out.dtype)


def finish(a, b, rows, half):
    vmem = pl.BlockSpec(memory_space=pltpu.VMEM)
    return pl.pallas_call(
        finish_kernel,
        out_shape=jax.ShapeDtypeStruct((rows, half), jnp.bfloat16),
        in_specs=[vmem] * 2,
        out_specs=vmem,
    )(hold(a), hold(b))


def ring_body(tokens, expert_ids, gate_probs, w_gate, w_up, w_down):
    n = lax.axis_size("ep")
    rows, half = tokens.shape
    size = tiles_of(rows, half)[-1]
    order = list(range(0, n, 2)) + list(range(n - 1, 0, -2))
    ahead = [(order[i], order[(i + 1) % n]) for i in range(n)]
    back = [(b, a) for a, b in ahead]
    swap = functools.partial(lax.ppermute, axis_name="tp", perm=[(0, 1), (1, 0)])
    far = n // 2
    place = jnp.stack([lax.axis_index("tp"), lax.axis_index("ep")]).astype(jnp.int32)
    packed = pack(tokens, expert_ids, gate_probs, n)
    gate, up = turn_weights(after(place, packed), w_gate[0].T, w_up[0].T)

    came, across, value, parts = {0: packed}, {}, {}, {}

    def run(keys, wait_for=None):
        at = place if wait_for is None else after(place, wait_for)
        mine, theirs = run_expert(at, [came[k] for k in keys], [across[k] for k in keys], weights, n, rows)
        return [(keys[2 * i : 2 * i + 2], *pair) for i, pair in enumerate(zip(mine, theirs))]

    def keep(keys, mine, theirs):
        pairs = ((mine, theirs), lax.optimization_barrier((mine, theirs)))
        start = 0
        for i, k in enumerate(keys):
            mine, theirs = pairs[i % 2]
            span = slice(start, start + size)
            start = span.stop
            parts[k] = mine[span], theirs[span]
            value[k] = mine[span].astype(jnp.float32) + theirs[span].astype(jnp.float32)

    came[1] = lax.ppermute(packed, "ep", ahead)
    came[-1] = lax.ppermute(packed, "ep", back)
    weights, done, near = [gate, up], up, []
    for k in range(2, far + 1):
        came[k - 1], came[1 - k] = after(came[k - 1], done), after(came[1 - k], done)
        came[k] = lax.ppermute(came[k - 1], "ep", ahead)
        if k < far:
            came[-k] = lax.ppermute(came[1 - k], "ep", back)
        across[k - 1], across[1 - k] = swap(came[k - 1]), swap(came[1 - k])
        if k == 2:
            weights += halve_weights(after(place, came[1]), w_down[0])
            done = weights[-1]
        else:
            near += run([k - 2, 2 - k])
            done = near[-1][-1]
    came[far] = after(came[far], done)
    across[far] = swap(came[far])
    across[0] = swap(after(packed, came[far]))
    last = [far, far - 1, 1 - far]
    mine, theirs, others = run_expert_in_stages(place, [came[k] for k in last], [across[k] for k in last], swap, weights, n, rows)
    keep([far], mine, theirs)
    theirs, mine = others(after(place, value[far]))
    quarter = theirs.shape[0] // 4
    keep(last[1:], mine, jnp.concatenate([swap(theirs[i * quarter : (i + 1) * quarter]) for i in range(4)], axis=0))
    for keys, mine, theirs in near:
        keep(keys, mine, swap(after(theirs, value[far])))

    to_ahead = value[far].astype(jnp.bfloat16)
    to_back = (value[far - 1]).astype(jnp.bfloat16)
    for k in range(far - 1, -1, -1):
        behind = lax.ppermute(to_ahead, "ep", ahead)
        if k == far - 1:
            ((keys, mine, done),) = run([0], to_ahead)
            keep(keys, mine, swap(done))
        else:
            to_back = done = add(*parts[k], after(front, to_ahead))
        if k:
            front = lax.ppermute(to_back, "ep", back)
            to_ahead = (value[-k] + after(behind, done).astype(jnp.float32)).astype(jnp.bfloat16)
    return finish(to_back, behind, rows, half)


def swiglu_expert(rows, gate_part, up_part, down_part):
    gated = jnp.dot(rows, gate_part, preferred_element_type=jnp.float32)
    lifted = jnp.dot(rows, up_part, preferred_element_type=jnp.float32)
    hidden = (jax.nn.silu(gated) * lifted).astype(jnp.bfloat16)
    return jnp.dot(hidden, down_part, preferred_element_type=jnp.float32)


def slot_table(expert_ids, n_experts):
    routed = expert_ids.reshape(-1)
    pair_count = routed.shape[0]
    onehot = (routed[:, None] == jnp.arange(n_experts, dtype=jnp.int32)[None, :]).astype(
        jnp.bfloat16
    )
    row_index = lax.broadcasted_iota(jnp.int32, (pair_count, pair_count), 0)
    col_index = lax.broadcasted_iota(jnp.int32, (pair_count, pair_count), 1)
    earlier = (row_index > col_index).astype(jnp.bfloat16)
    before = jnp.dot(earlier, onehot, preferred_element_type=jnp.float32)
    slots = jnp.sum(before * onehot.astype(jnp.float32), axis=1).astype(jnp.int32)
    return (routed, slots)


def slot_body(tokens, expert_ids, gate_probs, w_gate, w_up, w_down):
    n_experts = lax.axis_size("ep")
    tok_rows, top_count = expert_ids.shape
    capacity = 3 * tok_rows * top_count // (2 * n_experts)
    routed, slots = slot_table(expert_ids, n_experts)
    positions = routed * capacity + slots
    pair_token = jnp.repeat(jnp.arange(tok_rows, dtype=jnp.int32), top_count)
    buffer_rows = n_experts * capacity
    owners = jnp.full((buffer_rows,), tok_rows, jnp.int32).at[positions].set(pair_token)
    half_slots = capacity // 2
    whole_tokens = lax.all_gather(tokens, "tp", axis=1, tiled=True)
    width = whole_tokens.shape[1]
    gate_full, up_full = (
        lax.all_gather(w_gate, "tp", axis=2, tiled=True),
        lax.all_gather(w_up, "tp", axis=2, tiled=True),
    )
    down_full = lax.all_gather(w_down, "tp", axis=1, tiled=True)
    padded = jnp.concatenate([whole_tokens, jnp.zeros((1, width), whole_tokens.dtype)], 0)
    outgoing = padded[owners].reshape(n_experts, capacity, width)
    lane = lax.axis_index("tp")
    mine = lax.dynamic_slice_in_dim(outgoing, lane * half_slots, half_slots, 1)
    block = lax.all_to_all(mine, "ep", split_axis=0, concat_axis=0, tiled=True)
    sources, items, columns = block.shape
    result = swiglu_expert(
        block.reshape(sources * items, columns), gate_full[0], up_full[0], down_full[0]
    )
    result = result.astype(jnp.bfloat16).reshape(sources, items, columns)
    returned = lax.all_to_all(result, "ep", split_axis=0, concat_axis=0, tiled=True)
    received = returned.reshape(n_experts * half_slots, width)
    in_half = slots // half_slots == lane
    local_pos = routed * half_slots + slots % half_slots
    picked = received[local_pos].astype(jnp.float32).reshape(tok_rows, top_count, width)
    weighted = jnp.where(in_half.reshape(tok_rows, top_count), gate_probs, 0.0)
    partial_value = jnp.sum(weighted[:, :, None] * picked, axis=1)
    return lax.psum_scatter(partial_value, "tp", scatter_dimension=1, tiled=True).astype(
        jnp.bfloat16
    )


def solution(mesh):
    in_specs = (
        P(("groups", "ep"), "tp"),
        P(("groups", "ep"), None),
        P(("groups", "ep"), None),
        P("ep", None, "tp"),
        P("ep", None, "tp"),
        P("ep", "tp", None),
    )
    out_specs = P(("groups", "ep"), "tp")

    def body(tokens, expert_ids, *rest):
        n, top = lax.axis_size("ep"), expert_ids.shape[1]
        small = n <= 4 * top and n % 2 == 0 and n >= 8 and lax.axis_size("tp") == 2 and tokens.shape[1] % 128 + SPLITS * n <= 128
        return (ring_body if small else slot_body)(tokens, expert_ids, *rest)

    return jax.shard_map(body, mesh=mesh, in_specs=in_specs, out_specs=out_specs, check_vma=False)
```

```python
import functools

import jax
import jax.numpy as jnp
from jax import lax
from jax.experimental import pallas as pl
from jax.experimental.pallas import tpu as pltpu
from jax.sharding import PartitionSpec as P

SPLITS = 3


def in_vmem(shape, dtype=jnp.bfloat16):
    return pltpu.MemorySpace.VMEM(shape, dtype)


def hold(x):
    return pltpu.with_memory_space_constraint(x, pltpu.VMEM)


def after(x, done):
    return lax.optimization_barrier((x, done))[0]


def tiles_of(rows, columns):
    whole, rest = divmod(columns, 128)
    parts = 1
    while rest and 128 // (2 * parts) >= rest and rows % (32 * parts) == 0:
        parts *= 2
    return whole, rest, parts, whole * rows + (rows // parts if rest else 0)


def tile_places(rows, columns):
    whole, rest, parts, size = tiles_of(rows, columns)
    for j in range(whole):
        yield slice(0, rows), slice(128 * j, 128 * j + 128), slice(j * rows, (j + 1) * rows), slice(0, 128)
    for q in range(parts if rest else 0):
        share, lane = rows // parts, q * (128 // parts)
        yield slice(q * share, (q + 1) * share), slice(128 * whole, columns), slice(whole * rows, size), slice(lane, lane + rest)


def pack_kernel(n_experts, tokens_in, ids_in, probs_in, packed, tokens, ids, probs, sems):
    copies = [
        pltpu.make_async_copy(src, dst, sems.at[i])
        for i, (src, dst) in enumerate(((ids_in, ids), (probs_in, probs), (tokens_in, tokens)))
    ]
    for copy in copies:
        copy.start()
    top, rows = ids.shape
    half = tokens.shape[1]
    copies[0].wait()
    copies[1].wait()
    expert = lax.broadcasted_iota(jnp.int32, (n_experts, rows), 0)
    rest = jnp.zeros((n_experts, rows), jnp.float32)
    for k in range(top):
        rest += jnp.where(ids[k : k + 1, :] == expert, probs[k : k + 1, :], 0.0)
    terms = []
    for _ in range(SPLITS):
        term = rest.astype(jnp.bfloat16).astype(jnp.float32)
        terms.append(term)
        rest = rest - term
    terms = jnp.concatenate(terms, axis=0).T.astype(jnp.bfloat16)
    copies[2].wait()
    for r, c, at, lanes in tile_places(rows, half + terms.shape[1]):
        if c.stop <= half:
            packed[at, lanes] = tokens[r, c]
        else:
            split = lanes.start + half - c.start
            packed[at, lanes.start : split] = tokens[r, c.start : half]
            packed[at, split : lanes.stop] = terms[r, :]


def pack(tokens, expert_ids, gate_probs, n_experts):
    rows, half = tokens.shape
    args = (tokens, expert_ids.T, gate_probs.T)
    return pl.pallas_call(
        functools.partial(pack_kernel, n_experts),
        out_shape=in_vmem((tiles_of(rows, half + SPLITS * n_experts)[-1], 128)),
        in_specs=[pl.BlockSpec(memory_space=pltpu.HBM)] * 3,
        out_specs=pl.BlockSpec(memory_space=pltpu.VMEM),
        scratch_shapes=[pltpu.VMEM(a.shape, a.dtype) for a in args] + [pltpu.SemaphoreType.DMA((3,))],
        compiler_params=pltpu.CompilerParams(vmem_limit_bytes=8 << 20),
    )(*[pltpu.with_memory_space_constraint(a, pltpu.HBM) for a in args])


def pieces(hidden):
    first = -(-hidden // 256) * 128
    return ((0, first), (first, hidden))


def turn_kernel(after_this, gate_in, up_in, gate, up, gate_buf, up_buf, sems):
    steps = []
    for i, (src, buf, out) in enumerate(((gate_in, gate_buf, gate), (up_in, up_buf, up))):
        for j, (start, stop) in enumerate(pieces(src.shape[0])):
            span = pl.ds(start, stop - start)
            steps.append((pltpu.make_async_copy(src.at[span], buf.at[span], sems.at[i, j]), buf, out, start, stop))
    for copy, *_ in steps:
        copy.start()
    for copy, buf, out, start, stop in steps:
        copy.wait()
        out[:, start:stop] = buf[start:stop, :].T


def turn_weights(after_this, *weights):
    hidden, width = weights[0].shape
    return pl.pallas_call(
        turn_kernel,
        out_shape=[in_vmem((width, hidden))] * 2,
        in_specs=[pl.BlockSpec(memory_space=pltpu.SMEM)] + [pl.BlockSpec(memory_space=pltpu.HBM)] * 2,
        out_specs=[pl.BlockSpec(memory_space=pltpu.VMEM)] * 2,
        scratch_shapes=[pltpu.VMEM((hidden, width), jnp.bfloat16)] * 2 + [pltpu.SemaphoreType.DMA((2, 2))],
        compiler_params=pltpu.CompilerParams(vmem_limit_bytes=32 << 20),
        cost_estimate=pl.CostEstimate(flops=0, bytes_accessed=8 * hidden * width, transcendentals=0),
    )(after_this, *[pltpu.with_memory_space_constraint(w, pltpu.HBM) for w in weights])


def halve_kernel(place, down_in, down_mine, down_theirs, down_buf, sems):
    lane = place[0]
    half = down_mine.shape[1]
    spans = [slice(start, stop) for start, stop in pieces(down_in.shape[0])]
    copies = [
        pltpu.make_async_copy(down_in.at[pl.ds(s.start, s.stop - s.start)], down_buf.at[pl.ds(s.start, s.stop - s.start)], sems.at[i])
        for i, s in enumerate(spans)
    ]
    for copy in copies:
        copy.start()
    for copy, s in zip(copies, spans):
        copy.wait()

        @pl.when(lane == 0)
        def _():
            down_mine[s, :] = down_buf[s, :half]
            down_theirs[s, :] = down_buf[s, half:]

        @pl.when(lane != 0)
        def _():
            down_mine[s, :] = down_buf[s, half:]
            down_theirs[s, :] = down_buf[s, :half]


def halve_weights(place, w_down):
    hidden, width = w_down.shape
    return pl.pallas_call(
        halve_kernel,
        out_shape=[in_vmem((hidden, width // 2))] * 2,
        in_specs=[pl.BlockSpec(memory_space=pltpu.SMEM), pl.BlockSpec(memory_space=pltpu.HBM)],
        out_specs=[pl.BlockSpec(memory_space=pltpu.VMEM)] * 2,
        scratch_shapes=[pltpu.VMEM((hidden, width), jnp.bfloat16), pltpu.SemaphoreType.DMA((2,))],
        compiler_params=pltpu.CompilerParams(vmem_limit_bytes=32 << 20),
        cost_estimate=pl.CostEstimate(flops=0, bytes_accessed=8 * hidden * width, transcendentals=0),
    )(place, pltpu.with_memory_space_constraint(w_down, pltpu.HBM))


def gather_rows(blocks, x, rows, columns):
    half = x.shape[1]
    for i, block in enumerate(blocks):
        for r, c, at, lanes in tile_places(rows, columns):
            stop = min(c.stop, half)
            x[i * rows + r.start : i * rows + r.stop, c.start : stop] = block[at, lanes.start : lanes.start + stop - c.start]
    start = len(blocks) * rows
    if start < x.shape[0]:
        x[start:, :] = jnp.zeros((x.shape[0] - start, half), x.dtype)


def project(x, lane, w):
    half = x.shape[1]
    return jnp.dot(x[...], w[pl.ds(pl.multiple_of(lane * half, 16), half), :], preferred_element_type=jnp.float32)


def activate(gated, lifted):
    return (gated / (1.0 + jnp.exp(-gated)) * lifted).astype(jnp.bfloat16)


def gate_weights(blocks, half, expert, n_experts, rows):
    columns = half + SPLITS * n_experts
    weights = []
    for block in blocks:
        pieces = []
        for _, c, at, lanes in tile_places(rows, columns):
            if c.stop == columns:
                terms = block[at, lanes.start + half - c.start : lanes.stop].astype(jnp.float32)
                column = lax.broadcasted_iota(jnp.int32, terms.shape, 1)
                pieces.append(jnp.sum(jnp.where(lax.rem(column, n_experts) == expert, terms, 0.0), axis=1, keepdims=True))
        weights.append(jnp.concatenate(pieces, axis=0))
    return weights


def lower(hidden, w, weights, *outs):
    value = jnp.dot(hidden, w[...], preferred_element_type=jnp.float32)
    rows, half = weights[0].shape[0], w.shape[1]
    size = tiles_of(rows, half)[-1]
    places = [(out, start) for out in outs for start in range(0, out.shape[0], size)]
    for i, (weight, (out, start)) in enumerate(zip(weights, places)):
        scaled = (value[i * rows : (i + 1) * rows] * weight).astype(jnp.bfloat16)
        for r, c, at, lanes in tile_places(rows, half):
            out[start + at.start : start + at.stop, lanes] = scaled[r, c]


def expert_kernel(n_blocks, n_experts, rows, place, *refs):
    own, across = refs[:n_blocks], refs[n_blocks : 2 * n_blocks]
    w_gate, w_up, down_mine, down_theirs, *outs, x_own, x_across = refs[2 * n_blocks :]
    lane, expert = place[0], place[1]
    half = x_own.shape[1]
    columns = half + SPLITS * n_experts
    gather_rows(own, x_own, rows, columns)
    gather_rows(across, x_across, rows, columns)
    gated = project(x_own, lane, w_gate) + project(x_across, 1 - lane, w_gate)
    lifted = project(x_own, lane, w_up) + project(x_across, 1 - lane, w_up)
    hidden = activate(gated, lifted)
    weights = gate_weights(own, half, expert, n_experts, rows)
    mine, theirs = outs[: len(outs) // 2], outs[len(outs) // 2 :]
    lower(hidden, down_theirs, weights, *theirs)
    lower(hidden, down_mine, weights, *mine)


def first_kernel(n_blocks, n_experts, rows, place, *refs):
    own = refs[:n_blocks]
    w_gate, w_up, gated, lifted, x = refs[n_blocks:]
    gather_rows(own, x, rows, x.shape[1] + SPLITS * n_experts)
    gated[...] = project(x, place[0], w_gate)
    lifted[...] = project(x, place[0], w_up)


def second_kernel(n_blocks, n_experts, rows, place, *refs):
    own, across = refs[:n_blocks], refs[n_blocks : 2 * n_blocks]
    gated, lifted, w_gate, w_up, down_theirs, hidden, *theirs, x = refs[2 * n_blocks :]
    half = x.shape[1]
    gather_rows(across, x, rows, half + SPLITS * n_experts)
    there = 1 - place[0]
    hidden[...] = activate(gated[...] + project(x, there, w_gate), lifted[...] + project(x, there, w_up))
    lower(hidden[...], down_theirs, gate_weights(own, half, place[1], n_experts, rows), *theirs)


def third_kernel(n_blocks, n_experts, rows, place, *refs):
    own = refs[:n_blocks]
    hidden, down_mine, *mine = refs[n_blocks:]
    lower(hidden[...], down_mine, gate_weights(own, down_mine.shape[1], place[1], n_experts, rows), *mine)


def call(kernel, place, args, out_shape, scratch_shapes, flops):
    vmem = pl.BlockSpec(memory_space=pltpu.VMEM)
    return pl.pallas_call(
        kernel,
        out_shape=out_shape,
        in_specs=[pl.BlockSpec(memory_space=pltpu.SMEM)] + [vmem] * len(args),
        out_specs=[vmem] * len(out_shape),
        scratch_shapes=scratch_shapes,
        compiler_params=pltpu.CompilerParams(vmem_limit_bytes=16 << 20),
        cost_estimate=pl.CostEstimate(flops=flops, bytes_accessed=flops // 128, transcendentals=0),
    )(place, *[hold(a) for a in args])


def padded(rows):
    return max(rows, 128)


def run_expert(place, own, across, weights, n_experts, block_rows):
    width, hidden = weights[0].shape
    half = width // 2
    rows, pairs = len(own) * block_rows, max(1, len(own) // 2)
    outs = call(
        functools.partial(expert_kernel, len(own), n_experts, block_rows),
        place,
        (*own, *across, *weights),
        [in_vmem((len(own) // pairs * tiles_of(block_rows, half)[-1], 128))] * (2 * pairs),
        [pltpu.VMEM((padded(rows), half), jnp.bfloat16)] * 2,
        6 * padded(rows) * hidden * width,
    )
    return outs[:pairs], outs[pairs:]


def run_expert_in_stages(place, own, across, swap, weights, n_experts, block_rows):
    gate, up, down_mine, down_theirs = weights
    width, hidden = gate.shape
    half = width // 2
    n_blocks = len(own)
    rows, size = n_blocks * block_rows, tiles_of(block_rows, half)[-1]
    products = [in_vmem((padded(rows), hidden), jnp.float32)] * 2
    outs = [in_vmem((size, 128)), in_vmem(((n_blocks - 1) * size, 128))]
    x = [pltpu.VMEM((padded(rows), half), jnp.bfloat16)]
    flops = 2 * padded(rows) * hidden * width
    gated, lifted = call(functools.partial(first_kernel, n_blocks, n_experts, block_rows), place, (*own, gate, up), products, x, flops)
    units, *theirs = call(
        functools.partial(second_kernel, n_blocks, n_experts, block_rows),
        place,
        (*own, *across, gated, lifted, gate, up, down_theirs),
        [in_vmem((padded(rows), hidden)), *outs],
        x,
        flops + flops // 2,
    )
    theirs = [swap(a) for a in theirs]
    mine = call(
        functools.partial(third_kernel, n_blocks, n_experts, block_rows),
        place,
        (*own, units, down_mine),
        outs,
        [],
        flops // 2,
    )
    return mine, theirs


def add_kernel(*refs):
    *terms, out = refs
    out[...] = sum(t[...].astype(jnp.float32) for t in terms).astype(out.dtype)


def add(*terms):
    vmem = pl.BlockSpec(memory_space=pltpu.VMEM)
    return pl.pallas_call(
        add_kernel,
        out_shape=in_vmem(terms[0].shape),
        in_specs=[vmem] * len(terms),
        out_specs=vmem,
        cost_estimate=pl.CostEstimate(flops=0, bytes_accessed=12 << 20, transcendentals=0),
    )(*[hold(t) for t in terms])


def finish_kernel(a, b, out):
    rows, half = out.shape
    for r, c, at, lanes in tile_places(rows, half):
        total = a[at, lanes].astype(jnp.float32) + b[at, lanes].astype(jnp.float32)
        out[r, c] = total.astype(out.dtype)


def finish(a, b, rows, half):
    vmem = pl.BlockSpec(memory_space=pltpu.VMEM)
    return pl.pallas_call(
        finish_kernel,
        out_shape=jax.ShapeDtypeStruct((rows, half), jnp.bfloat16),
        in_specs=[vmem] * 2,
        out_specs=vmem,
    )(hold(a), hold(b))


def ring_body(tokens, expert_ids, gate_probs, w_gate, w_up, w_down):
    n = lax.axis_size("ep")
    rows, half = tokens.shape
    size = tiles_of(rows, half)[-1]
    order = list(range(0, n, 2)) + list(range(n - 1, 0, -2))
    ahead = [(order[i], order[(i + 1) % n]) for i in range(n)]
    back = [(b, a) for a, b in ahead]
    swap = functools.partial(lax.ppermute, axis_name="tp", perm=[(0, 1), (1, 0)])
    far = n // 2
    place = jnp.stack([lax.axis_index("tp"), lax.axis_index("ep")]).astype(jnp.int32)
    packed = pack(tokens, expert_ids, gate_probs, n)
    gate, up = turn_weights(after(place, packed), w_gate[0].T, w_up[0].T)

    came, across, value, parts = {0: packed}, {}, {}, {}

    def run(keys, wait_for=None):
        at = place if wait_for is None else after(place, wait_for)
        mine, theirs = run_expert(at, [came[k] for k in keys], [across[k] for k in keys], weights, n, rows)
        return [(keys[2 * i : 2 * i + 2], *pair) for i, pair in enumerate(zip(mine, theirs))]

    def keep(keys, mine, theirs):
        pairs = ((mine, theirs), lax.optimization_barrier((mine, theirs)))
        start = 0
        for i, k in enumerate(keys):
            mine, theirs = pairs[i % 2]
            span = slice(start, start + size)
            start = span.stop
            parts[k] = mine[span], theirs[span]
            value[k] = mine[span].astype(jnp.float32) + theirs[span].astype(jnp.float32)

    came[1] = lax.ppermute(packed, "ep", ahead)
    came[-1] = lax.ppermute(packed, "ep", back)
    weights, done, near = [gate, up], up, []
    for k in range(2, far + 1):
        came[k - 1], came[1 - k] = after(came[k - 1], done), after(came[1 - k], done)
        came[k] = lax.ppermute(came[k - 1], "ep", ahead)
        if k < far:
            came[-k] = lax.ppermute(came[1 - k], "ep", back)
        across[k - 1], across[1 - k] = swap(came[k - 1]), swap(came[1 - k])
        if k == 2:
            weights += halve_weights(after(place, came[1]), w_down[0])
            done = weights[-1]
        else:
            near += run([k - 2, 2 - k])
            done = near[-1][-1]
    came[far] = after(came[far], done)
    across[far] = swap(came[far])
    across[0] = swap(after(packed, came[far]))
    last = [far, far - 1, 1 - far]
    for keys, mine, theirs in zip(([far], last[1:]), *run_expert_in_stages(place, [came[k] for k in last], [across[k] for k in last], swap, weights, n, rows)):
        keep(keys, mine, theirs)

    to_ahead = value[far].astype(jnp.bfloat16)
    to_back = value[far - 1].astype(jnp.bfloat16)
    for keys, mine, theirs in near:
        keep(keys, mine, swap(after(theirs, to_back)))
    for k in range(far - 1, -1, -1):
        behind = lax.ppermute(to_ahead, "ep", ahead)
        if k == far - 1:
            ((keys, mine, done),) = run([0], (to_ahead, to_back))
            keep(keys, mine, swap(done))
        else:
            to_back = done = add(*parts[k], after(front, to_ahead))
        if k:
            front = lax.ppermute(to_back, "ep", back)
            to_ahead = (value[-k] + after(behind, done).astype(jnp.float32)).astype(jnp.bfloat16)
    return finish(to_back, behind, rows, half)


def swiglu_expert(rows, gate_part, up_part, down_part):
    gated = jnp.dot(rows, gate_part, preferred_element_type=jnp.float32)
    lifted = jnp.dot(rows, up_part, preferred_element_type=jnp.float32)
    hidden = (jax.nn.silu(gated) * lifted).astype(jnp.bfloat16)
    return jnp.dot(hidden, down_part, preferred_element_type=jnp.float32)


def slot_table(expert_ids, n_experts):
    routed = expert_ids.reshape(-1)
    pair_count = routed.shape[0]
    onehot = (routed[:, None] == jnp.arange(n_experts, dtype=jnp.int32)[None, :]).astype(
        jnp.bfloat16
    )
    row_index = lax.broadcasted_iota(jnp.int32, (pair_count, pair_count), 0)
    col_index = lax.broadcasted_iota(jnp.int32, (pair_count, pair_count), 1)
    earlier = (row_index > col_index).astype(jnp.bfloat16)
    before = jnp.dot(earlier, onehot, preferred_element_type=jnp.float32)
    slots = jnp.sum(before * onehot.astype(jnp.float32), axis=1).astype(jnp.int32)
    return (routed, slots)


def slot_body(tokens, expert_ids, gate_probs, w_gate, w_up, w_down):
    n_experts = lax.axis_size("ep")
    tok_rows, top_count = expert_ids.shape
    capacity = 3 * tok_rows * top_count // (2 * n_experts)
    routed, slots = slot_table(expert_ids, n_experts)
    positions = routed * capacity + slots
    pair_token = jnp.repeat(jnp.arange(tok_rows, dtype=jnp.int32), top_count)
    buffer_rows = n_experts * capacity
    owners = jnp.full((buffer_rows,), tok_rows, jnp.int32).at[positions].set(pair_token)
    half_slots = capacity // 2
    whole_tokens = lax.all_gather(tokens, "tp", axis=1, tiled=True)
    width = whole_tokens.shape[1]
    gate_full, up_full = (
        lax.all_gather(w_gate, "tp", axis=2, tiled=True),
        lax.all_gather(w_up, "tp", axis=2, tiled=True),
    )
    down_full = lax.all_gather(w_down, "tp", axis=1, tiled=True)
    padded = jnp.concatenate([whole_tokens, jnp.zeros((1, width), whole_tokens.dtype)], 0)
    outgoing = padded[owners].reshape(n_experts, capacity, width)
    lane = lax.axis_index("tp")
    mine = lax.dynamic_slice_in_dim(outgoing, lane * half_slots, half_slots, 1)
    block = lax.all_to_all(mine, "ep", split_axis=0, concat_axis=0, tiled=True)
    sources, items, columns = block.shape
    result = swiglu_expert(
        block.reshape(sources * items, columns), gate_full[0], up_full[0], down_full[0]
    )
    result = result.astype(jnp.bfloat16).reshape(sources, items, columns)
    returned = lax.all_to_all(result, "ep", split_axis=0, concat_axis=0, tiled=True)
    received = returned.reshape(n_experts * half_slots, width)
    in_half = slots // half_slots == lane
    local_pos = routed * half_slots + slots % half_slots
    picked = received[local_pos].astype(jnp.float32).reshape(tok_rows, top_count, width)
    weighted = jnp.where(in_half.reshape(tok_rows, top_count), gate_probs, 0.0)
    partial_value = jnp.sum(weighted[:, :, None] * picked, axis=1)
    return lax.psum_scatter(partial_value, "tp", scatter_dimension=1, tiled=True).astype(
        jnp.bfloat16
    )


def solution(mesh):
    in_specs = (
        P(("groups", "ep"), "tp"),
        P(("groups", "ep"), None),
        P(("groups", "ep"), None),
        P("ep", None, "tp"),
        P("ep", None, "tp"),
        P("ep", "tp", None),
    )
    out_specs = P(("groups", "ep"), "tp")

    def body(tokens, expert_ids, *rest):
        n, top = lax.axis_size("ep"), expert_ids.shape[1]
        small = n <= 4 * top and n % 2 == 0 and n >= 8 and lax.axis_size("tp") == 2 and tokens.shape[1] % 128 + SPLITS * n <= 128
        return (ring_body if small else slot_body)(tokens, expert_ids, *rest)

    return jax.shard_map(body, mesh=mesh, in_specs=in_specs, out_specs=out_specs, check_vma=False)
```

```python
import functools

import jax
import jax.numpy as jnp
from jax import lax
from jax.experimental import pallas as pl
from jax.experimental.pallas import tpu as pltpu
from jax.sharding import PartitionSpec as P

SPLITS = 3


def in_vmem(shape, dtype=jnp.bfloat16):
    return pltpu.MemorySpace.VMEM(shape, dtype)


def hold(x):
    return pltpu.with_memory_space_constraint(x, pltpu.VMEM)


def after(x, done):
    return lax.optimization_barrier((x, done))[0]


def tiles_of(rows, columns):
    whole, rest = divmod(columns, 128)
    parts = 1
    while rest and 128 // (2 * parts) >= rest and rows % (32 * parts) == 0:
        parts *= 2
    return whole, rest, parts, whole * rows + (rows // parts if rest else 0)


def tile_places(rows, columns):
    whole, rest, parts, size = tiles_of(rows, columns)
    for j in range(whole):
        yield slice(0, rows), slice(128 * j, 128 * j + 128), slice(j * rows, (j + 1) * rows), slice(0, 128)
    for q in range(parts if rest else 0):
        share, lane = rows // parts, q * (128 // parts)
        yield slice(q * share, (q + 1) * share), slice(128 * whole, columns), slice(whole * rows, size), slice(lane, lane + rest)


def pack_kernel(n_experts, tokens_in, ids_in, probs_in, packed, tokens, ids, probs, sems):
    copies = [
        pltpu.make_async_copy(src, dst, sems.at[i])
        for i, (src, dst) in enumerate(((ids_in, ids), (probs_in, probs), (tokens_in, tokens)))
    ]
    for copy in copies:
        copy.start()
    top, rows = ids.shape
    half = tokens.shape[1]
    copies[0].wait()
    copies[1].wait()
    expert = lax.broadcasted_iota(jnp.int32, (n_experts, rows), 0)
    rest = jnp.zeros((n_experts, rows), jnp.float32)
    for k in range(top):
        rest += jnp.where(ids[k : k + 1, :] == expert, probs[k : k + 1, :], 0.0)
    terms = []
    for _ in range(SPLITS):
        term = rest.astype(jnp.bfloat16).astype(jnp.float32)
        terms.append(term)
        rest = rest - term
    terms = jnp.concatenate(terms, axis=0).T.astype(jnp.bfloat16)
    copies[2].wait()
    for r, c, at, lanes in tile_places(rows, half + terms.shape[1]):
        if c.stop <= half:
            packed[at, lanes] = tokens[r, c]
        else:
            split = lanes.start + half - c.start
            packed[at, lanes.start : split] = tokens[r, c.start : half]
            packed[at, split : lanes.stop] = terms[r, :]


def pack(tokens, expert_ids, gate_probs, n_experts):
    rows, half = tokens.shape
    args = (tokens, expert_ids.T, gate_probs.T)
    return pl.pallas_call(
        functools.partial(pack_kernel, n_experts),
        out_shape=in_vmem((tiles_of(rows, half + SPLITS * n_experts)[-1], 128)),
        in_specs=[pl.BlockSpec(memory_space=pltpu.HBM)] * 3,
        out_specs=pl.BlockSpec(memory_space=pltpu.VMEM),
        scratch_shapes=[pltpu.VMEM(a.shape, a.dtype) for a in args] + [pltpu.SemaphoreType.DMA((3,))],
        compiler_params=pltpu.CompilerParams(vmem_limit_bytes=8 << 20),
    )(*[pltpu.with_memory_space_constraint(a, pltpu.HBM) for a in args])


def pieces(hidden):
    first = -(-hidden // 256) * 128
    return ((0, first), (first, hidden))


def turn_kernel(after_this, gate_in, up_in, gate, up, gate_buf, up_buf, sems):
    steps = []
    for i, (src, buf, out) in enumerate(((gate_in, gate_buf, gate), (up_in, up_buf, up))):
        for j, (start, stop) in enumerate(pieces(src.shape[0])):
            span = pl.ds(start, stop - start)
            steps.append((pltpu.make_async_copy(src.at[span], buf.at[span], sems.at[i, j]), buf, out, start, stop))
    for copy, *_ in steps[:2]:
        copy.start()
    for i, (copy, buf, out, start, stop) in enumerate(steps):
        copy.wait()
        if i + 2 < len(steps):
            steps[i + 2][0].start()
        out[:, start:stop] = buf[start:stop, :].T


def turn_weights(after_this, *weights):
    hidden, width = weights[0].shape
    return pl.pallas_call(
        turn_kernel,
        out_shape=[in_vmem((width, hidden))] * 2,
        in_specs=[pl.BlockSpec(memory_space=pltpu.SMEM)] + [pl.BlockSpec(memory_space=pltpu.HBM)] * 2,
        out_specs=[pl.BlockSpec(memory_space=pltpu.VMEM)] * 2,
        scratch_shapes=[pltpu.VMEM((hidden, width), jnp.bfloat16)] * 2 + [pltpu.SemaphoreType.DMA((2, 2))],
        compiler_params=pltpu.CompilerParams(vmem_limit_bytes=32 << 20),
        cost_estimate=pl.CostEstimate(flops=0, bytes_accessed=8 * hidden * width, transcendentals=0),
    )(after_this, *[pltpu.with_memory_space_constraint(w, pltpu.HBM) for w in weights])


def halve_kernel(place, down_in, down_mine, down_theirs, down_buf, sems):
    lane = place[0]
    half = down_mine.shape[1]
    spans = [slice(start, stop) for start, stop in pieces(down_in.shape[0])]
    copies = [
        pltpu.make_async_copy(down_in.at[pl.ds(s.start, s.stop - s.start)], down_buf.at[pl.ds(s.start, s.stop - s.start)], sems.at[i])
        for i, s in enumerate(spans)
    ]
    for copy in copies:
        copy.start()
    for copy, s in zip(copies, spans):
        copy.wait()

        @pl.when(lane == 0)
        def _():
            down_mine[s, :] = down_buf[s, :half]
            down_theirs[s, :] = down_buf[s, half:]

        @pl.when(lane != 0)
        def _():
            down_mine[s, :] = down_buf[s, half:]
            down_theirs[s, :] = down_buf[s, :half]


def halve_weights(place, w_down):
    hidden, width = w_down.shape
    return pl.pallas_call(
        halve_kernel,
        out_shape=[in_vmem((hidden, width // 2))] * 2,
        in_specs=[pl.BlockSpec(memory_space=pltpu.SMEM), pl.BlockSpec(memory_space=pltpu.HBM)],
        out_specs=[pl.BlockSpec(memory_space=pltpu.VMEM)] * 2,
        scratch_shapes=[pltpu.VMEM((hidden, width), jnp.bfloat16), pltpu.SemaphoreType.DMA((2,))],
        compiler_params=pltpu.CompilerParams(vmem_limit_bytes=32 << 20),
        cost_estimate=pl.CostEstimate(flops=0, bytes_accessed=8 * hidden * width, transcendentals=0),
    )(place, pltpu.with_memory_space_constraint(w_down, pltpu.HBM))


def gather_rows(blocks, x, rows, columns):
    half = x.shape[1]
    for i, block in enumerate(blocks):
        for r, c, at, lanes in tile_places(rows, columns):
            stop = min(c.stop, half)
            x[i * rows + r.start : i * rows + r.stop, c.start : stop] = block[at, lanes.start : lanes.start + stop - c.start]
    start = len(blocks) * rows
    if start < x.shape[0]:
        x[start:, :] = jnp.zeros((x.shape[0] - start, half), x.dtype)


def project(x, lane, w):
    half = x.shape[1]
    return jnp.dot(x[...], w[pl.ds(pl.multiple_of(lane * half, 16), half), :], preferred_element_type=jnp.float32)


def activate(gated, lifted):
    return (gated / (1.0 + jnp.exp(-gated)) * lifted).astype(jnp.bfloat16)


def gate_weights(blocks, half, expert, n_experts, rows):
    columns = half + SPLITS * n_experts
    weights = []
    for block in blocks:
        pieces = []
        for _, c, at, lanes in tile_places(rows, columns):
            if c.stop == columns:
                terms = block[at, lanes.start + half - c.start : lanes.stop].astype(jnp.float32)
                column = lax.broadcasted_iota(jnp.int32, terms.shape, 1)
                pieces.append(jnp.sum(jnp.where(lax.rem(column, n_experts) == expert, terms, 0.0), axis=1, keepdims=True))
        weights.append(jnp.concatenate(pieces, axis=0))
    return weights


def lower(hidden, w, weights, *outs):
    value = jnp.dot(hidden, w[...], preferred_element_type=jnp.float32)
    rows, half = weights[0].shape[0], w.shape[1]
    size = tiles_of(rows, half)[-1]
    places = [(out, start) for out in outs for start in range(0, out.shape[0], size)]
    for i, (weight, (out, start)) in enumerate(zip(weights, places)):
        scaled = (value[i * rows : (i + 1) * rows] * weight).astype(jnp.bfloat16)
        for r, c, at, lanes in tile_places(rows, half):
            out[start + at.start : start + at.stop, lanes] = scaled[r, c]


def expert_kernel(n_blocks, n_experts, rows, place, *refs):
    own, across = refs[:n_blocks], refs[n_blocks : 2 * n_blocks]
    w_gate, w_up, down_mine, down_theirs, *outs, x_own, x_across = refs[2 * n_blocks :]
    lane, expert = place[0], place[1]
    half = x_own.shape[1]
    columns = half + SPLITS * n_experts
    gather_rows(own, x_own, rows, columns)
    gather_rows(across, x_across, rows, columns)
    gated = project(x_own, lane, w_gate) + project(x_across, 1 - lane, w_gate)
    lifted = project(x_own, lane, w_up) + project(x_across, 1 - lane, w_up)
    hidden = activate(gated, lifted)
    weights = gate_weights(own, half, expert, n_experts, rows)
    mine, theirs = outs[: len(outs) // 2], outs[len(outs) // 2 :]
    lower(hidden, down_theirs, weights, *theirs)
    lower(hidden, down_mine, weights, *mine)


def first_kernel(n_blocks, n_experts, rows, place, *refs):
    own = refs[:n_blocks]
    w_gate, w_up, gated, lifted, x = refs[n_blocks:]
    gather_rows(own, x, rows, x.shape[1] + SPLITS * n_experts)
    gated[...] = project(x, place[0], w_gate)
    lifted[...] = project(x, place[0], w_up)


def second_kernel(n_blocks, n_experts, rows, place, *refs):
    own, across = refs[:n_blocks], refs[n_blocks : 2 * n_blocks]
    gated, lifted, w_gate, w_up, down_theirs, hidden, *theirs, x = refs[2 * n_blocks :]
    half = x.shape[1]
    gather_rows(across, x, rows, half + SPLITS * n_experts)
    there = 1 - place[0]
    hidden[...] = activate(gated[...] + project(x, there, w_gate), lifted[...] + project(x, there, w_up))
    lower(hidden[...], down_theirs, gate_weights(own, half, place[1], n_experts, rows), *theirs)


def third_kernel(n_blocks, n_experts, rows, place, *refs):
    own = refs[:n_blocks]
    hidden, down_mine, *mine = refs[n_blocks:]
    lower(hidden[...], down_mine, gate_weights(own, down_mine.shape[1], place[1], n_experts, rows), *mine)


def call(kernel, place, args, out_shape, scratch_shapes, flops):
    vmem = pl.BlockSpec(memory_space=pltpu.VMEM)
    return pl.pallas_call(
        kernel,
        out_shape=out_shape,
        in_specs=[pl.BlockSpec(memory_space=pltpu.SMEM)] + [vmem] * len(args),
        out_specs=[vmem] * len(out_shape),
        scratch_shapes=scratch_shapes,
        compiler_params=pltpu.CompilerParams(vmem_limit_bytes=16 << 20),
        cost_estimate=pl.CostEstimate(flops=flops, bytes_accessed=flops // 128, transcendentals=0),
    )(place, *[hold(a) for a in args])


def padded(rows):
    return max(rows, 128)


def run_expert(place, own, across, weights, n_experts, block_rows):
    width, hidden = weights[0].shape
    half = width // 2
    rows, pairs = len(own) * block_rows, max(1, len(own) // 2)
    outs = call(
        functools.partial(expert_kernel, len(own), n_experts, block_rows),
        place,
        (*own, *across, *weights),
        [in_vmem((len(own) // pairs * tiles_of(block_rows, half)[-1], 128))] * (2 * pairs),
        [pltpu.VMEM((padded(rows), half), jnp.bfloat16)] * 2,
        6 * padded(rows) * hidden * width,
    )
    return outs[:pairs], outs[pairs:]


def run_expert_in_stages(place, own, across, swap, weights, n_experts, block_rows):
    gate, up, down_mine, down_theirs = weights
    width, hidden = gate.shape
    half = width // 2
    n_blocks = len(own)
    rows, size = n_blocks * block_rows, tiles_of(block_rows, half)[-1]
    products = [in_vmem((padded(rows), hidden), jnp.float32)] * 2
    outs = [in_vmem((size, 128)), in_vmem(((n_blocks - 1) * size, 128))]
    x = [pltpu.VMEM((padded(rows), half), jnp.bfloat16)]
    flops = 2 * padded(rows) * hidden * width
    gated, lifted = call(functools.partial(first_kernel, n_blocks, n_experts, block_rows), place, (*own, gate, up), products, x, flops)
    units, *theirs = call(
        functools.partial(second_kernel, n_blocks, n_experts, block_rows),
        place,
        (*own, *across, gated, lifted, gate, up, down_theirs),
        [in_vmem((padded(rows), hidden)), *outs],
        x,
        flops + flops // 2,
    )
    theirs = [swap(a) for a in theirs]
    mine = call(
        functools.partial(third_kernel, n_blocks, n_experts, block_rows),
        place,
        (*own, units, down_mine),
        outs,
        [],
        flops // 2,
    )
    return mine, theirs


def add_kernel(*refs):
    *terms, out = refs
    out[...] = sum(t[...].astype(jnp.float32) for t in terms).astype(out.dtype)


def add(*terms):
    vmem = pl.BlockSpec(memory_space=pltpu.VMEM)
    return pl.pallas_call(
        add_kernel,
        out_shape=in_vmem(terms[0].shape),
        in_specs=[vmem] * len(terms),
        out_specs=vmem,
        cost_estimate=pl.CostEstimate(flops=0, bytes_accessed=12 << 20, transcendentals=0),
    )(*[hold(t) for t in terms])


def finish_kernel(a, b, out):
    rows, half = out.shape
    for r, c, at, lanes in tile_places(rows, half):
        total = a[at, lanes].astype(jnp.float32) + b[at, lanes].astype(jnp.float32)
        out[r, c] = total.astype(out.dtype)


def finish(a, b, rows, half):
    vmem = pl.BlockSpec(memory_space=pltpu.VMEM)
    return pl.pallas_call(
        finish_kernel,
        out_shape=jax.ShapeDtypeStruct((rows, half), jnp.bfloat16),
        in_specs=[vmem] * 2,
        out_specs=vmem,
    )(hold(a), hold(b))


def ring_body(tokens, expert_ids, gate_probs, w_gate, w_up, w_down):
    n = lax.axis_size("ep")
    rows, half = tokens.shape
    size = tiles_of(rows, half)[-1]
    order = list(range(0, n, 2)) + list(range(n - 1, 0, -2))
    ahead = [(order[i], order[(i + 1) % n]) for i in range(n)]
    back = [(b, a) for a, b in ahead]
    swap = functools.partial(lax.ppermute, axis_name="tp", perm=[(0, 1), (1, 0)])
    far = n // 2
    place = jnp.stack([lax.axis_index("tp"), lax.axis_index("ep")]).astype(jnp.int32)
    packed = pack(tokens, expert_ids, gate_probs, n)
    gate, up = turn_weights(after(place, packed), w_gate[0].T, w_up[0].T)

    came, across, value, parts = {0: packed}, {}, {}, {}

    def run(keys, wait_for=None):
        at = place if wait_for is None else after(place, wait_for)
        mine, theirs = run_expert(at, [came[k] for k in keys], [across[k] for k in keys], weights, n, rows)
        return [(keys[2 * i : 2 * i + 2], *pair) for i, pair in enumerate(zip(mine, theirs))]

    def keep(keys, mine, theirs):
        pairs = ((mine, theirs), lax.optimization_barrier((mine, theirs)))
        start = 0
        for i, k in enumerate(keys):
            mine, theirs = pairs[i % 2]
            span = slice(start, start + size)
            start = span.stop
            parts[k] = mine[span], theirs[span]
            value[k] = mine[span].astype(jnp.float32) + theirs[span].astype(jnp.float32)

    came[1] = lax.ppermute(packed, "ep", ahead)
    came[-1] = lax.ppermute(packed, "ep", back)
    weights, done, near = [gate, up], up, []
    for k in range(2, far + 1):
        came[k - 1], came[1 - k] = after(came[k - 1], done), after(came[1 - k], done)
        came[k] = lax.ppermute(came[k - 1], "ep", ahead)
        if k < far:
            came[-k] = lax.ppermute(came[1 - k], "ep", back)
        across[k - 1], across[1 - k] = swap(came[k - 1]), swap(came[1 - k])
        if k == 2:
            weights += halve_weights(after(place, came[1]), w_down[0])
            done = weights[-1]
        else:
            near += run([k - 2, 2 - k])
            done = near[-1][-1]
    came[far] = after(came[far], done)
    across[far] = swap(came[far])
    across[0] = swap(after(packed, came[far]))
    last = [far, far - 1, 1 - far]
    for keys, mine, theirs in zip(([far], last[1:]), *run_expert_in_stages(place, [came[k] for k in last], [across[k] for k in last], swap, weights, n, rows)):
        keep(keys, mine, theirs)

    to_ahead = value[far].astype(jnp.bfloat16)
    to_back = value[far - 1].astype(jnp.bfloat16)
    for keys, mine, theirs in near:
        keep(keys, mine, swap(after(theirs, to_back)))
    for k in range(far - 1, -1, -1):
        behind = lax.ppermute(to_ahead, "ep", ahead)
        if k == far - 1:
            ((keys, mine, done),) = run([0], (to_ahead, to_back))
            keep(keys, mine, swap(done))
        else:
            to_back = done = add(*parts[k], after(front, to_ahead))
        if k:
            front = lax.ppermute(to_back, "ep", back)
            to_ahead = (value[-k] + after(behind, done).astype(jnp.float32)).astype(jnp.bfloat16)
    return finish(to_back, behind, rows, half)


def swiglu_expert(rows, gate_part, up_part, down_part):
    gated = jnp.dot(rows, gate_part, preferred_element_type=jnp.float32)
    lifted = jnp.dot(rows, up_part, preferred_element_type=jnp.float32)
    hidden = (jax.nn.silu(gated) * lifted).astype(jnp.bfloat16)
    return jnp.dot(hidden, down_part, preferred_element_type=jnp.float32)


def slot_table(expert_ids, n_experts):
    routed = expert_ids.reshape(-1)
    pair_count = routed.shape[0]
    onehot = (routed[:, None] == jnp.arange(n_experts, dtype=jnp.int32)[None, :]).astype(
        jnp.bfloat16
    )
    row_index = lax.broadcasted_iota(jnp.int32, (pair_count, pair_count), 0)
    col_index = lax.broadcasted_iota(jnp.int32, (pair_count, pair_count), 1)
    earlier = (row_index > col_index).astype(jnp.bfloat16)
    before = jnp.dot(earlier, onehot, preferred_element_type=jnp.float32)
    slots = jnp.sum(before * onehot.astype(jnp.float32), axis=1).astype(jnp.int32)
    return (routed, slots)


def slot_body(tokens, expert_ids, gate_probs, w_gate, w_up, w_down):
    n_experts = lax.axis_size("ep")
    tok_rows, top_count = expert_ids.shape
    capacity = 3 * tok_rows * top_count // (2 * n_experts)
    routed, slots = slot_table(expert_ids, n_experts)
    positions = routed * capacity + slots
    pair_token = jnp.repeat(jnp.arange(tok_rows, dtype=jnp.int32), top_count)
    buffer_rows = n_experts * capacity
    owners = jnp.full((buffer_rows,), tok_rows, jnp.int32).at[positions].set(pair_token)
    half_slots = capacity // 2
    whole_tokens = lax.all_gather(tokens, "tp", axis=1, tiled=True)
    width = whole_tokens.shape[1]
    gate_full, up_full = (
        lax.all_gather(w_gate, "tp", axis=2, tiled=True),
        lax.all_gather(w_up, "tp", axis=2, tiled=True),
    )
    down_full = lax.all_gather(w_down, "tp", axis=1, tiled=True)
    padded = jnp.concatenate([whole_tokens, jnp.zeros((1, width), whole_tokens.dtype)], 0)
    outgoing = padded[owners].reshape(n_experts, capacity, width)
    lane = lax.axis_index("tp")
    mine = lax.dynamic_slice_in_dim(outgoing, lane * half_slots, half_slots, 1)
    block = lax.all_to_all(mine, "ep", split_axis=0, concat_axis=0, tiled=True)
    sources, items, columns = block.shape
    result = swiglu_expert(
        block.reshape(sources * items, columns), gate_full[0], up_full[0], down_full[0]
    )
    result = result.astype(jnp.bfloat16).reshape(sources, items, columns)
    returned = lax.all_to_all(result, "ep", split_axis=0, concat_axis=0, tiled=True)
    received = returned.reshape(n_experts * half_slots, width)
    in_half = slots // half_slots == lane
    local_pos = routed * half_slots + slots % half_slots
    picked = received[local_pos].astype(jnp.float32).reshape(tok_rows, top_count, width)
    weighted = jnp.where(in_half.reshape(tok_rows, top_count), gate_probs, 0.0)
    partial_value = jnp.sum(weighted[:, :, None] * picked, axis=1)
    return lax.psum_scatter(partial_value, "tp", scatter_dimension=1, tiled=True).astype(
        jnp.bfloat16
    )


def solution(mesh):
    in_specs = (
        P(("groups", "ep"), "tp"),
        P(("groups", "ep"), None),
        P(("groups", "ep"), None),
        P("ep", None, "tp"),
        P("ep", None, "tp"),
        P("ep", "tp", None),
    )
    out_specs = P(("groups", "ep"), "tp")

    def body(tokens, expert_ids, *rest):
        n, top = lax.axis_size("ep"), expert_ids.shape[1]
        small = n <= 4 * top and n % 2 == 0 and n >= 8 and lax.axis_size("tp") == 2 and tokens.shape[1] % 128 + SPLITS * n <= 128
        return (ring_body if small else slot_body)(tokens, expert_ids, *rest)

    return jax.shard_map(body, mesh=mesh, in_specs=in_specs, out_specs=out_specs, check_vma=False)
```

```python
import functools

import jax
import jax.numpy as jnp
from jax import lax
from jax.experimental import pallas as pl
from jax.experimental.pallas import tpu as pltpu
from jax.sharding import PartitionSpec as P

SPLITS = 3


def in_vmem(shape, dtype=jnp.bfloat16):
    return pltpu.MemorySpace.VMEM(shape, dtype)


def hold(x):
    return pltpu.with_memory_space_constraint(x, pltpu.VMEM)


def after(x, done):
    return lax.optimization_barrier((x, done))[0]


def tiles_of(rows, columns):
    whole, rest = divmod(columns, 128)
    parts = 1
    while rest and 128 // (2 * parts) >= rest and rows % (32 * parts) == 0:
        parts *= 2
    return whole, rest, parts, whole * rows + (rows // parts if rest else 0)


def tile_places(rows, columns):
    whole, rest, parts, size = tiles_of(rows, columns)
    for j in range(whole):
        yield slice(0, rows), slice(128 * j, 128 * j + 128), slice(j * rows, (j + 1) * rows), slice(0, 128)
    for q in range(parts if rest else 0):
        share, lane = rows // parts, q * (128 // parts)
        yield slice(q * share, (q + 1) * share), slice(128 * whole, columns), slice(whole * rows, size), slice(lane, lane + rest)


def pack_kernel(n_experts, tokens_in, ids_in, probs_in, packed, tokens, ids, probs, sems):
    copies = [
        pltpu.make_async_copy(src, dst, sems.at[i])
        for i, (src, dst) in enumerate(((ids_in, ids), (probs_in, probs), (tokens_in, tokens)))
    ]
    for copy in copies:
        copy.start()
    top, rows = ids.shape
    half = tokens.shape[1]
    copies[0].wait()
    copies[1].wait()
    expert = lax.broadcasted_iota(jnp.int32, (n_experts, rows), 0)
    rest = jnp.zeros((n_experts, rows), jnp.float32)
    for k in range(top):
        rest += jnp.where(ids[k : k + 1, :] == expert, probs[k : k + 1, :], 0.0)
    terms = []
    for _ in range(SPLITS):
        term = rest.astype(jnp.bfloat16).astype(jnp.float32)
        terms.append(term)
        rest = rest - term
    terms = jnp.concatenate(terms, axis=0).T.astype(jnp.bfloat16)
    copies[2].wait()
    for r, c, at, lanes in tile_places(rows, half + terms.shape[1]):
        if c.stop <= half:
            packed[at, lanes] = tokens[r, c]
        else:
            split = lanes.start + half - c.start
            packed[at, lanes.start : split] = tokens[r, c.start : half]
            packed[at, split : lanes.stop] = terms[r, :]


def pack(tokens, expert_ids, gate_probs, n_experts):
    rows, half = tokens.shape
    args = (tokens, expert_ids.T, gate_probs.T)
    return pl.pallas_call(
        functools.partial(pack_kernel, n_experts),
        out_shape=in_vmem((tiles_of(rows, half + SPLITS * n_experts)[-1], 128)),
        in_specs=[pl.BlockSpec(memory_space=pltpu.HBM)] * 3,
        out_specs=pl.BlockSpec(memory_space=pltpu.VMEM),
        scratch_shapes=[pltpu.VMEM(a.shape, a.dtype) for a in args] + [pltpu.SemaphoreType.DMA((3,))],
        compiler_params=pltpu.CompilerParams(vmem_limit_bytes=8 << 20),
    )(*[pltpu.with_memory_space_constraint(a, pltpu.HBM) for a in args])


PIECES = 3


def pieces(hidden):
    step = -(-hidden // (128 * PIECES)) * 128
    return [(min(i * step, hidden), min((i + 1) * step, hidden)) for i in range(PIECES)]


def turn_kernel(after_this, gate_in, up_in, gate, up, gate_buf, up_buf, sems):
    steps = []
    for i, (src, buf, out) in enumerate(((gate_in, gate_buf, gate), (up_in, up_buf, up))):
        for j, (start, stop) in enumerate(pieces(src.shape[0])):
            span = pl.ds(start, stop - start)
            steps.append((pltpu.make_async_copy(src.at[span], buf.at[span], sems.at[i, j]), buf, out, start, stop))
    for copy, *_ in steps:
        copy.start()
    for copy, buf, out, start, stop in steps:
        copy.wait()
        out[:, start:stop] = buf[start:stop, :].T


def turn_weights(after_this, *weights):
    hidden, width = weights[0].shape
    return pl.pallas_call(
        turn_kernel,
        out_shape=[in_vmem((width, hidden))] * 2,
        in_specs=[pl.BlockSpec(memory_space=pltpu.SMEM)] + [pl.BlockSpec(memory_space=pltpu.HBM)] * 2,
        out_specs=[pl.BlockSpec(memory_space=pltpu.VMEM)] * 2,
        scratch_shapes=[pltpu.VMEM((hidden, width), jnp.bfloat16)] * 2 + [pltpu.SemaphoreType.DMA((2, PIECES))],
        compiler_params=pltpu.CompilerParams(vmem_limit_bytes=32 << 20),
        cost_estimate=pl.CostEstimate(flops=0, bytes_accessed=8 * hidden * width, transcendentals=0),
    )(after_this, *[pltpu.with_memory_space_constraint(w, pltpu.HBM) for w in weights])


def halve_kernel(place, down_in, down_mine, down_theirs, down_buf, sems):
    lane = place[0]
    half = down_mine.shape[1]
    spans = [slice(start, stop) for start, stop in pieces(down_in.shape[0])]
    copies = [
        pltpu.make_async_copy(down_in.at[pl.ds(s.start, s.stop - s.start)], down_buf.at[pl.ds(s.start, s.stop - s.start)], sems.at[i])
        for i, s in enumerate(spans)
    ]
    for copy in copies:
        copy.start()
    for copy, s in zip(copies, spans):
        copy.wait()

        @pl.when(lane == 0)
        def _():
            down_mine[s, :] = down_buf[s, :half]
            down_theirs[s, :] = down_buf[s, half:]

        @pl.when(lane != 0)
        def _():
            down_mine[s, :] = down_buf[s, half:]
            down_theirs[s, :] = down_buf[s, :half]


def halve_weights(place, w_down):
    hidden, width = w_down.shape
    return pl.pallas_call(
        halve_kernel,
        out_shape=[in_vmem((hidden, width // 2))] * 2,
        in_specs=[pl.BlockSpec(memory_space=pltpu.SMEM), pl.BlockSpec(memory_space=pltpu.HBM)],
        out_specs=[pl.BlockSpec(memory_space=pltpu.VMEM)] * 2,
        scratch_shapes=[pltpu.VMEM((hidden, width), jnp.bfloat16), pltpu.SemaphoreType.DMA((PIECES,))],
        compiler_params=pltpu.CompilerParams(vmem_limit_bytes=32 << 20),
        cost_estimate=pl.CostEstimate(flops=0, bytes_accessed=8 * hidden * width, transcendentals=0),
    )(place, pltpu.with_memory_space_constraint(w_down, pltpu.HBM))


def gather_rows(blocks, x, rows, columns):
    half = x.shape[1]
    for i, block in enumerate(blocks):
        for r, c, at, lanes in tile_places(rows, columns):
            stop = min(c.stop, half)
            x[i * rows + r.start : i * rows + r.stop, c.start : stop] = block[at, lanes.start : lanes.start + stop - c.start]
    start = len(blocks) * rows
    if start < x.shape[0]:
        x[start:, :] = jnp.zeros((x.shape[0] - start, half), x.dtype)


def project(x, lane, w):
    half = x.shape[1]
    return jnp.dot(x[...], w[pl.ds(pl.multiple_of(lane * half, 16), half), :], preferred_element_type=jnp.float32)


def activate(gated, lifted):
    return (gated / (1.0 + jnp.exp(-gated)) * lifted).astype(jnp.bfloat16)


def gate_weights(blocks, half, expert, n_experts, rows):
    columns = half + SPLITS * n_experts
    weights = []
    for block in blocks:
        pieces = []
        for _, c, at, lanes in tile_places(rows, columns):
            if c.stop == columns:
                terms = block[at, lanes.start + half - c.start : lanes.stop].astype(jnp.float32)
                column = lax.broadcasted_iota(jnp.int32, terms.shape, 1)
                pieces.append(jnp.sum(jnp.where(lax.rem(column, n_experts) == expert, terms, 0.0), axis=1, keepdims=True))
        weights.append(jnp.concatenate(pieces, axis=0))
    return weights


def lower(hidden, w, weights, *outs):
    value = jnp.dot(hidden, w[...], preferred_element_type=jnp.float32)
    rows, half = weights[0].shape[0], w.shape[1]
    size = tiles_of(rows, half)[-1]
    places = [(out, start) for out in outs for start in range(0, out.shape[0], size)]
    for i, (weight, (out, start)) in enumerate(zip(weights, places)):
        scaled = (value[i * rows : (i + 1) * rows] * weight).astype(jnp.bfloat16)
        for r, c, at, lanes in tile_places(rows, half):
            out[start + at.start : start + at.stop, lanes] = scaled[r, c]


def expert_kernel(n_blocks, n_experts, rows, place, *refs):
    own, across = refs[:n_blocks], refs[n_blocks : 2 * n_blocks]
    w_gate, w_up, down_mine, down_theirs, *outs, x_own, x_across = refs[2 * n_blocks :]
    lane, expert = place[0], place[1]
    half = x_own.shape[1]
    columns = half + SPLITS * n_experts
    gather_rows(own, x_own, rows, columns)
    gather_rows(across, x_across, rows, columns)
    gated = project(x_own, lane, w_gate) + project(x_across, 1 - lane, w_gate)
    lifted = project(x_own, lane, w_up) + project(x_across, 1 - lane, w_up)
    hidden = activate(gated, lifted)
    weights = gate_weights(own, half, expert, n_experts, rows)
    mine, theirs = outs[: len(outs) // 2], outs[len(outs) // 2 :]
    lower(hidden, down_theirs, weights, *theirs)
    lower(hidden, down_mine, weights, *mine)


def first_kernel(n_blocks, n_experts, rows, place, *refs):
    own = refs[:n_blocks]
    w_gate, w_up, gated, lifted, x = refs[n_blocks:]
    gather_rows(own, x, rows, x.shape[1] + SPLITS * n_experts)
    gated[...] = project(x, place[0], w_gate)
    lifted[...] = project(x, place[0], w_up)


def second_kernel(n_blocks, n_experts, rows, place, *refs):
    own, across = refs[:n_blocks], refs[n_blocks : 2 * n_blocks]
    gated, lifted, w_gate, w_up, down_theirs, hidden, *theirs, x = refs[2 * n_blocks :]
    half = x.shape[1]
    gather_rows(across, x, rows, half + SPLITS * n_experts)
    there = 1 - place[0]
    hidden[...] = activate(gated[...] + project(x, there, w_gate), lifted[...] + project(x, there, w_up))
    lower(hidden[...], down_theirs, gate_weights(own, half, place[1], n_experts, rows), *theirs)


def third_kernel(n_blocks, n_experts, rows, place, *refs):
    own = refs[:n_blocks]
    hidden, down_mine, *mine = refs[n_blocks:]
    lower(hidden[...], down_mine, gate_weights(own, down_mine.shape[1], place[1], n_experts, rows), *mine)


def call(kernel, place, args, out_shape, scratch_shapes, flops):
    vmem = pl.BlockSpec(memory_space=pltpu.VMEM)
    return pl.pallas_call(
        kernel,
        out_shape=out_shape,
        in_specs=[pl.BlockSpec(memory_space=pltpu.SMEM)] + [vmem] * len(args),
        out_specs=[vmem] * len(out_shape),
        scratch_shapes=scratch_shapes,
        compiler_params=pltpu.CompilerParams(vmem_limit_bytes=16 << 20),
        cost_estimate=pl.CostEstimate(flops=flops, bytes_accessed=flops // 128, transcendentals=0),
    )(place, *[hold(a) for a in args])


def padded(rows):
    return max(rows, 128)


def run_expert(place, own, across, weights, n_experts, block_rows):
    width, hidden = weights[0].shape
    half = width // 2
    rows, pairs = len(own) * block_rows, max(1, len(own) // 2)
    outs = call(
        functools.partial(expert_kernel, len(own), n_experts, block_rows),
        place,
        (*own, *across, *weights),
        [in_vmem((len(own) // pairs * tiles_of(block_rows, half)[-1], 128))] * (2 * pairs),
        [pltpu.VMEM((padded(rows), half), jnp.bfloat16)] * 2,
        6 * padded(rows) * hidden * width,
    )
    return outs[:pairs], outs[pairs:]


def run_expert_in_stages(place, own, across, swap, weights, n_experts, block_rows):
    gate, up, down_mine, down_theirs = weights
    width, hidden = gate.shape
    half = width // 2
    n_blocks = len(own)
    rows, size = n_blocks * block_rows, tiles_of(block_rows, half)[-1]
    products = [in_vmem((padded(rows), hidden), jnp.float32)] * 2
    outs = [in_vmem((size, 128)), in_vmem(((n_blocks - 1) * size, 128))]
    x = [pltpu.VMEM((padded(rows), half), jnp.bfloat16)]
    flops = 2 * padded(rows) * hidden * width
    gated, lifted = call(functools.partial(first_kernel, n_blocks, n_experts, block_rows), place, (*own, gate, up), products, x, flops)
    units, *theirs = call(
        functools.partial(second_kernel, n_blocks, n_experts, block_rows),
        place,
        (*own, *across, gated, lifted, gate, up, down_theirs),
        [in_vmem((padded(rows), hidden)), *outs],
        x,
        flops + flops // 2,
    )
    theirs = [swap(a) for a in theirs]
    mine = call(
        functools.partial(third_kernel, n_blocks, n_experts, block_rows),
        place,
        (*own, units, down_mine),
        outs,
        [],
        flops // 2,
    )
    return mine, theirs


def add_kernel(*refs):
    *terms, out = refs
    out[...] = sum(t[...].astype(jnp.float32) for t in terms).astype(out.dtype)


def add(*terms):
    vmem = pl.BlockSpec(memory_space=pltpu.VMEM)
    return pl.pallas_call(
        add_kernel,
        out_shape=in_vmem(terms[0].shape),
        in_specs=[vmem] * len(terms),
        out_specs=vmem,
        cost_estimate=pl.CostEstimate(flops=0, bytes_accessed=12 << 20, transcendentals=0),
    )(*[hold(t) for t in terms])


def finish_kernel(a, b, out):
    rows, half = out.shape
    for r, c, at, lanes in tile_places(rows, half):
        total = a[at, lanes].astype(jnp.float32) + b[at, lanes].astype(jnp.float32)
        out[r, c] = total.astype(out.dtype)


def finish(a, b, rows, half):
    vmem = pl.BlockSpec(memory_space=pltpu.VMEM)
    return pl.pallas_call(
        finish_kernel,
        out_shape=jax.ShapeDtypeStruct((rows, half), jnp.bfloat16),
        in_specs=[vmem] * 2,
        out_specs=vmem,
    )(hold(a), hold(b))


def ring_body(tokens, expert_ids, gate_probs, w_gate, w_up, w_down):
    n = lax.axis_size("ep")
    rows, half = tokens.shape
    size = tiles_of(rows, half)[-1]
    order = list(range(0, n, 2)) + list(range(n - 1, 0, -2))
    ahead = [(order[i], order[(i + 1) % n]) for i in range(n)]
    back = [(b, a) for a, b in ahead]
    swap = functools.partial(lax.ppermute, axis_name="tp", perm=[(0, 1), (1, 0)])
    far = n // 2
    place = jnp.stack([lax.axis_index("tp"), lax.axis_index("ep")]).astype(jnp.int32)
    packed = pack(tokens, expert_ids, gate_probs, n)
    gate, up = turn_weights(after(place, packed), w_gate[0].T, w_up[0].T)

    came, across, value, parts = {0: packed}, {}, {}, {}

    def run(keys, wait_for=None):
        at = place if wait_for is None else after(place, wait_for)
        mine, theirs = run_expert(at, [came[k] for k in keys], [across[k] for k in keys], weights, n, rows)
        return [(keys[2 * i : 2 * i + 2], *pair) for i, pair in enumerate(zip(mine, theirs))]

    def keep(keys, mine, theirs):
        pairs = ((mine, theirs), lax.optimization_barrier((mine, theirs)))
        start = 0
        for i, k in enumerate(keys):
            mine, theirs = pairs[i % 2]
            span = slice(start, start + size)
            start = span.stop
            parts[k] = mine[span], theirs[span]
            value[k] = mine[span].astype(jnp.float32) + theirs[span].astype(jnp.float32)

    came[1] = lax.ppermute(packed, "ep", ahead)
    came[-1] = lax.ppermute(packed, "ep", back)
    weights, done, near = [gate, up], up, []
    for k in range(2, far + 1):
        came[k - 1], came[1 - k] = after(came[k - 1], done), after(came[1 - k], done)
        came[k] = lax.ppermute(came[k - 1], "ep", ahead)
        if k < far:
            came[-k] = lax.ppermute(came[1 - k], "ep", back)
        across[k - 1], across[1 - k] = swap(came[k - 1]), swap(came[1 - k])
        if k == 2:
            weights += halve_weights(after(place, came[1]), w_down[0])
            done = weights[-1]
        else:
            near += run([k - 2, 2 - k])
            done = near[-1][-1]
    came[far] = after(came[far], done)
    across[far] = swap(came[far])
    across[0] = swap(after(packed, came[far]))
    last = [far, far - 1, 1 - far]
    for keys, mine, theirs in zip(([far], last[1:]), *run_expert_in_stages(place, [came[k] for k in last], [across[k] for k in last], swap, weights, n, rows)):
        keep(keys, mine, theirs)

    to_ahead = value[far].astype(jnp.bfloat16)
    to_back = value[far - 1].astype(jnp.bfloat16)
    for keys, mine, theirs in near:
        keep(keys, mine, swap(after(theirs, to_back)))
    for k in range(far - 1, -1, -1):
        behind = lax.ppermute(to_ahead, "ep", ahead)
        if k == far - 1:
            ((keys, mine, done),) = run([0], (to_ahead, to_back))
            keep(keys, mine, swap(done))
        else:
            to_back = done = add(*parts[k], after(front, to_ahead))
        if k:
            front = lax.ppermute(to_back, "ep", back)
            to_ahead = (value[-k] + after(behind, done).astype(jnp.float32)).astype(jnp.bfloat16)
    return finish(to_back, behind, rows, half)


def swiglu_expert(rows, gate_part, up_part, down_part):
    gated = jnp.dot(rows, gate_part, preferred_element_type=jnp.float32)
    lifted = jnp.dot(rows, up_part, preferred_element_type=jnp.float32)
    hidden = (jax.nn.silu(gated) * lifted).astype(jnp.bfloat16)
    return jnp.dot(hidden, down_part, preferred_element_type=jnp.float32)


def slot_table(expert_ids, n_experts):
    routed = expert_ids.reshape(-1)
    pair_count = routed.shape[0]
    onehot = (routed[:, None] == jnp.arange(n_experts, dtype=jnp.int32)[None, :]).astype(
        jnp.bfloat16
    )
    row_index = lax.broadcasted_iota(jnp.int32, (pair_count, pair_count), 0)
    col_index = lax.broadcasted_iota(jnp.int32, (pair_count, pair_count), 1)
    earlier = (row_index > col_index).astype(jnp.bfloat16)
    before = jnp.dot(earlier, onehot, preferred_element_type=jnp.float32)
    slots = jnp.sum(before * onehot.astype(jnp.float32), axis=1).astype(jnp.int32)
    return (routed, slots)


def slot_body(tokens, expert_ids, gate_probs, w_gate, w_up, w_down):
    n_experts = lax.axis_size("ep")
    tok_rows, top_count = expert_ids.shape
    capacity = 3 * tok_rows * top_count // (2 * n_experts)
    routed, slots = slot_table(expert_ids, n_experts)
    positions = routed * capacity + slots
    pair_token = jnp.repeat(jnp.arange(tok_rows, dtype=jnp.int32), top_count)
    buffer_rows = n_experts * capacity
    owners = jnp.full((buffer_rows,), tok_rows, jnp.int32).at[positions].set(pair_token)
    half_slots = capacity // 2
    whole_tokens = lax.all_gather(tokens, "tp", axis=1, tiled=True)
    width = whole_tokens.shape[1]
    gate_full, up_full = (
        lax.all_gather(w_gate, "tp", axis=2, tiled=True),
        lax.all_gather(w_up, "tp", axis=2, tiled=True),
    )
    down_full = lax.all_gather(w_down, "tp", axis=1, tiled=True)
    padded = jnp.concatenate([whole_tokens, jnp.zeros((1, width), whole_tokens.dtype)], 0)
    outgoing = padded[owners].reshape(n_experts, capacity, width)
    lane = lax.axis_index("tp")
    mine = lax.dynamic_slice_in_dim(outgoing, lane * half_slots, half_slots, 1)
    block = lax.all_to_all(mine, "ep", split_axis=0, concat_axis=0, tiled=True)
    sources, items, columns = block.shape
    result = swiglu_expert(
        block.reshape(sources * items, columns), gate_full[0], up_full[0], down_full[0]
    )
    result = result.astype(jnp.bfloat16).reshape(sources, items, columns)
    returned = lax.all_to_all(result, "ep", split_axis=0, concat_axis=0, tiled=True)
    received = returned.reshape(n_experts * half_slots, width)
    in_half = slots // half_slots == lane
    local_pos = routed * half_slots + slots % half_slots
    picked = received[local_pos].astype(jnp.float32).reshape(tok_rows, top_count, width)
    weighted = jnp.where(in_half.reshape(tok_rows, top_count), gate_probs, 0.0)
    partial_value = jnp.sum(weighted[:, :, None] * picked, axis=1)
    return lax.psum_scatter(partial_value, "tp", scatter_dimension=1, tiled=True).astype(
        jnp.bfloat16
    )


def solution(mesh):
    in_specs = (
        P(("groups", "ep"), "tp"),
        P(("groups", "ep"), None),
        P(("groups", "ep"), None),
        P("ep", None, "tp"),
        P("ep", None, "tp"),
        P("ep", "tp", None),
    )
    out_specs = P(("groups", "ep"), "tp")

    def body(tokens, expert_ids, *rest):
        n, top = lax.axis_size("ep"), expert_ids.shape[1]
        small = n <= 4 * top and n % 2 == 0 and n >= 8 and lax.axis_size("tp") == 2 and tokens.shape[1] % 128 + SPLITS * n <= 128
        return (ring_body if small else slot_body)(tokens, expert_ids, *rest)

    return jax.shard_map(body, mesh=mesh, in_specs=in_specs, out_specs=out_specs, check_vma=False)
```

```python
import functools

import jax
import jax.numpy as jnp
from jax import lax
from jax.experimental import pallas as pl
from jax.experimental.pallas import tpu as pltpu
from jax.sharding import PartitionSpec as P

SPLITS = 3


def in_vmem(shape, dtype=jnp.bfloat16):
    return pltpu.MemorySpace.VMEM(shape, dtype)


def hold(x):
    return pltpu.with_memory_space_constraint(x, pltpu.VMEM)


def after(x, done):
    return lax.optimization_barrier((x, done))[0]


def tiles_of(rows, columns):
    whole, rest = divmod(columns, 128)
    parts = 1
    while rest and 128 // (2 * parts) >= rest and rows % (32 * parts) == 0:
        parts *= 2
    return whole, rest, parts, whole * rows + (rows // parts if rest else 0)


def tile_places(rows, columns):
    whole, rest, parts, size = tiles_of(rows, columns)
    for j in range(whole):
        yield slice(0, rows), slice(128 * j, 128 * j + 128), slice(j * rows, (j + 1) * rows), slice(0, 128)
    for q in range(parts if rest else 0):
        share, lane = rows // parts, q * (128 // parts)
        yield slice(q * share, (q + 1) * share), slice(128 * whole, columns), slice(whole * rows, size), slice(lane, lane + rest)


def pack_kernel(n_experts, tokens_in, ids_in, probs_in, packed, tokens, ids, probs, sems):
    copies = [
        pltpu.make_async_copy(src, dst, sems.at[i])
        for i, (src, dst) in enumerate(((ids_in, ids), (probs_in, probs), (tokens_in, tokens)))
    ]
    for copy in copies:
        copy.start()
    top, rows = ids.shape
    half = tokens.shape[1]
    copies[0].wait()
    copies[1].wait()
    expert = lax.broadcasted_iota(jnp.int32, (n_experts, rows), 0)
    rest = jnp.zeros((n_experts, rows), jnp.float32)
    for k in range(top):
        rest += jnp.where(ids[k : k + 1, :] == expert, probs[k : k + 1, :], 0.0)
    terms = []
    for _ in range(SPLITS):
        term = rest.astype(jnp.bfloat16).astype(jnp.float32)
        terms.append(term)
        rest = rest - term
    terms = jnp.concatenate(terms, axis=0).T.astype(jnp.bfloat16)
    copies[2].wait()
    for r, c, at, lanes in tile_places(rows, half + terms.shape[1]):
        if c.stop <= half:
            packed[at, lanes] = tokens[r, c]
        else:
            split = lanes.start + half - c.start
            packed[at, lanes.start : split] = tokens[r, c.start : half]
            packed[at, split : lanes.stop] = terms[r, :]


def pack(tokens, expert_ids, gate_probs, n_experts):
    rows, half = tokens.shape
    args = (tokens, expert_ids.T, gate_probs.T)
    return pl.pallas_call(
        functools.partial(pack_kernel, n_experts),
        out_shape=in_vmem((tiles_of(rows, half + SPLITS * n_experts)[-1], 128)),
        in_specs=[pl.BlockSpec(memory_space=pltpu.HBM)] * 3,
        out_specs=pl.BlockSpec(memory_space=pltpu.VMEM),
        scratch_shapes=[pltpu.VMEM(a.shape, a.dtype) for a in args] + [pltpu.SemaphoreType.DMA((3,))],
        compiler_params=pltpu.CompilerParams(vmem_limit_bytes=8 << 20),
    )(*[pltpu.with_memory_space_constraint(a, pltpu.HBM) for a in args])


PIECES = 6


def pieces(hidden):
    step = -(-hidden // (128 * PIECES)) * 128
    return [(min(i * step, hidden), min((i + 1) * step, hidden)) for i in range(PIECES)]


def turn_kernel(after_this, gate_in, up_in, gate, up, gate_buf, up_buf, sems):
    steps = []
    for i, (src, buf, out) in enumerate(((gate_in, gate_buf, gate), (up_in, up_buf, up))):
        for j, (start, stop) in enumerate(pieces(src.shape[0])):
            span = pl.ds(start, stop - start)
            steps.append((pltpu.make_async_copy(src.at[span], buf.at[span], sems.at[i, j]), buf, out, start, stop))
    for copy, *_ in steps:
        copy.start()
    for copy, buf, out, start, stop in steps:
        copy.wait()
        out[:, start:stop] = buf[start:stop, :].T


def turn_weights(after_this, *weights):
    hidden, width = weights[0].shape
    return pl.pallas_call(
        turn_kernel,
        out_shape=[in_vmem((width, hidden))] * 2,
        in_specs=[pl.BlockSpec(memory_space=pltpu.SMEM)] + [pl.BlockSpec(memory_space=pltpu.HBM)] * 2,
        out_specs=[pl.BlockSpec(memory_space=pltpu.VMEM)] * 2,
        scratch_shapes=[pltpu.VMEM((hidden, width), jnp.bfloat16)] * 2 + [pltpu.SemaphoreType.DMA((2, PIECES))],
        compiler_params=pltpu.CompilerParams(vmem_limit_bytes=32 << 20),
        cost_estimate=pl.CostEstimate(flops=0, bytes_accessed=8 * hidden * width, transcendentals=0),
    )(after_this, *[pltpu.with_memory_space_constraint(w, pltpu.HBM) for w in weights])


def halve_kernel(place, down_in, down_mine, down_theirs, down_buf, sems):
    lane = place[0]
    half = down_mine.shape[1]
    spans = [slice(start, stop) for start, stop in pieces(down_in.shape[0])]
    copies = [
        pltpu.make_async_copy(down_in.at[pl.ds(s.start, s.stop - s.start)], down_buf.at[pl.ds(s.start, s.stop - s.start)], sems.at[i])
        for i, s in enumerate(spans)
    ]
    for copy in copies:
        copy.start()
    for copy, s in zip(copies, spans):
        copy.wait()

        @pl.when(lane == 0)
        def _():
            down_mine[s, :] = down_buf[s, :half]
            down_theirs[s, :] = down_buf[s, half:]

        @pl.when(lane != 0)
        def _():
            down_mine[s, :] = down_buf[s, half:]
            down_theirs[s, :] = down_buf[s, :half]


def halve_weights(place, w_down):
    hidden, width = w_down.shape
    return pl.pallas_call(
        halve_kernel,
        out_shape=[in_vmem((hidden, width // 2))] * 2,
        in_specs=[pl.BlockSpec(memory_space=pltpu.SMEM), pl.BlockSpec(memory_space=pltpu.HBM)],
        out_specs=[pl.BlockSpec(memory_space=pltpu.VMEM)] * 2,
        scratch_shapes=[pltpu.VMEM((hidden, width), jnp.bfloat16), pltpu.SemaphoreType.DMA((PIECES,))],
        compiler_params=pltpu.CompilerParams(vmem_limit_bytes=32 << 20),
        cost_estimate=pl.CostEstimate(flops=0, bytes_accessed=8 * hidden * width, transcendentals=0),
    )(place, pltpu.with_memory_space_constraint(w_down, pltpu.HBM))


def gather_rows(blocks, x, rows, columns):
    half = x.shape[1]
    for i, block in enumerate(blocks):
        for r, c, at, lanes in tile_places(rows, columns):
            stop = min(c.stop, half)
            x[i * rows + r.start : i * rows + r.stop, c.start : stop] = block[at, lanes.start : lanes.start + stop - c.start]
    start = len(blocks) * rows
    if start < x.shape[0]:
        x[start:, :] = jnp.zeros((x.shape[0] - start, half), x.dtype)


def project(x, lane, w):
    half = x.shape[1]
    return jnp.dot(x[...], w[pl.ds(pl.multiple_of(lane * half, 16), half), :], preferred_element_type=jnp.float32)


def activate(gated, lifted):
    return (gated / (1.0 + jnp.exp(-gated)) * lifted).astype(jnp.bfloat16)


def gate_weights(blocks, half, expert, n_experts, rows):
    columns = half + SPLITS * n_experts
    weights = []
    for block in blocks:
        pieces = []
        for _, c, at, lanes in tile_places(rows, columns):
            if c.stop == columns:
                terms = block[at, lanes.start + half - c.start : lanes.stop].astype(jnp.float32)
                column = lax.broadcasted_iota(jnp.int32, terms.shape, 1)
                pieces.append(jnp.sum(jnp.where(lax.rem(column, n_experts) == expert, terms, 0.0), axis=1, keepdims=True))
        weights.append(jnp.concatenate(pieces, axis=0))
    return weights


def lower(hidden, w, weights, *outs):
    value = jnp.dot(hidden, w[...], preferred_element_type=jnp.float32)
    rows, half = weights[0].shape[0], w.shape[1]
    size = tiles_of(rows, half)[-1]
    places = [(out, start) for out in outs for start in range(0, out.shape[0], size)]
    for i, (weight, (out, start)) in enumerate(zip(weights, places)):
        scaled = (value[i * rows : (i + 1) * rows] * weight).astype(jnp.bfloat16)
        for r, c, at, lanes in tile_places(rows, half):
            out[start + at.start : start + at.stop, lanes] = scaled[r, c]


def expert_kernel(n_blocks, n_experts, rows, place, *refs):
    own, across = refs[:n_blocks], refs[n_blocks : 2 * n_blocks]
    w_gate, w_up, down_mine, down_theirs, *outs, x_own, x_across = refs[2 * n_blocks :]
    lane, expert = place[0], place[1]
    half = x_own.shape[1]
    columns = half + SPLITS * n_experts
    gather_rows(own, x_own, rows, columns)
    gather_rows(across, x_across, rows, columns)
    gated = project(x_own, lane, w_gate) + project(x_across, 1 - lane, w_gate)
    lifted = project(x_own, lane, w_up) + project(x_across, 1 - lane, w_up)
    hidden = activate(gated, lifted)
    weights = gate_weights(own, half, expert, n_experts, rows)
    mine, theirs = outs[: len(outs) // 2], outs[len(outs) // 2 :]
    lower(hidden, down_theirs, weights, *theirs)
    lower(hidden, down_mine, weights, *mine)


def first_kernel(n_blocks, n_experts, rows, place, *refs):
    own = refs[:n_blocks]
    w_gate, w_up, gated, lifted, x = refs[n_blocks:]
    gather_rows(own, x, rows, x.shape[1] + SPLITS * n_experts)
    gated[...] = project(x, place[0], w_gate)
    lifted[...] = project(x, place[0], w_up)


def second_kernel(n_blocks, n_experts, rows, place, *refs):
    own, across = refs[:n_blocks], refs[n_blocks : 2 * n_blocks]
    gated, lifted, w_gate, w_up, down_theirs, hidden, *theirs, x = refs[2 * n_blocks :]
    half = x.shape[1]
    gather_rows(across, x, rows, half + SPLITS * n_experts)
    there = 1 - place[0]
    hidden[...] = activate(gated[...] + project(x, there, w_gate), lifted[...] + project(x, there, w_up))
    lower(hidden[...], down_theirs, gate_weights(own, half, place[1], n_experts, rows), *theirs)


def third_kernel(n_blocks, n_experts, rows, place, *refs):
    own = refs[:n_blocks]
    hidden, down_mine, *mine = refs[n_blocks:]
    lower(hidden[...], down_mine, gate_weights(own, down_mine.shape[1], place[1], n_experts, rows), *mine)


def call(kernel, place, args, out_shape, scratch_shapes, flops):
    vmem = pl.BlockSpec(memory_space=pltpu.VMEM)
    return pl.pallas_call(
        kernel,
        out_shape=out_shape,
        in_specs=[pl.BlockSpec(memory_space=pltpu.SMEM)] + [vmem] * len(args),
        out_specs=[vmem] * len(out_shape),
        scratch_shapes=scratch_shapes,
        compiler_params=pltpu.CompilerParams(vmem_limit_bytes=16 << 20),
        cost_estimate=pl.CostEstimate(flops=flops, bytes_accessed=flops // 128, transcendentals=0),
    )(place, *[hold(a) for a in args])


def padded(rows):
    return max(rows, 128)


def run_expert(place, own, across, weights, n_experts, block_rows):
    width, hidden = weights[0].shape
    half = width // 2
    rows, pairs = len(own) * block_rows, max(1, len(own) // 2)
    outs = call(
        functools.partial(expert_kernel, len(own), n_experts, block_rows),
        place,
        (*own, *across, *weights),
        [in_vmem((len(own) // pairs * tiles_of(block_rows, half)[-1], 128))] * (2 * pairs),
        [pltpu.VMEM((padded(rows), half), jnp.bfloat16)] * 2,
        6 * padded(rows) * hidden * width,
    )
    return outs[:pairs], outs[pairs:]


def run_expert_in_stages(place, own, across, swap, weights, n_experts, block_rows):
    gate, up, down_mine, down_theirs = weights
    width, hidden = gate.shape
    half = width // 2
    n_blocks = len(own)
    rows, size = n_blocks * block_rows, tiles_of(block_rows, half)[-1]
    products = [in_vmem((padded(rows), hidden), jnp.float32)] * 2
    outs = [in_vmem((size, 128)), in_vmem(((n_blocks - 1) * size, 128))]
    x = [pltpu.VMEM((padded(rows), half), jnp.bfloat16)]
    flops = 2 * padded(rows) * hidden * width
    gated, lifted = call(functools.partial(first_kernel, n_blocks, n_experts, block_rows), place, (*own, gate, up), products, x, flops)
    units, *theirs = call(
        functools.partial(second_kernel, n_blocks, n_experts, block_rows),
        place,
        (*own, *across, gated, lifted, gate, up, down_theirs),
        [in_vmem((padded(rows), hidden)), *outs],
        x,
        flops + flops // 2,
    )
    theirs = [swap(a) for a in theirs]
    mine = call(
        functools.partial(third_kernel, n_blocks, n_experts, block_rows),
        place,
        (*own, units, down_mine),
        outs,
        [],
        flops // 2,
    )
    return mine, theirs


def add_kernel(*refs):
    *terms, out = refs
    out[...] = sum(t[...].astype(jnp.float32) for t in terms).astype(out.dtype)


def add(*terms):
    vmem = pl.BlockSpec(memory_space=pltpu.VMEM)
    return pl.pallas_call(
        add_kernel,
        out_shape=in_vmem(terms[0].shape),
        in_specs=[vmem] * len(terms),
        out_specs=vmem,
        cost_estimate=pl.CostEstimate(flops=0, bytes_accessed=12 << 20, transcendentals=0),
    )(*[hold(t) for t in terms])


def finish_kernel(a, b, out):
    rows, half = out.shape
    for r, c, at, lanes in tile_places(rows, half):
        total = a[at, lanes].astype(jnp.float32) + b[at, lanes].astype(jnp.float32)
        out[r, c] = total.astype(out.dtype)


def finish(a, b, rows, half):
    vmem = pl.BlockSpec(memory_space=pltpu.VMEM)
    return pl.pallas_call(
        finish_kernel,
        out_shape=jax.ShapeDtypeStruct((rows, half), jnp.bfloat16),
        in_specs=[vmem] * 2,
        out_specs=vmem,
    )(hold(a), hold(b))


def ring_body(tokens, expert_ids, gate_probs, w_gate, w_up, w_down):
    n = lax.axis_size("ep")
    rows, half = tokens.shape
    size = tiles_of(rows, half)[-1]
    order = list(range(0, n, 2)) + list(range(n - 1, 0, -2))
    ahead = [(order[i], order[(i + 1) % n]) for i in range(n)]
    back = [(b, a) for a, b in ahead]
    swap = functools.partial(lax.ppermute, axis_name="tp", perm=[(0, 1), (1, 0)])
    far = n // 2
    place = jnp.stack([lax.axis_index("tp"), lax.axis_index("ep")]).astype(jnp.int32)
    packed = pack(tokens, expert_ids, gate_probs, n)
    gate, up = turn_weights(after(place, packed), w_gate[0].T, w_up[0].T)

    came, across, value, parts = {0: packed}, {}, {}, {}

    def run(keys, wait_for=None):
        at = place if wait_for is None else after(place, wait_for)
        mine, theirs = run_expert(at, [came[k] for k in keys], [across[k] for k in keys], weights, n, rows)
        return [(keys[2 * i : 2 * i + 2], *pair) for i, pair in enumerate(zip(mine, theirs))]

    def keep(keys, mine, theirs):
        pairs = ((mine, theirs), lax.optimization_barrier((mine, theirs)))
        start = 0
        for i, k in enumerate(keys):
            mine, theirs = pairs[i % 2]
            span = slice(start, start + size)
            start = span.stop
            parts[k] = mine[span], theirs[span]
            value[k] = mine[span].astype(jnp.float32) + theirs[span].astype(jnp.float32)

    came[1] = lax.ppermute(packed, "ep", ahead)
    came[-1] = lax.ppermute(packed, "ep", back)
    weights, done, near = [gate, up], up, []
    for k in range(2, far + 1):
        came[k - 1], came[1 - k] = after(came[k - 1], done), after(came[1 - k], done)
        came[k] = lax.ppermute(came[k - 1], "ep", ahead)
        if k < far:
            came[-k] = lax.ppermute(came[1 - k], "ep", back)
        across[k - 1], across[1 - k] = swap(came[k - 1]), swap(came[1 - k])
        if k == 2:
            weights += halve_weights(after(place, came[1]), w_down[0])
            done = weights[-1]
        else:
            near += run([k - 2, 2 - k])
            done = near[-1][-1]
    came[far] = after(came[far], done)
    across[far] = swap(came[far])
    across[0] = swap(after(packed, came[far]))
    last = [far, far - 1, 1 - far]
    for keys, mine, theirs in zip(([far], last[1:]), *run_expert_in_stages(place, [came[k] for k in last], [across[k] for k in last], swap, weights, n, rows)):
        keep(keys, mine, theirs)

    to_ahead = value[far].astype(jnp.bfloat16)
    to_back = value[far - 1].astype(jnp.bfloat16)
    for keys, mine, theirs in near:
        keep(keys, mine, swap(after(theirs, to_back)))
    for k in range(far - 1, -1, -1):
        behind = lax.ppermute(to_ahead, "ep", ahead)
        if k == far - 1:
            ((keys, mine, done),) = run([0], (to_ahead, to_back))
            keep(keys, mine, swap(done))
        else:
            to_back = done = add(*parts[k], after(front, to_ahead))
        if k:
            front = lax.ppermute(to_back, "ep", back)
            to_ahead = (value[-k] + after(behind, done).astype(jnp.float32)).astype(jnp.bfloat16)
    return finish(to_back, behind, rows, half)


def swiglu_expert(rows, gate_part, up_part, down_part):
    gated = jnp.dot(rows, gate_part, preferred_element_type=jnp.float32)
    lifted = jnp.dot(rows, up_part, preferred_element_type=jnp.float32)
    hidden = (jax.nn.silu(gated) * lifted).astype(jnp.bfloat16)
    return jnp.dot(hidden, down_part, preferred_element_type=jnp.float32)


def slot_table(expert_ids, n_experts):
    routed = expert_ids.reshape(-1)
    pair_count = routed.shape[0]
    onehot = (routed[:, None] == jnp.arange(n_experts, dtype=jnp.int32)[None, :]).astype(
        jnp.bfloat16
    )
    row_index = lax.broadcasted_iota(jnp.int32, (pair_count, pair_count), 0)
    col_index = lax.broadcasted_iota(jnp.int32, (pair_count, pair_count), 1)
    earlier = (row_index > col_index).astype(jnp.bfloat16)
    before = jnp.dot(earlier, onehot, preferred_element_type=jnp.float32)
    slots = jnp.sum(before * onehot.astype(jnp.float32), axis=1).astype(jnp.int32)
    return (routed, slots)


def slot_body(tokens, expert_ids, gate_probs, w_gate, w_up, w_down):
    n_experts = lax.axis_size("ep")
    tok_rows, top_count = expert_ids.shape
    capacity = 3 * tok_rows * top_count // (2 * n_experts)
    routed, slots = slot_table(expert_ids, n_experts)
    positions = routed * capacity + slots
    pair_token = jnp.repeat(jnp.arange(tok_rows, dtype=jnp.int32), top_count)
    buffer_rows = n_experts * capacity
    owners = jnp.full((buffer_rows,), tok_rows, jnp.int32).at[positions].set(pair_token)
    half_slots = capacity // 2
    whole_tokens = lax.all_gather(tokens, "tp", axis=1, tiled=True)
    width = whole_tokens.shape[1]
    gate_full, up_full = (
        lax.all_gather(w_gate, "tp", axis=2, tiled=True),
        lax.all_gather(w_up, "tp", axis=2, tiled=True),
    )
    down_full = lax.all_gather(w_down, "tp", axis=1, tiled=True)
    padded = jnp.concatenate([whole_tokens, jnp.zeros((1, width), whole_tokens.dtype)], 0)
    outgoing = padded[owners].reshape(n_experts, capacity, width)
    lane = lax.axis_index("tp")
    mine = lax.dynamic_slice_in_dim(outgoing, lane * half_slots, half_slots, 1)
    block = lax.all_to_all(mine, "ep", split_axis=0, concat_axis=0, tiled=True)
    sources, items, columns = block.shape
    result = swiglu_expert(
        block.reshape(sources * items, columns), gate_full[0], up_full[0], down_full[0]
    )
    result = result.astype(jnp.bfloat16).reshape(sources, items, columns)
    returned = lax.all_to_all(result, "ep", split_axis=0, concat_axis=0, tiled=True)
    received = returned.reshape(n_experts * half_slots, width)
    in_half = slots // half_slots == lane
    local_pos = routed * half_slots + slots % half_slots
    picked = received[local_pos].astype(jnp.float32).reshape(tok_rows, top_count, width)
    weighted = jnp.where(in_half.reshape(tok_rows, top_count), gate_probs, 0.0)
    partial_value = jnp.sum(weighted[:, :, None] * picked, axis=1)
    return lax.psum_scatter(partial_value, "tp", scatter_dimension=1, tiled=True).astype(
        jnp.bfloat16
    )


def solution(mesh):
    in_specs = (
        P(("groups", "ep"), "tp"),
        P(("groups", "ep"), None),
        P(("groups", "ep"), None),
        P("ep", None, "tp"),
        P("ep", None, "tp"),
        P("ep", "tp", None),
    )
    out_specs = P(("groups", "ep"), "tp")

    def body(tokens, expert_ids, *rest):
        n, top = lax.axis_size("ep"), expert_ids.shape[1]
        small = n <= 4 * top and n % 2 == 0 and n >= 8 and lax.axis_size("tp") == 2 and tokens.shape[1] % 128 + SPLITS * n <= 128
        return (ring_body if small else slot_body)(tokens, expert_ids, *rest)

    return jax.shard_map(body, mesh=mesh, in_specs=in_specs, out_specs=out_specs, check_vma=False)
```
